32 devices in a mesh: seq: 4 (over z), head: 4 (over y, x), dp: 2 (over core).
Axes of the slice: x: 2, y: 2, z: 4, core: 2. Of those that a mesh axis runs over, the one named last changes fastest.
Arguments:
- hidden_in: bfloat16 [2, 6144, 1024], P('dp', 'seq'), may hold values from -6 to 6
- doc_ids: int32 [2, 6144], P('dp', 'seq'), may hold values from 0 to 4, as said below
- norm_gain: float32 [1024], replicated, may hold values from 0.5 to 1.5
- w_gate: bfloat16 [1024, 2048], P(None, 'head'), may hold values from -0.1875 to 0.1875
- w_value: bfloat16 [1024, 2048], P(None, 'head'), may hold values from -0.1875 to 0.1875
- w_bc: bfloat16 [1024, 256], replicated, may hold values from -0.09375 to 0.09375
- w_step: bfloat16 [1024, 32], P(None, 'head'), may hold values from -0.1875 to 0.1875
- conv_value: float32 [5, 2048], P(None, 'head'), may hold values from -3 to 3
- conv_bc: float32 [5, 256], replicated, may hold values from -3 to 3
- dt_bias: float32 [32], P('head'), may hold values from -1 to 1
- a_log: float32 [32], P('head'), may hold values from -20 to -2
- d_skip: float32 [32], P('head'), may hold values from 0.5 to 2
- out_gain: float32 [2048], P('head'), may hold values from 0.5 to 1.5
- w_out: bfloat16 [2048, 1024], P('head'), may hold values from -0.125 to 0.125
- cotangent: bfloat16 [2, 6144, 1024], P('dp', 'seq', 'head'), may hold values from -6 to 6
Outputs:
- block_out: bfloat16 [2, 6144, 1024], P('dp', 'seq', 'head')
- grad_in: bfloat16 [2, 6144, 1024], P('dp', 'seq')
- grad_norm_gain: float32 [1024], replicated
- grad_w_gate: float32 [1024, 2048], P(None, 'head')
- grad_w_value: float32 [1024, 2048], P(None, 'head')
- grad_w_bc: float32 [1024, 256], replicated
- grad_w_step: float32 [1024, 32], P(None, 'head')
- grad_conv_value: float32 [5, 2048], P(None, 'head')
- grad_conv_bc: float32 [5, 256], replicated
- grad_dt_bias: float32 [32], P('head')
- grad_a_log: float32 [32], P('head')
- grad_d_skip: float32 [32], P('head')
- grad_out_gain: float32 [2048], P('head')
- grad_w_out: float32 [2048, 1024], P('head')
The draws below stay inside these ranges and needn't reach their ends.
Inputs may be any that keep to these rules, and one draw needn't show every extreme that they name: `doc_ids`: each sequence's document numbers start at 0 and never fall; a document is a run of equal numbers.
All inputs are finite; a program needn't handle non-finite values.
Results may differ from the reference program's by a relative error of at most 0.025.
The reference program's roundings to bfloat16 on the way count: a program that leaves them out, or rounds other values in their place, can miss the bound.
Values may be sent and summed in bfloat16 or wider, within the bound.
A program may use at most 320 MiB of HBM per device.

```python
import math
from functools import partial
import jax
import jax.numpy as jnp
from jax import lax

D = 1024
HEADS = 32
HEADDIM = 64
STATE = 128
CONV = 4
BLOCK = 256
TOK_DEV = 1536
INNER = 2048
SEQS = 2
LENGTH = 6144


def document_row(row_key):
    key_list = jax.random.split(row_key, 4)
    first_start = jax.random.randint(key_list[0], (), 2, TOK_DEV)
    first_end = jax.random.randint(key_list[1], (), LENGTH - TOK_DEV + 1, LENGTH - 1)
    early_cut = jax.random.randint(key_list[2], (), 1, first_start)
    late_cut = jax.random.randint(key_list[3], (), first_end + 1, LENGTH)
    where_at = jnp.arange(LENGTH, dtype=jnp.int32)
    return (where_at >= early_cut).astype(jnp.int32) + (where_at >= first_start).astype(jnp.int32) + (where_at >= first_end).astype(jnp.int32) + (where_at >= late_cut).astype(jnp.int32)


def draw_doc_ids(key, part):
    key = jax.random.fold_in(key, 7)
    return jax.vmap(document_row)(jax.random.split(key, SEQS))


def draw_a_log(key, part):
    key = jax.random.fold_in(key, 11)
    key_list = jax.random.split(key, 3)
    keep_share = 0.5
    slow_mask = jax.random.uniform(key_list[0], (HEADS,)) < keep_share
    fast_rate = jax.random.uniform(key_list[1], (HEADS,), minval=math.log(0.02), maxval=math.log(0.08))
    slow_rate = jax.random.uniform(key_list[2], (HEADS,), minval=math.log(0.1 / LENGTH), maxval=math.log(1.0 / LENGTH))
    return jnp.where(slow_mask, slow_rate, fast_rate).astype(jnp.float32)


def block_levels(key, dims, shards, low, largest):
    gain, own = 1.0, jax.random.fold_in(key, 6)
    for position, parts in shards:
        steps = jnp.exp(jax.random.uniform(jax.random.fold_in(own, position), (parts,), jnp.float32, low / len(shards), largest / len(shards)))
        gain = gain * jnp.repeat(steps, dims[position] // parts).reshape([-1 if axis == position else 1 for axis in range(len(dims))])
    return gain


def gaussian(own_key, extent, scale, most, cuts=(), kind=jnp.bfloat16):
    drawn = jax.random.normal(own_key, extent, jnp.float32) * scale
    if len(cuts) > 0:
        drawn = block_levels(own_key, extent, cuts, -0.22, 0.18) * drawn
    return jnp.clip(drawn, min=-most, max=most).astype(kind)


def setup_inputs(seed: int = 0) -> dict:
    keys = jax.random.split(jax.random.key(seed), 16)
    return {
        "hidden_in": gaussian(keys[0], (SEQS, LENGTH, D), 1.0, 6.0, ((0, 2), (1, 4))),
        "doc_ids": draw_doc_ids(jax.random.fold_in(keys[15], 71), 0),
        "norm_gain": jnp.clip(1.0 + 0.1 * jax.random.normal(keys[2], (D,), jnp.float32), 0.5, 1.5),
        "w_gate": gaussian(keys[3], (D, INNER), D ** -0.5, 0.1875, ((1, 4),)),
        "w_value": gaussian(keys[4], (D, INNER), D ** -0.5, 0.1875, ((1, 4),)),
        "w_bc": gaussian(keys[5], (D, 2 * STATE), (4 * D) ** -0.5, 0.09375),
        "w_step": gaussian(keys[6], (D, HEADS), D ** -0.5, 0.1875, ((1, 4),)),
        "conv_value": gaussian(keys[7], (CONV + 1, INNER), CONV ** -0.5, 3.0, ((1, 4),), jnp.float32),
        "conv_bc": gaussian(keys[8], (CONV + 1, 2 * STATE), CONV ** -0.5, 3.0, (), jnp.float32),
        "dt_bias": jnp.clip(jax.random.uniform(keys[9], (HEADS,), jnp.float32, -1.0, 1.0) * block_levels(keys[9], (HEADS,), ((0, 4),), -0.4, 0.0), -1.0, 1.0),
        "a_log": draw_a_log(jax.random.fold_in(keys[15], 71), 0),
        "d_skip": jnp.clip(0.5 + 1.5 * jax.random.uniform(keys[11], (HEADS,), jnp.float32) ** block_levels(keys[11], (HEADS,), ((0, 4),), -0.2, 0.2), 0.5, 2.0),
        "out_gain": jnp.clip(1.0 + 0.1 * jax.random.normal(keys[12], (INNER,), jnp.float32), 0.5, 1.5),
        "w_out": gaussian(keys[13], (INNER, D), INNER ** -0.5, 0.125, ((0, 4),)),
        "cotangent": gaussian(keys[14], (SEQS, LENGTH, D), 1.0, 6.0, ((0, 2), (1, 4), (2, 4))),
    }


HIGHEST = lax.Precision.HIGHEST
eps = 1e-05

@jax.custom_vjp
def low(v):
    return lax.optimization_barrier(v.astype(jnp.bfloat16)).astype(jnp.float32)

@jax.custom_vjp
def low_back(v):
    return v

def low_keep(v):
    return (low(v), None)

def low_pass(kept, grad):
    return (grad,)

def back_keep(v):
    return (v, None)

def back_low(kept, grad):
    return (low(grad),)
low.defvjp(low_keep, low_pass)
low_back.defvjp(back_keep, back_low)

def ssd_block(carry, block):
    state_in, doc_prev = carry
    x_heads, b_mat, c_mat, step_size, log_decay, doc_row = block
    size = log_decay.shape[0]
    cum_decay = jnp.cumsum(log_decay, axis=0)
    where_at = jnp.arange(size)
    causal = (where_at[:, None] >= where_at[None, :]) & (doc_row[:, None] == doc_row[None, :])
    spread = cum_decay[:, None, :] - cum_decay[None, :, :]
    decay = jnp.where(causal[:, :, None], jnp.exp(jnp.where(causal[:, :, None], spread, 0.0)), 0.0)
    scores = jnp.einsum('tn,sn->ts', c_mat, b_mat, precision=HIGHEST)
    mixing = scores[:, :, None] * decay * step_size[None, :, :]
    y_intra = jnp.einsum('tsh,shp->thp', mixing, x_heads, precision=HIGHEST)
    carried = (doc_row == doc_prev).astype(cum_decay.dtype)
    y_inter = jnp.einsum('tn,hpn->thp', c_mat, state_in, precision=HIGHEST) * (jnp.exp(cum_decay) * carried[:, None])[:, :, None]
    doc_last = doc_row[size - 1]
    to_end = jnp.exp(cum_decay[size - 1][None, :] - cum_decay) * (doc_row == doc_last).astype(cum_decay.dtype)[:, None] * step_size
    kept = jnp.exp(cum_decay[size - 1]) * (doc_last == doc_prev).astype(cum_decay.dtype)
    state_out = kept[:, None, None] * state_in + jnp.einsum('sh,shp,sn->hpn', to_end, x_heads, b_mat, precision=HIGHEST)
    return ((state_out, doc_last), y_intra + y_inter)

def forward_block(doc_row, x, norm_gain, w_gate, w_value, w_bc, w_step, conv_value, conv_bc, dt_bias, a_log, d_skip, out_gain, w_out):
    r = lax.rsqrt(lax.optimization_barrier(jnp.mean(x * x, axis=1, keepdims=True)) + eps)
    normed = low(x * r * norm_gain)
    z = low_back(jnp.dot(normed, w_gate, precision=HIGHEST))
    x_val = low_back(jnp.dot(normed, w_value, precision=HIGHEST))
    b_c = low_back(jnp.dot(normed, w_bc, precision=HIGHEST))
    step_raw = low_back(jnp.dot(normed, w_step, precision=HIGHEST))
    conv_in = jnp.concatenate([x_val, b_c], axis=1)
    n_edge = CONV - 1
    conv_ext = jnp.pad(conv_in, ((n_edge, 0), (0, 0)))
    taps_all = jnp.concatenate([conv_value, conv_bc], axis=1)
    conv_pre = taps_all[CONV][None, :] + taps_all[0] * conv_ext[n_edge:n_edge + LENGTH]
    for offset in range(1, CONV):
        conv_pre = conv_pre + taps_all[offset] * conv_ext[n_edge - offset:n_edge - offset + LENGTH]
    u = jax.nn.silu(conv_pre)
    x_heads = u[:, :INNER].reshape(LENGTH, HEADS, HEADDIM)
    b_mat = u[:, INNER:INNER + STATE]
    c_mat = u[:, INNER + STATE:]
    step_size = jax.nn.softplus(step_raw + dt_bias)
    log_decay = -jnp.exp(a_log) * step_size
    n_blocks = LENGTH // BLOCK
    blocks = (x_heads.reshape(n_blocks, BLOCK, HEADS, HEADDIM), b_mat.reshape(n_blocks, BLOCK, STATE), c_mat.reshape(n_blocks, BLOCK, STATE), step_size.reshape(n_blocks, BLOCK, HEADS), log_decay.reshape(n_blocks, BLOCK, HEADS), doc_row.reshape(n_blocks, BLOCK))
    init_carry = (jnp.zeros((HEADS, HEADDIM, STATE), jnp.float32), jnp.int32(-1))
    final_carry, block_ys = lax.scan(jax.checkpoint(ssd_block), init_carry, blocks)
    y = (block_ys.reshape(LENGTH, HEADS, HEADDIM) + d_skip[None, :, None] * x_heads).reshape(LENGTH, INNER)
    g = y * jax.nn.silu(z)
    r_out = lax.rsqrt(lax.optimization_barrier(jnp.mean(g * g, axis=1, keepdims=True)) + eps)
    gated = low(g * r_out * out_gain)
    return x + jnp.dot(gated, w_out, precision=HIGHEST)

def reference(hidden_in, doc_ids, norm_gain, w_gate, w_value, w_bc, w_step, conv_value, conv_bc, dt_bias, a_log, d_skip, out_gain, w_out, cotangent):
    params = tuple((p.astype(jnp.float32) for p in (norm_gain, w_gate, w_value, w_bc, w_step, conv_value, conv_bc, dt_bias, a_log, d_skip, out_gain, w_out)))
    outputs = []
    input_grads = []
    totals = [jnp.zeros_like(p) for p in params]
    for seq_index in range(SEQS):
        forward_one = partial(forward_block, doc_ids[seq_index])
        output, pullback = jax.vjp(forward_one, hidden_in[seq_index].astype(jnp.float32), *params)
        gradients = pullback(cotangent[seq_index].astype(jnp.float32))
        outputs.append(output.astype(jnp.bfloat16))
        input_grads.append(gradients[0].astype(jnp.bfloat16))
        totals = [total + grad_one for total, grad_one in zip(totals, gradients[1:])]
    block_out = jnp.stack(outputs)
    grad_in = jnp.stack(input_grads)
    return (block_out, grad_in, totals[0], totals[1], totals[2], totals[3], totals[4], totals[5], totals[6], totals[7], totals[8], totals[9], totals[10], totals[11])
```

```python
import functools

import jax
import jax.numpy as jnp
from jax import lax
from jax.experimental import pallas as pl
from jax.experimental.pallas import tpu as pltpu
from jax.sharding import PartitionSpec as P

BLOCK = 256
EDGE = 8
EPS = 1e-05
NEG = -1e30
F32 = jnp.float32
BF16 = jnp.bfloat16
NN = (((1,), (0,)), ((), ()))
NT = (((1,), (1,)), ((), ()))
TN = (((0,), (0,)), ((), ()))
VMEM_LIMIT = 56 * 1024 * 1024


def dot(a, b, dims=NN):
    return lax.dot_general(a, b, dims, preferred_element_type=F32)


def halves(v):
    hi = v.astype(BF16)
    return hi, (v - hi.astype(F32)).astype(BF16)


def dot_left(v, m, dims=NN):
    hi, lo = halves(v)
    return dot(hi, m, dims) + dot(lo, m, dims)


def dot_right(m, v, dims=NN):
    hi, lo = halves(v)
    return dot(m, hi, dims) + dot(m, lo, dims)


def dot3(a, b, dims=NN):
    (ah, al), (bh, bl) = halves(a), halves(b)
    return dot(ah, bh, dims) + (dot(al, bh, dims) + dot(ah, bl, dims))


def score_pair(c, b, first):
    hi, lo = halves(c)
    cc, bb = jnp.concatenate([hi, lo], axis=1), jnp.concatenate([b, b], axis=1)
    return dot(cc, bb, NT) if first else dot(bb, cc, NT)


def sigmoid(v):
    return 1.0 / (1.0 + jnp.exp(-v))


def softplus(v):
    return jnp.maximum(v, 0.0) + jnp.log1p(jnp.exp(-jnp.abs(v)))


def iota(shape, axis):
    return lax.broadcasted_iota(jnp.int32, shape, axis)


def spread_matrix(heads, inner):
    return (iota((heads, inner), 1) // (inner // heads) == iota((heads, inner), 0)).astype(BF16)


def gather_matrix(heads, inner):
    return (iota((inner, heads), 0) // (inner // heads) == iota((inner, heads), 1)).astype(BF16)


def in_norm(x, gain):
    r = lax.rsqrt(jnp.mean(x * x, axis=1, keepdims=True) + EPS)
    return (x * r * gain).astype(BF16)


def conv_forward(ext_ref, start, size, taps):
    n_taps = taps.shape[0] - 1
    pre = taps[n_taps : n_taps + 1, :] + taps[0:1, :] * ext_ref[pl.ds(start + EDGE, size), :]
    for k in range(1, n_taps):
        pre = pre + taps[k : k + 1, :] * ext_ref[pl.ds(start + EDGE - k, size), :]
    return pre


def front_kernel(
    x_ref, halo_ref, gain_ref, wg_ref, wv_ref, wbc_ref, ws_ref, wst_ref, taps_ref, dtb_ref, dtbt_ref,
    rate_ref, ratet_ref, skip_ref, aux_ref, docr_ref,
    normed_ref, z_ref, cin_ref, head_ref, y_ref, c_ref, v_ref, cum_ref, vt_ref, cumt_ref, inc_ref,
    kept_ref, end_ref, carry_ref, ext,
):
    step_id = pl.program_id(0)
    size = x_ref.shape[0]
    inner = wv_ref.shape[1]
    heads = ws_ref.shape[1]
    state = wbc_ref.shape[1] // 2
    gain = gain_ref[...]

    @pl.when(step_id == 0)
    def _():
        edge = in_norm(halo_ref[...].astype(F32), gain)
        rows = edge.shape[0]
        ext[0:EDGE, :inner] = dot(edge, wv_ref[...])[rows - EDGE :]
        ext[0:EDGE, inner:] = dot(edge, wbc_ref[...])[rows - EDGE :]
        head_ref[...] = ext[0:EDGE, :]
        end_ref[...] = jnp.zeros_like(end_ref)
        carry_ref[...] = jnp.ones_like(carry_ref)

    @pl.when(step_id > 0)
    def _():
        ext[0:EDGE, :] = ext[size : size + EDGE, :]

    normed = in_norm(x_ref[...].astype(F32), gain)
    normed_ref[...] = normed
    z_ref[...] = dot(normed, wg_ref[...])
    ext[EDGE:, :inner] = dot(normed, wv_ref[...])
    ext[EDGE:, inner:] = dot(normed, wbc_ref[...])
    cin_ref[...] = ext[EDGE:, :]
    v = dot(normed, ws_ref[...]) + dtb_ref[...]
    vt = dot(wst_ref[...], normed, NT) + dtbt_ref[...]
    pre = conv_forward(ext, 0, size, taps_ref[...])
    u = pre * sigmoid(pre)
    xh = u[:, :inner]
    b_mat, c_full = u[:, inner : inner + state].astype(BF16), u[:, inner + state :]
    step = softplus(v)
    where_t, where_s = iota((size, size), 0), iota((size, size), 1)
    lower = (where_t >= where_s).astype(BF16)
    cum = dot_right(lower, rate_ref[...] * step)
    cumt = dot_left(ratet_ref[...] * softplus(vt), lower, NT)
    doc, last = aux_ref[:, 0:1], aux_ref[:, 2:3]
    mask = jnp.where((where_t >= where_s) & (doc == docr_ref[...]), 0.0, NEG)
    scores = score_pair(c_full, b_mat, True)
    spread = spread_matrix(heads, inner)
    xs = xh * dot_left(step, spread)
    total = cum[size - 1 : size, :]
    to_end = dot_left(jnp.exp(total - cum) * last, spread)
    inc = dot(b_mat, (xs * to_end).astype(BF16), TN)
    kept = dot_left(jnp.exp(total) * aux_ref[0:1, 3:4], spread)
    lanes = 2 * (inner // heads)
    first = iota((size, lanes), 1) < lanes // 2
    xs = xs.astype(BF16)
    parts = []
    for pair in range(heads // 2):
        xp = xs[:, pair * lanes : (pair + 1) * lanes]
        mixed = []
        for h in (2 * pair, 2 * pair + 1):
            decay = jnp.exp(cum[:, h : h + 1] - cumt[h : h + 1, :] + mask)
            mixed.append((scores * decay).astype(BF16))
        both = jnp.concatenate(mixed, axis=1)
        zero = jnp.zeros_like(xp)
        xx = jnp.concatenate([jnp.where(first, xp, zero), jnp.where(first, zero, xp)], axis=0)
        parts.append(dot(both, xx))
    y_ref[...] = jnp.concatenate(parts, axis=1) + skip_ref[...] * xh
    c_ref[...] = c_full
    v_ref[...] = v
    cum_ref[...] = cum
    vt_ref[...] = vt
    cumt_ref[...] = cumt
    inc_ref[0] = inc
    kept_ref[0] = kept
    end_ref[...] = kept * end_ref[...] + inc
    carry_ref[...] = carry_ref[...] * kept


def mid_kernel(
    yi_ref, z_ref, c_ref, cum_ref, aux_ref, cot_ref, w_out_ref, gain_ref, inc_ref, kept_ref, all_ref, weight_ref,
    y_ref, si_ref, dgn_ref, sums_ref, state,
):
    step_id = pl.program_id(0)
    inner = z_ref.shape[1]
    heads = cum_ref.shape[1]

    @pl.when(step_id == 0)
    def _():
        total = jnp.zeros_like(state)
        for k in range(all_ref.shape[0]):
            total = total + weight_ref[k] * all_ref[k].astype(F32)
        state[...] = total

    si = state[...]
    si_ref[0] = si
    state[...] = kept_ref[0] * si + inc_ref[0]
    into = dot_left(jnp.exp(cum_ref[...]) * aux_ref[:, 1:2], spread_matrix(heads, inner))
    y = yi_ref[...] + into * dot3(c_ref[...], si)
    y_ref[...] = y
    z = z_ref[...]
    g = y * (z * sigmoid(z))
    dgn = dot(cot_ref[...], w_out_ref[...], NT)
    dgn_ref[...] = dgn
    ones = jnp.ones((8, inner), BF16)
    sq = dot_right(ones, g * g, NT)
    inn = dot_right(ones, dgn * gain_ref[...] * g, NT)
    sums_ref[0:1, :] = sq[0:1]
    sums_ref[1:2, :] = inn[0:1]


def gate_kernel(
    inner_all, y_ref, z_ref, c_ref, cum_ref, aux_ref, cot_ref, w_out_ref, gain_ref, dgn_ref, sums_ref, kept_ref,
    normed_ref, dy_ref, dz_ref, out_ref, g_out_ref, g_gate_ref, g_gain_ref, g_state_ref, prod,
):
    step_id = pl.program_id(0)
    inner = z_ref.shape[1]
    heads = cum_ref.shape[1]

    @pl.when(step_id == 0)
    def _():
        for ref in (g_out_ref, g_gate_ref, g_gain_ref, g_state_ref):
            ref[...] = jnp.zeros_like(ref)
        prod[...] = jnp.ones_like(prod)

    y, z, dgn, gain = y_ref[...], z_ref[...], dgn_ref[...], gain_ref[...]
    sig = sigmoid(z)
    act = z * sig
    g = y * act
    r = lax.rsqrt(sums_ref[:, 0:1] / inner_all + EPS)
    gr = g * r
    gn = (gr * gain).astype(BF16)
    g_gain_ref[...] += jnp.sum(dgn * gr, axis=0, keepdims=True)
    dg = r * (dgn * gain) - g * (r * r * r * sums_ref[:, 1:2] / inner_all)
    dy = dg * act
    dz = (dg * y * (sig * (1.0 + z * (1.0 - sig)))).astype(BF16)
    dy_ref[...] = dy.astype(BF16)
    dz_ref[...] = dz
    out_ref[...] = dot(gn, w_out_ref[...]).astype(BF16)
    g_out_ref[...] += dot(gn, cot_ref[...], TN)
    g_gate_ref[...] += dot(normed_ref[...], dz, TN)
    into = dot_left(jnp.exp(cum_ref[...]) * aux_ref[:, 1:2], spread_matrix(heads, inner))
    g_state_ref[...] += prod[...] * dot(c_ref[...].astype(BF16), (dy * into).astype(BF16), TN)
    prod[...] = prod[...] * kept_ref[0]


def back_kernel(
    cin_ref, before_ref, dy_ref, y_ref, v_ref, cum_ref, vt_ref, cumt_ref, aux_ref, docr_ref, si_ref, kept_ref,
    taps_ref, rate_ref, skip_ref, all_ref, weight_ref,
    pre_ref, dstep_ref, g_dt_ref, g_log_ref, g_skip_ref, g_conv_ref, adj, ext,
):
    step_id = pl.program_id(0)
    size, inner = dy_ref.shape
    heads = cum_ref.shape[1]
    state = adj.shape[0]
    n_taps = taps_ref.shape[0] - 1

    @pl.when(step_id == 0)
    def _():
        total = jnp.zeros_like(adj)
        for k in range(all_ref.shape[0]):
            total = total + weight_ref[k] * all_ref[k].astype(F32)
        adj[...] = total
        for ref in (g_dt_ref, g_log_ref, g_skip_ref, g_conv_ref):
            ref[...] = jnp.zeros_like(ref)

    spread, collect = spread_matrix(heads, inner), gather_matrix(heads, inner)
    ext[0:EDGE, :] = before_ref[...]
    ext[EDGE:, :] = cin_ref[...]
    pre = conv_forward(ext, 0, size, taps_ref[...])
    sig = sigmoid(pre)
    u = pre * sig
    dsilu = sig * (1.0 + pre * (1.0 - sig))
    xh = u[:, :inner]
    b_mat, c_full = u[:, inner : inner + state].astype(BF16), u[:, inner + state :]
    c_mat = c_full.astype(BF16)
    v = v_ref[...]
    step = softplus(v)
    cum, cumt = cum_ref[...], cumt_ref[...]
    where_s, where_t = iota((size, size), 0), iota((size, size), 1)
    doc, carried, last = aux_ref[:, 0:1], aux_ref[:, 1:2], aux_ref[:, 2:3]
    mask = jnp.where((where_t >= where_s) & (doc == docr_ref[...]), 0.0, NEG)
    scores = score_pair(c_full, b_mat, False)
    step_e = dot_left(step, spread)
    total = cum[size - 1 : size, :]
    to_end = dot_left(jnp.exp(total - cum) * last, spread)
    into = dot_left(jnp.exp(cum) * carried, spread)
    xs = xh * step_e
    xsb = xs.astype(BF16)
    dyb = dy_ref[...]
    dy = dyb.astype(F32)
    si = si_ref[0]
    back = adj[...]
    backb = back.astype(BF16)
    dye = dy * into
    xse = xs * to_end
    d_c = dot3(dye, si, NT)
    d_b = dot3(xse, back, NT)
    dye, xse = dye.astype(BF16), xse.astype(BF16)
    d_xs_inter = to_end * dot(b_mat, backb)
    lanes = 2 * (inner // heads)
    first = iota((size, lanes), 1) < lanes // 2
    d_scores = jnp.zeros((size, size), F32)
    parts = []
    for pair in range(heads // 2):
        cols = slice(pair * lanes, (pair + 1) * lanes)
        xp, dp = xsb[:, cols], dyb[:, cols]
        zero = jnp.zeros_like(dp)
        d_two = (jnp.where(first, dp, zero), jnp.where(first, zero, dp))
        mixed = []
        for i, h in enumerate((2 * pair, 2 * pair + 1)):
            decay = jnp.exp(cumt[h : h + 1, :] - cum[:, h : h + 1] + mask)
            mixed.append((scores * decay).astype(BF16))
            d_scores = d_scores + dot(xp, d_two[i], NT) * decay
        parts.append(dot(jnp.concatenate(mixed, axis=1), jnp.concatenate(d_two, axis=0)))
    d_xs_intra = jnp.concatenate(parts, axis=1)
    d_sb = d_scores.astype(BF16)
    d_b = d_b + dot(d_sb, c_mat)
    d_c = d_c + dot(d_sb, b_mat, TN)
    skip = skip_ref[...]
    d_xs = d_xs_intra + d_xs_inter
    y_ssd = y_ref[...] - skip * xh
    d_step_dir = dot_left(xh * d_xs, collect)
    d_cum = dot_left(dy * y_ssd - (xsb.astype(F32) * d_xs_intra + xs * d_xs_inter), collect)
    inc = dot(b_mat, xse, TN)
    end_state = kept_ref[0] * si + inc
    through = dot_left(jnp.sum(back * end_state, axis=0, keepdims=True), collect)
    upper = (where_t >= where_s).astype(BF16)
    d_la = dot_right(upper, d_cum) + through
    d_la = d_la * aux_ref[:, 4:5]
    rate = rate_ref[...]
    g_log_ref[...] += jnp.sum(rate * step * d_la, axis=0, keepdims=True)
    d_v = (d_step_dir + rate * d_la) * sigmoid(v)
    g_dt_ref[...] += jnp.sum(d_v, axis=0, keepdims=True)
    dstep_ref[...] = d_v.astype(BF16)
    g_skip_ref[...] += jnp.sum(dy * xh, axis=0, keepdims=True)
    adj[...] = kept_ref[0] * back + dot(c_mat, dye, TN)
    pre_ref[:, :inner] = (skip * dy + step_e * d_xs) * dsilu[:, :inner]
    pre_ref[:, inner : inner + state] = d_b * dsilu[:, inner : inner + state]
    pre_ref[:, inner + state :] = d_c * dsilu[:, inner + state :]
    d_pre = pre_ref[...]
    for k in range(n_taps):
        g_conv_ref[k : k + 1, :] += jnp.sum(d_pre * ext[pl.ds(EDGE - k, size), :], axis=0, keepdims=True)
    g_conv_ref[n_taps : n_taps + 1, :] += jnp.sum(d_pre, axis=0, keepdims=True)


def proj_back_kernel(
    pre_ref, next_ref, taps_ref, normed_ref, dz_ref, dstep_ref, wg_ref, wv_ref, ws_ref,
    part_ref, g_value_ref, g_step_ref, ext,
):
    step_id = pl.program_id(0)
    size = pre_ref.shape[0]
    inner = wv_ref.shape[1]
    width = wg_ref.shape[0]

    @pl.when(step_id == 0)
    def _():
        g_value_ref[...] = jnp.zeros_like(g_value_ref)
        g_step_ref[...] = jnp.zeros_like(g_step_ref)

    ext[0:size, :] = pre_ref[...]
    ext[size:, :] = next_ref[...]
    taps = taps_ref[...]
    d_in = taps[0:1, :] * ext[0:size, :]
    for k in range(1, taps.shape[0] - 1):
        d_in = d_in + taps[k : k + 1, :] * ext[pl.ds(k, size), :]
    d_val = d_in[:, :inner].astype(BF16)
    dstep = dstep_ref[...]
    part = dot(dz_ref[...], wg_ref[...], NT) + dot(d_val, wv_ref[...], NT) + dot(dstep, ws_ref[...], NT)
    part_ref[:, :width] = part.astype(BF16)
    part_ref[:, width:] = d_in[:, inner:].astype(BF16)
    normed = normed_ref[...]
    g_value_ref[...] += dot(normed, d_val, TN)
    g_step_ref[...] += dot(normed, dstep, TN)


def last_kernel(
    part_ref, x_ref, cot_ref, gain_ref, wbc_ref, grad_ref, g_bc_ref, g_norm_ref,
):
    width = x_ref.shape[1]

    @pl.when(pl.program_id(0) == 0)
    def _():
        g_bc_ref[...] = jnp.zeros_like(g_bc_ref)
        g_norm_ref[...] = jnp.zeros_like(g_norm_ref)

    x = x_ref[...].astype(F32)
    gain = gain_ref[...]
    r = lax.rsqrt(jnp.mean(x * x, axis=1, keepdims=True) + EPS)
    xr = x * r
    normed = (xr * gain).astype(BF16)
    d_bc = part_ref[:, width:]
    d_normed = part_ref[:, :width].astype(F32) + dot(d_bc, wbc_ref[...], NT)
    g_bc_ref[...] += dot(normed, d_bc, TN)
    g_norm_ref[...] += jnp.sum(d_normed * xr, axis=0, keepdims=True)
    q = d_normed * gain
    d_x = r * q - xr * (r * r * jnp.mean(q * x, axis=1, keepdims=True))
    grad_ref[...] = (d_x + cot_ref[...].astype(F32)).astype(BF16)


def shift(block, axis, distance):
    devices = range(lax.axis_size(axis))
    return lax.ppermute(block, axis, [(i - distance, i) for i in devices if i - distance in devices])


def whole(a):
    return pl.BlockSpec(a.shape, lambda i: (0,) * len(a.shape))


def shape(dims, dtype=F32):
    return jax.ShapeDtypeStruct(dims, dtype)


def params():
    return pltpu.CompilerParams(vmem_limit_bytes=VMEM_LIMIT, dimension_semantics=("arbitrary",))


def chain_weights(carry, axis, reverse):
    n, here = lax.axis_size(axis), lax.axis_index(axis)
    rows = []
    for k in range(n):
        used = jnp.ones_like(carry[0])
        for j in range(n):
            between = ((here < j) & (j < k)) if reverse else ((k < j) & (j < here))
            used = used * jnp.where(between, carry[j], 1.0)
        reach = (k > here) if reverse else (k < here)
        rows.append(jnp.where(reach, used, 0.0))
    return jnp.stack(rows)


def on_device(
    hidden_in, doc_ids, norm_gain, w_gate, w_value, w_bc, w_step, conv_value, conv_bc, dt_bias, a_log, d_skip,
    out_gain, w_out, cotangent,
):
    x = hidden_in[0]
    docs = doc_ids[0]
    tokens, width = x.shape
    inner = w_gate.shape[1]
    heads = w_step.shape[1]
    head_dim = inner // heads
    bc_width = w_bc.shape[1]
    state = bc_width // 2
    channels = inner + bc_width
    blocks = tokens // BLOCK
    n_head = lax.axis_size("head")
    inner_all = inner * n_head
    n_taps = conv_value.shape[0] - 1

    edge_x, edge_doc = shift((x[tokens - 16 :], (docs[tokens - 1 :] + 1).astype(F32)), "seq", 1)
    doc_before = edge_doc[0] - 1.0
    docf = docs.astype(F32)
    by_block = docf.reshape(blocks, BLOCK)
    prev_doc = jnp.concatenate([doc_before[None], by_block[:-1, -1]])
    carried = (by_block == prev_doc[:, None]).astype(F32)
    last = (by_block == by_block[:, -1:]).astype(F32)
    kept_mask = jnp.broadcast_to((by_block[:, -1] == prev_doc).astype(F32)[:, None], by_block.shape)
    keep = (docf == jnp.concatenate([doc_before[None], docf[:-1]])).astype(F32).reshape(by_block.shape)
    none = jnp.zeros_like(keep)
    aux = jnp.stack([by_block, carried, last, kept_mask, keep, none, none, none], axis=-1).reshape(tokens, 8)
    docr = docf.reshape(1, tokens)

    taps = jnp.concatenate([conv_value, conv_bc], axis=1)
    gain = norm_gain[None]
    rate = -jnp.exp(a_log)[None]
    skip = jnp.repeat(d_skip, head_dim)[None]
    cot = lax.all_gather(cotangent[0], "head", axis=1, tiled=True)

    def rows(n, size=BLOCK):
        return pl.BlockSpec((size, n), lambda i: (i, 0))

    def cols(n):
        return pl.BlockSpec((n, BLOCK), lambda i: (0, i))

    def per_block(*dims):
        return pl.BlockSpec((1, *dims), lambda i: (i,) + (0,) * len(dims))

    def fixed(*dims):
        return pl.BlockSpec(dims, lambda i: (0,) * len(dims))

    w_step_t = w_step.T
    front = (x, edge_x, gain, w_gate, w_value, w_bc, w_step, w_step_t, taps, dt_bias[None], dt_bias[:, None],
             rate, rate.T, skip, aux, docr)
    (normed, z, cin, head_edge, y_intra, c_mat, v, cum, vt, cumt, inc, kept, end, carry) = pl.pallas_call(
        front_kernel,
        grid=(blocks,),
        in_specs=[rows(width)] + [whole(a) for a in front[1:14]] + [rows(8), cols(1)],
        out_specs=[rows(width), rows(inner), rows(channels), fixed(EDGE, channels), rows(inner), rows(state),
                   rows(heads), rows(heads), cols(heads), cols(heads), per_block(state, inner),
                   per_block(1, inner), fixed(state, inner), fixed(1, inner)],
        out_shape=[shape((tokens, width), BF16), shape((tokens, inner)), shape((tokens, channels)),
                   shape((EDGE, channels)), shape((tokens, inner)), shape((tokens, state)),
                   shape((tokens, heads)), shape((tokens, heads)), shape((heads, tokens)), shape((heads, tokens)),
                   shape((blocks, state, inner)), shape((blocks, 1, inner)), shape((state, inner)),
                   shape((1, inner))],
        scratch_shapes=[pltpu.VMEM((EDGE + BLOCK, channels), F32)],
        compiler_params=params(),
        name="front",
    )(*front)

    ends = lax.all_gather(end.astype(BF16), "seq")
    carries = lax.all_gather(carry, "seq")
    og = out_gain[None]
    mid = (y_intra, z, c_mat, cum, aux, cot, w_out, og, inc, kept, ends, chain_weights(carries, "seq", False))
    y, si, dgn, sums = pl.pallas_call(
        mid_kernel,
        grid=(blocks,),
        in_specs=[rows(inner), rows(inner), rows(state), rows(heads), rows(8), rows(width), whole(w_out), whole(og),
                  per_block(state, inner), per_block(1, inner), whole(ends), whole(mid[-1])],
        out_specs=[rows(inner), per_block(state, inner), rows(inner), cols(2)],
        out_shape=[shape((tokens, inner)), shape((blocks, state, inner)), shape((tokens, inner)), shape((2, tokens))],
        scratch_shapes=[pltpu.VMEM((state, inner), F32)],
        compiler_params=params(),
        name="mid",
    )(*mid)

    sums = lax.psum(sums, "head").T
    gate = (y, z, c_mat, cum, aux, cot, w_out, og, dgn, sums, kept, normed)
    dy, dz, out_part, g_w_out, g_w_gate, g_out_gain, g_state = pl.pallas_call(
        functools.partial(gate_kernel, inner_all),
        grid=(blocks,),
        in_specs=[rows(inner), rows(inner), rows(state), rows(heads), rows(8), rows(width), whole(w_out), whole(og),
                  rows(inner), rows(2), per_block(1, inner), rows(width)],
        out_specs=[rows(inner), rows(inner), rows(width), fixed(inner, width), fixed(width, inner), fixed(1, inner),
                   fixed(state, inner)],
        out_shape=[shape((tokens, inner), BF16), shape((tokens, inner), BF16), shape((tokens, width), BF16),
                   shape((inner, width)), shape((width, inner)), shape((1, inner)), shape((state, inner))],
        scratch_shapes=[pltpu.VMEM((1, inner), F32)],
        compiler_params=params(),
        name="gate",
    )(*gate)

    out_cols = lax.psum_scatter(out_part, "head", scatter_dimension=1, tiled=True).astype(F32)
    part_width = out_cols.shape[1]
    residual = lax.dynamic_slice_in_dim(x, lax.axis_index("head") * part_width, part_width, 1).astype(F32)
    block_out = (residual + out_cols).astype(BF16)[None]

    g_states = lax.all_gather(g_state.astype(BF16), "seq")
    before = jnp.concatenate([head_edge, cin.reshape(blocks, BLOCK, channels)[:-1, BLOCK - EDGE :].reshape(-1, channels)])

    def turn(spec_rows, n):
        return pl.BlockSpec((spec_rows, n), lambda i: (blocks - 1 - i, 0))

    def turn_cols(n):
        return pl.BlockSpec((n, BLOCK), lambda i: (0, blocks - 1 - i))

    def turn_block(*dims):
        return pl.BlockSpec((1, *dims), lambda i: (blocks - 1 - i,) + (0,) * len(dims))

    back = (cin, before, dy, y, v, cum, vt, cumt, aux, docr, si, kept, taps, rate, skip, g_states,
            chain_weights(carries, "seq", True))
    pre, dstep, g_dt, g_log, g_skip, g_conv = pl.pallas_call(
        back_kernel,
        grid=(blocks,),
        in_specs=[turn(BLOCK, channels), turn(EDGE, channels), turn(BLOCK, inner), turn(BLOCK, inner),
                  turn(BLOCK, heads), turn(BLOCK, heads), turn_cols(heads), turn_cols(heads), turn(BLOCK, 8),
                  turn_cols(1), turn_block(state, inner), turn_block(1, inner), whole(taps), whole(rate), whole(skip),
                  whole(g_states), whole(back[-1])],
        out_specs=[turn(BLOCK, channels), turn(BLOCK, heads), fixed(1, heads), fixed(1, heads), fixed(1, inner),
                   fixed(8, channels)],
        out_shape=[shape((tokens, channels)), shape((tokens, heads), BF16), shape((1, heads)), shape((1, heads)),
                   shape((1, inner)), shape((8, channels))],
        scratch_shapes=[pltpu.VMEM((state, inner), F32),
                        pltpu.VMEM((EDGE + BLOCK, channels), F32)],
        compiler_params=params(),
        name="back",
    )(*back)

    edge_back = shift(pre[:EDGE], "seq", -1)
    following = jnp.concatenate([pre.reshape(blocks, BLOCK, channels)[1:, :EDGE].reshape(-1, channels), edge_back])
    proj = (pre, following, taps, normed, dz, dstep, w_gate, w_value, w_step)
    part, g_w_value, g_w_step = pl.pallas_call(
        proj_back_kernel,
        grid=(blocks,),
        in_specs=[rows(channels), rows(channels, EDGE), whole(taps), rows(width), rows(inner), rows(heads),
                  whole(w_gate), whole(w_value), whole(w_step)],
        out_specs=[rows(width + bc_width), fixed(width, inner), fixed(width, heads)],
        out_shape=[shape((tokens, width + bc_width), BF16), shape((width, inner)), shape((width, heads))],
        scratch_shapes=[pltpu.VMEM((EDGE + BLOCK, channels), F32)],
        compiler_params=params(),
        name="proj_back",
    )(*proj)

    own = lax.psum_scatter(part, "head", scatter_dimension=0, tiled=True)
    slab = own.shape[0]
    start = lax.axis_index("head") * slab
    x_own = lax.dynamic_slice_in_dim(x, start, slab, 0)
    cot_own = lax.dynamic_slice_in_dim(cot, start, slab, 0)
    size = slab // 3
    fin = (own, x_own, cot_own, gain, w_bc)
    grad_own, g_w_bc, g_norm = pl.pallas_call(
        last_kernel,
        grid=(slab // size,),
        in_specs=[rows(width + bc_width, size), rows(width, size), rows(width, size), whole(gain), whole(w_bc)],
        out_specs=[rows(width, size), fixed(width, bc_width), fixed(1, width)],
        out_shape=[shape((slab, width), BF16), shape((width, bc_width)), shape((1, width))],
        compiler_params=params(),
        name="last",
    )(*fin)
    grad_in = lax.all_gather(grad_own, "head", axis=0, tiled=True)[None]

    g_w_gate, g_w_out = lax.psum((g_w_gate.astype(BF16), g_w_out.astype(BF16)), ("seq", "dp"))
    g_w_value = lax.psum(g_w_value.astype(BF16), ("seq", "dp"))
    g_w_bc = lax.psum(g_w_bc.astype(BF16), ("seq", "dp", "head"))
    g_norm, g_conv_bc = lax.psum((g_norm, g_conv[:, inner:]), ("seq", "dp", "head"))
    g_w_step, g_conv, g_dt, g_log, g_skip, g_out_gain = lax.psum(
        (g_w_step, g_conv[:, :inner], g_dt, g_log, g_skip, g_out_gain), ("seq", "dp")
    )
    return (
        block_out,
        grad_in,
        g_norm[0],
        g_w_gate.astype(F32),
        g_w_value.astype(F32),
        g_w_bc.astype(F32),
        g_w_step,
        g_conv[: n_taps + 1],
        g_conv_bc[: n_taps + 1],
        g_dt[0],
        g_log[0],
        g_skip.reshape(heads, head_dim).sum(axis=1),
        g_out_gain[0],
        g_w_out.astype(F32),
    )


def solution(mesh):
    return jax.shard_map(
        on_device,
        mesh=mesh,
        in_specs=(
            P("dp", "seq", None),
            P("dp", "seq"),
            P(),
            P(None, "head"),
            P(None, "head"),
            P(),
            P(None, "head"),
            P(None, "head"),
            P(),
            P("head"),
            P("head"),
            P("head"),
            P("head"),
            P("head", None),
            P("dp", "seq", "head"),
        ),
        out_specs=(
            P("dp", "seq", "head"),
            P("dp", "seq", None),
            P(),
            P(None, "head"),
            P(None, "head"),
            P(),
            P(None, "head"),
            P(None, "head"),
            P(),
            P("head"),
            P("head"),
            P("head"),
            P("head"),
            P("head", None),
        ),
        check_vma=False,
    )
```

```python
import functools
import types

import jax
import jax.numpy as jnp
from jax import lax
from jax.experimental import pallas as pl
from jax.experimental.pallas import tpu as pltpu
from jax.sharding import PartitionSpec as P

BLOCK = 256
EDGE = 8
TAIL = 16
EPS = 1e-05
NEG = -1e30
F32 = jnp.float32
BF16 = jnp.bfloat16
NN = (((1,), (0,)), ((), ()))
NT = (((1,), (1,)), ((), ()))
TN = (((0,), (0,)), ((), ()))
MESH = pl.DeviceIdType.MESH
CUM, AUX, DYY, STEP, TO_END, INTO, RMS = 8, 16, 24, 32, 40, 48, 56
DIRECT = 8
LAG = 4
HEAD_AXIS, SEQ_AXIS, DP_AXIS = "head", "seq", "dp"
COT, HALO, ENDS, CARRY, BACK, SUM, OUT, PART, GRAD, EDGES, BC, BCG, PACK1, PACK2, PACK3 = (
    "cot", "halo", "ends", "carry", "back", "sum", "out", "part", "grad", "edge", "bc", "bcg", "pack1", "pack2", "pack3"
)
WO, WG, WV, WQ = "wo", "wg", "wv", "wq"
VMEM_LIMIT = 63 * 1024 * 1024


def dot(a, b, dims=NN):
    return lax.dot_general(a, b, dims, preferred_element_type=F32)


def halves(v):
    hi = v.astype(BF16)
    return hi, (v - hi.astype(F32)).astype(BF16)


def dot_left(v, m, dims=NN):
    hi, lo = halves(v)
    return dot(hi, m, dims) + dot(lo, m, dims)


def dot_right(m, v, dims=NN):
    hi, lo = halves(v)
    return dot(m, hi, dims) + dot(m, lo, dims)


def dot3(a, b, dims=NN):
    (ah, al), (bh, bl) = halves(a), halves(b)
    return dot(ah, bh, dims) + (dot(al, bh, dims) + dot(ah, bl, dims))


def score_pair(c, b, first):
    hi, lo = halves(c)
    cc, bb = jnp.concatenate([hi, lo], axis=1), jnp.concatenate([b, b], axis=1)
    return dot(cc, bb, NT) if first else dot(bb, cc, NT)


def sigmoid(v):
    return 1.0 / (1.0 + jnp.exp(-v))


def softplus(v):
    return jnp.maximum(v, 0.0) + jnp.log1p(jnp.exp(-jnp.abs(v)))


def iota(shape, axis):
    return lax.broadcasted_iota(jnp.int32, shape, axis)


def in_norm(x, gain):
    r = lax.rsqrt(jnp.mean(x * x, axis=1, keepdims=True) + EPS)
    return (x * r * gain).astype(BF16)


def repeat(n, body):
    def run(i, carry):
        body(i)
        return carry

    lax.fori_loop(0, n, run, 0)


def kernel(r):
    nh, ns = lax.axis_size(HEAD_AXIS), lax.axis_size(SEQ_AXIS)
    head, seq, dp = lax.axis_index(HEAD_AXIS), lax.axis_index(SEQ_AXIS), lax.axis_index(DP_AXIS)
    me = {HEAD_AXIS: head, SEQ_AXIS: seq, DP_AXIS: dp}
    count = {HEAD_AXIS: nh, SEQ_AXIS: ns, DP_AXIS: 2}
    tokens, width = r.x.shape
    inner, heads = r.wg.shape[1], r.ws.shape[0]
    state = r.wbc.shape[1] // 2
    channels = inner + 2 * state
    blocks, part, slab = tokens // BLOCK, width // nh, BLOCK // nh
    inner_all = inner * nh
    n_taps = r.cv.shape[0] - 1
    lanes = 2 * (inner // heads)

    def at(c):
        return pl.ds(pl.multiple_of(c * BLOCK, BLOCK), BLOCK)

    left, upper_half = lax.rem(head, 2), lax.div(head, 2)
    square = [head, 2 * upper_half + 1 - left, 2 * (1 - upper_half) + left, nh - 1 - head]

    def other(axis, o):
        if axis == HEAD_AXIS:
            return square[abs(o)]
        return lax.rem(me[axis] + o + count[axis], count[axis])

    def link(name, index, axis, o, src, dst):
        return pltpu.make_async_remote_copy(
            src_ref=src,
            dst_ref=dst,
            send_sem=getattr(r, name + "_s").at[index],
            recv_sem=getattr(r, name + "_r").at[index],
            device_id={axis: other(axis, o)},
            device_id_type=MESH,
        )

    def sent(name, index, axis, o, src):
        link(name, index, axis, o, src, src).wait_send()

    def came(name, index, axis, o, dst):
        link(name, index, axis, o, dst, dst).wait_recv()

    def gather_1(name, base, view):
        for o in (1, 2):
            link(name, base + o - 1, HEAD_AXIS, o, view(head), view(head)).start()

    def gather_2(name, base, view, half):
        for o in (1, 2):
            came(name, base + o - 1, HEAD_AXIS, o, view(square[o]))
            piece = half(square[o], o - 1)
            link(name, base + 1 + o, HEAD_AXIS, 3 - o, piece, piece).start()

    def gather_3(name, base, view, half):
        for o in (1, 2):
            came(name, base + 1 + o, HEAD_AXIS, 3 - o, half(square[3], o - 1))
            sent(name, base + o - 1, HEAD_AXIS, o, view(head))
            sent(name, base + 1 + o, HEAD_AXIS, 3 - o, half(square[o], o - 1))

    def scatter_1(name, base, block, inbox):
        for o in (1, 2):
            link(name, base + 2 * o - 2, HEAD_AXIS, o, block(square[o], o - 1), inbox.at[base + 2 * o - 2]).start()
            link(name, base + 2 * o - 1, HEAD_AXIS, o, block(square[3], o - 1), inbox.at[base + 2 * o - 1]).start()

    def scatter_2(name, base, block, inbox):
        for o in (1, 2):
            index = base + 2 * o - 1
            came(name, index, HEAD_AXIS, o, inbox.at[index])
            mine = block(square[3 - o], o - 1)
            mine[...] = (mine[...].astype(F32) + inbox[index].astype(F32)).astype(BF16)
            link(name, base + 3 + o, HEAD_AXIS, 3 - o, mine, inbox.at[base + 3 + o]).start()

    def scatter_3(name, base, block, inbox):
        totals = []
        for o in (1, 2):
            total = block(head, o - 1)[...].astype(F32)
            for index, by in ((base + 2 * o - 2, o), (base + 3 + o, 3 - o)):
                came(name, index, HEAD_AXIS, by, inbox.at[index])
                total = total + inbox[index].astype(F32)
            totals.append(total)
        return totals

    def scatter_sent(name, base, block):
        for o in (1, 2):
            sent(name, base + 2 * o - 2, HEAD_AXIS, o, block(square[o], o - 1))
            sent(name, base + 2 * o - 1, HEAD_AXIS, o, block(square[3], o - 1))
            sent(name, base + 3 + o, HEAD_AXIS, 3 - o, block(square[3 - o], o - 1))

    own = pltpu.make_async_copy(r.cot, r.cot_all.at[head], r.load.at[0])
    own.start()
    row, col = iota((BLOCK, BLOCK), 0), iota((BLOCK, BLOCK), 1)
    r.upper[...] = (row <= col).astype(BF16)
    r.eye[...] = (row == col).astype(BF16)
    dim = inner // heads
    r.spread[...] = (iota((heads, inner), 1) // dim == iota((heads, inner), 0)).astype(BF16)
    r.collect[...] = (iota((inner, heads), 0) // dim == iota((inner, heads), 1)).astype(BF16)
    for sel, lane in ((r.sel_step, STEP), (r.sel_end, TO_END), (r.sel_into, INTO)):
        sel[...] = (iota((128, inner), 1) // dim + lane == iota((128, inner), 0)).astype(BF16)
    r.tok[...] = jnp.zeros_like(r.tok)
    r.doc_out[...] = jnp.broadcast_to(r.docs[0:1, tokens - 1 : tokens].astype(F32), r.doc_out.shape)
    barrier = pltpu.get_barrier_semaphore()
    for axis in (HEAD_AXIS, SEQ_AXIS, DP_AXIS):
        for o in range(1, count[axis]):
            pl.semaphore_signal(barrier, inc=1, device_id={axis: other(axis, o)}, device_id_type=MESH)
    pl.semaphore_wait(barrier, nh + ns + 2 - 3)
    own.wait()

    def cot_of(h):
        return r.cot_all.at[h]

    def cot_half(h, i):
        return r.cot_all.at[h, pl.ds(i * (tokens // 2), tokens // 2)]

    gather_1(COT, 0, cot_of)
    x_tail = r.x.at[pl.ds(tokens - TAIL, TAIL)]
    link(HALO, 0, SEQ_AXIS, 1, x_tail, r.halo_x).start()
    link(HALO, 1, SEQ_AXIS, 1, r.doc_out, r.doc_in).start()

    taps = jnp.concatenate([r.cv[...], r.cb[...]], axis=1)
    rate = -jnp.exp(r.alog[...])
    skip = dot_left(r.dskip[...], r.spread[...])
    gain, out_gain = r.gain[...], r.og[...]

    def conv_pre(window, taps):
        pre = taps[n_taps : n_taps + 1, :] + taps[0:1, :] * window[EDGE:]
        for k in range(1, n_taps):
            pre = pre + taps[k : k + 1, :] * window[EDGE - k : EDGE - k + BLOCK]
        return pre

    def doc_row(c):
        return r.docs[0:1, at(c)].astype(F32)

    def expand(v):
        return dot_left(v, r.spread[...])

    def expand_tok(rows, sel, cols=slice(None)):
        return dot_left(r.tok[rows, :], sel[:, cols])

    def project(c):
        rows = at(c)
        normed = in_norm(r.x[rows, :].astype(F32), gain)
        r.normed[rows, :] = normed
        r.z[rows, :] = dot(normed, r.wg[...])
        inside = pl.ds(pl.multiple_of(c * BLOCK + EDGE, EDGE), BLOCK)
        r.cin[inside, :inner] = dot(normed, r.wv[...])
        r.cin[inside, inner:] = dot(normed, r.wbc[...])
        r.tok[rows, 0:heads] = dot(normed, r.ws[...], NT) + r.dtb[...]

    repeat(blocks, project)

    came(HALO, 0, SEQ_AXIS, -1, r.halo_x)
    came(HALO, 1, SEQ_AXIS, -1, r.doc_in)
    opened = jnp.where(seq == 0, 0.0, 1.0)
    edge = in_norm(r.halo_x[...].astype(F32), gain)
    r.cin[0:EDGE, :inner] = dot(edge, r.wv[...])[TAIL - EDGE :] * opened
    r.cin[0:EDGE, inner:] = dot(edge, r.wbc[...])[TAIL - EDGE :] * opened
    r.doc_prev[...] = jnp.where(seq == 0, -1.0, r.doc_in[...])

    r.carry[...] = jnp.ones_like(r.carry)

    def steps(c):
        rows = at(c)
        around = pl.ds(pl.multiple_of(c * BLOCK, BLOCK), BLOCK + EDGE)
        pre = conv_pre(r.cin[around, inner:], taps[:, inner:])
        u = pre * sigmoid(pre)
        r.b[rows, :] = u[:, :state].astype(BF16)
        r.c[rows, :] = u[:, state:]
        docs = doc_row(c)
        prev = r.doc_prev[0:1, 0:1]
        before = jnp.concatenate([prev, docs[:, : BLOCK - 1]], axis=1)
        ends = docs[:, BLOCK - 1 :]
        marks = [docs, (docs == prev).astype(F32), (docs == before).astype(F32), (docs == ends).astype(F32)]
        marks = jnp.concatenate(marks + [jnp.zeros((4, BLOCK), F32)], axis=0).astype(BF16)
        aux = dot(r.eye[...], marks, NT)
        r.tok[rows, AUX : AUX + 8] = aux
        step = softplus(r.tok[rows, 0:heads])
        la = rate * step
        la_hi, la_lo = halves(la)
        cum = dot(r.upper[...], la_hi, TN) + dot(r.upper[...], la_lo, TN)
        r.cumt[:, at(c)] = dot(la_hi, r.upper[...], TN) + dot(la_lo, r.upper[...], TN)
        total = cum[BLOCK - 1 :, :]
        r.tok[rows, CUM : CUM + heads] = cum
        r.tok[rows, STEP : STEP + heads] = step
        r.tok[rows, TO_END : TO_END + heads] = jnp.exp(total - cum) * aux[:, 3:4]
        r.tok[rows, INTO : INTO + heads] = jnp.exp(cum) * aux[:, 1:2]
        kept = expand(jnp.exp(total) * (ends == prev).astype(F32))
        r.kept[c] = kept
        r.carry[...] = r.carry[...] * kept
        r.doc_prev[...] = jnp.broadcast_to(ends, r.doc_prev.shape)

    repeat(blocks, steps)

    pairs = heads // 2
    direct = ns <= DIRECT
    if direct:
        for o in range(1, ns):
            link(CARRY, o - 1, SEQ_AXIS, o, r.carry, r.carry_in.at[o - 1]).start()
    for pair in range(pairs):
        r.carry_part[pair] = r.carry[:, pair * lanes : (pair + 1) * lanes]
    r.own[...] = jnp.zeros_like(r.own)

    def relay(turn):
        pair = turn - seq

        @pl.when(jnp.logical_and(pair >= 0, pair < pairs))
        def _():
            @pl.when(seq > 0)
            def _():
                came(ENDS, pair, SEQ_AXIS, -1, r.end_in.at[pair])

            into = jnp.where(seq > 0, r.end_in[pair], 0.0)
            r.end_out[pair] = r.carry_part[pair] * into + r.own[pair]
            r.own[pair] = into

            @pl.when(seq < ns - 1)
            def _():
                link(ENDS, pair, SEQ_AXIS, 1, r.end_out.at[pair], r.end_in.at[pair]).start()

    for pair in range(pairs):
        cols = slice(pair * lanes, (pair + 1) * lanes)

        def own_states(c, pair=pair, cols=cols):
            rows = at(c)
            around = pl.ds(pl.multiple_of(c * BLOCK, BLOCK), BLOCK + EDGE)
            pre = conv_pre(r.cin[around, cols], taps[:, cols])
            xh = pre * sigmoid(pre)
            xs = xh * expand_tok(rows, r.sel_step, cols)
            r.xs[rows, cols] = xs.astype(BF16)
            r.y[rows, cols] = skip[:, cols] * xh
            inc = dot(r.b[rows, :], (xs * expand_tok(rows, r.sel_end, cols)).astype(BF16), TN)
            r.inc[c, :, cols] = inc
            r.own[pair] = r.kept[c, :, cols] * r.own[pair] + inc

        repeat(blocks, own_states)
        relay(pair)

    gather_2(COT, 0, cot_of, cot_half)

    def pass_back():
        @pl.when(seq < ns - 1)
        def _():
            came(BACK, 0, SEQ_AXIS, 1, r.back_in.at[0])

        into = jnp.where(seq < ns - 1, r.back_in[0].astype(F32), 0.0)
        r.back_out[...] = (r.carry[...] * into + r.end[...]).astype(BF16)
        r.end[...] = into

        @pl.when(seq > 0)
        def _():
            link(BACK, 0, SEQ_AXIS, -1, r.back_out, r.back_in.at[0]).start()
            sent(BACK, 0, SEQ_AXIS, -1, r.back_out)

    first = iota((BLOCK, lanes), 1) < lanes // 2

    def split(pair):
        zero = jnp.zeros_like(pair)
        return jnp.where(first, pair, zero), jnp.where(first, zero, pair)

    def intra(c):
        rows = at(c)
        cum, cumt = r.tok[rows, CUM : CUM + heads], r.cumt[:, at(c)]
        mask = jnp.where((row >= col) & (r.tok[rows, AUX : AUX + 1] == doc_row(c)), 0.0, NEG)
        scores = score_pair(r.c[rows, :], r.b[rows, :], True)
        for pair in range(heads // 2):
            cols = slice(pair * lanes, (pair + 1) * lanes)
            mixed = []
            for h in (2 * pair, 2 * pair + 1):
                decay = jnp.exp(cum[:, h : h + 1] - cumt[h : h + 1, :] + mask)
                mixed.append((scores * decay).astype(BF16))
            two = jnp.concatenate(split(r.xs[rows, cols]), axis=0)
            r.y[rows, cols] += dot(jnp.concatenate(mixed, axis=1), two)
        relay(pairs + c)

    repeat(blocks, intra)

    if ns - 1 > blocks:
        repeat(ns - 1 - blocks, lambda i: relay(pairs + blocks + i))
    for pair in range(pairs):
        r.end[:, pair * lanes : (pair + 1) * lanes] = r.own[pair]
    gather_3(COT, 0, cot_of, cot_half)

    def dgn_of(rows):
        total = dot(r.cot_all[0, rows, :], r.wo[:, :part], NT)
        for k in range(1, nh):
            total = total + dot(r.cot_all[k, rows, :], r.wo[:, k * part : (k + 1) * part], NT)
        return total

    ones = jnp.ones((8, inner), BF16)

    def sums(c):
        rows = at(c)
        si = r.end[...]
        r.end[...] = r.kept[c] * si + r.inc[c]
        r.inc[c] = si
        into = expand_tok(rows, r.sel_into)
        y = r.y[rows, :] + into * dot3(r.c[rows, :], si)
        r.y[rows, :] = y
        z = r.z[rows, :]
        g = y * (z * sigmoid(z))
        squares = dot_right(ones, g * g, NT)
        products = dot_right(ones, dgn_of(rows) * out_gain * g, NT)
        r.sum_out[c] = jnp.concatenate([squares[0:1], products[0:1], jnp.zeros((6, BLOCK), F32)], axis=0)
        for o in range(1, nh):
            index = c * (nh - 1) + o - 1
            link(SUM, index, HEAD_AXIS, o, r.sum_out.at[c], r.sum_in.at[index]).start()
        r.parts[c, :, :width] = dot((g * out_gain).astype(BF16), r.wo[...]).astype(BF16)
        scatter_1(OUT, 6 * c, out_block(c), r.out_in)

    def out_block(c):
        half = BLOCK // 2
        return lambda h, i: r.parts.at[c, pl.ds(i * half, half), pl.ds(pl.multiple_of(h * part, part), part)]

    repeat(blocks, sums)
    r.inc[blocks] = r.end[...]

    r.end[...] = jnp.zeros_like(r.end)
    r.prod[...] = jnp.ones_like(r.prod)
    r.pack[...] = jnp.zeros_like(r.pack)
    r.g_gain[...] = jnp.zeros_like(r.g_gain)

    def gate(c):
        rows = at(c)
        scatter_2(OUT, 6 * c, out_block(c), r.out_in)
        total = r.sum_out[c]
        for o in range(1, nh):
            index = c * (nh - 1) + o - 1
            came(SUM, index, HEAD_AXIS, -o, r.sum_in.at[index])
            total = total + r.sum_in[index]
        both = dot_right(r.eye[...], total, NT)
        y, z = r.y[rows, :], r.z[rows, :]
        dgn = dgn_of(rows)
        sig = sigmoid(z)
        act = z * sig
        g = y * act
        rms = lax.rsqrt(both[:, 0:1] / inner_all + EPS)
        r.tok[rows, RMS : RMS + 1] = rms
        gr = g * rms
        r.xs[rows, :] = (gr * out_gain).astype(BF16)
        r.g_gain[...] += jnp.sum(dgn * gr, axis=0, keepdims=True)
        dg = rms * (dgn * out_gain) - g * (rms * rms * rms * both[:, 1:2] / inner_all)
        dy = dg * act
        dyb = dy.astype(BF16)
        r.dy[rows, :] = dyb
        r.tok[rows, DYY : DYY + heads] = dot_left(dyb.astype(F32) * y, r.collect[...])
        r.dz[rows, :] = (dg * y * (sig * (1.0 + z * (1.0 - sig)))).astype(BF16)
        into = expand_tok(rows, r.sel_into)
        r.end[...] += r.prod[...] * dot(r.c[rows, :].astype(BF16), (dy * into).astype(BF16), TN)
        r.prod[...] = r.prod[...] * r.kept[c]

    repeat(blocks, gate)

    if direct:
        r.back_out[...] = r.end[...].astype(BF16)
        for o in range(1, ns):
            link(BACK, o - 1, SEQ_AXIS, o, r.back_out, r.back_in.at[o - 1]).start()

    r.gw_out[...] = jnp.zeros_like(r.gw_out)
    r.gw_gate[...] = jnp.zeros_like(r.gw_gate)

    def weight_grads(c):
        rows = at(c)
        gn = r.xs[rows, :]
        for k in range(nh):
            r.gw_out[:, k * part : (k + 1) * part] += dot(gn, r.cot_all[k, rows, :], TN)
        r.gw_gate[...] += dot(r.normed[rows, :], r.dz[rows, :], TN)

    repeat(blocks, weight_grads)

    def ref(name, kind):
        return getattr(r, name + kind)

    def half_of(name, source, core):
        if name in (WO, WQ):
            half = source.shape[1] // 2
            return source.at[:, pl.ds(pl.multiple_of(core * half, half), half)]
        half = source.shape[0] // 2
        return source.at[pl.ds(pl.multiple_of(core * half, half), half)]

    def piece_of(name, half, place):
        piece = half.shape[0] // ns
        return half.at[pl.ds(pl.multiple_of(place * piece, piece), piece)]

    def total_a(name, source):
        return link(name + "a", 0, DP_AXIS, 1, half_of(name, source, 1 - dp), ref(name, "_pair"))

    def total_b(name, source):
        total_a(name, source).wait_send()
        came(name + "a", 0, DP_AXIS, 1, ref(name, "_pair"))
        mine = ref(name, "_mine")
        mine[...] = (half_of(name, source, dp)[...] + ref(name, "_pair")[...]).astype(mine.dtype)
        for o in range(1, ns):
            theirs = piece_of(name, mine, other(SEQ_AXIS, o))
            link(name + "b", o - 1, SEQ_AXIS, o, theirs, ref(name, "_in").at[o - 1]).start()

    def result(name, core, place):
        return piece_of(name, half_of(name, ref(name, "_sum"), core), place)

    def total_c(name):
        total = piece_of(name, ref(name, "_mine"), seq)[...].astype(F32)
        for o in range(1, ns):
            came(name + "b", o - 1, SEQ_AXIS, -o, ref(name, "_in").at[o - 1])
            total = total + ref(name, "_in")[o - 1].astype(F32)
        mine = result(name, dp, seq)
        mine[...] = total.astype(mine.dtype)
        for o in range(1, ns):
            link(name + "c", o - 1, SEQ_AXIS, o, mine, mine).start()
        link(name + "d", 0, DP_AXIS, 1, mine, mine).start()

    def total_d(name):
        for o in range(1, ns):
            piece = result(name, dp, other(SEQ_AXIS, -o))
            came(name + "c", o - 1, SEQ_AXIS, -o, piece)
            link(name + "d", o, DP_AXIS, 1, piece, piece).start()

    def total_e(name):
        for o in range(ns):
            came(name + "d", o, DP_AXIS, 1, result(name, 1 - dp, other(SEQ_AXIS, -o)))
            sent(name + "d", o, DP_AXIS, 1, result(name, dp, other(SEQ_AXIS, -o)))
        for o in range(1, ns):
            sent(name + "b", o - 1, SEQ_AXIS, o, piece_of(name, ref(name, "_mine"), other(SEQ_AXIS, o)))
            sent(name + "c", o - 1, SEQ_AXIS, o, result(name, dp, seq))

    total_a(WO, r.gw_out).start()
    total_a(WG, r.gw_gate).start()

    def chain_back(i):
        k = ns - 1 - i
        slot = jnp.maximum(lax.rem(seq - k + ns, ns) - 1, 0)

        @pl.when(k > seq)
        def _():
            r.end[...] = r.carry_in[slot] * r.end[...] + r.back_in[slot].astype(F32)

    if direct:
        for o in range(1, ns):
            came(BACK, o - 1, SEQ_AXIS, -o, r.back_in.at[o - 1])
            came(CARRY, o - 1, SEQ_AXIS, -o, r.carry_in.at[o - 1])
        r.end[...] = jnp.zeros_like(r.end)
        repeat(ns, chain_back)
    else:
        pass_back()
    r.g_dt[...] = jnp.zeros_like(r.g_dt)
    r.g_log[...] = jnp.zeros_like(r.g_log)
    r.g_skip[...] = jnp.zeros_like(r.g_skip)
    r.g_conv[...] = jnp.zeros_like(r.g_conv)
    r.gw_bc[...] = jnp.zeros_like(r.gw_bc)
    r.g_norm[...] = jnp.zeros_like(r.g_norm)

    def back(c):
        rows = at(c)
        around = pl.ds(pl.multiple_of(c * BLOCK, BLOCK), BLOCK + EDGE)
        inside = pl.ds(pl.multiple_of(c * BLOCK + EDGE, EDGE), BLOCK)
        b_mat, c_full = r.b[rows, :], r.c[rows, :]
        c_mat = c_full.astype(BF16)
        v = r.tok[rows, 0:heads]
        step = r.tok[rows, STEP : STEP + heads]
        cum, cumt, aux = r.tok[rows, CUM : CUM + heads], r.cumt[:, at(c)], r.tok[rows, AUX : AUX + 8]
        mask = jnp.where((row <= col) & (aux[:, 0:1] == doc_row(c)), 0.0, NEG)
        scores = score_pair(c_full, b_mat, False)
        d_scores = jnp.zeros((BLOCK, BLOCK), F32)
        d_b = jnp.zeros((BLOCK, state), F32)
        d_c = jnp.zeros((BLOCK, state), F32)
        d_step_own = jnp.zeros((BLOCK, heads), F32)
        d_cum = r.tok[rows, DYY : DYY + heads]
        through = jnp.zeros((1, heads), F32)

        def conv_grad(d_u, window, pre, sig, cols):
            d_pre = d_u * (sig * (1.0 + pre * (1.0 - sig)))
            for k in range(n_taps):
                shifted = window[EDGE - k : EDGE - k + BLOCK]
                r.g_conv[k : k + 1, cols] += jnp.sum(d_pre * shifted, axis=0, keepdims=True)
            r.g_conv[n_taps : n_taps + 1, cols] += jnp.sum(d_pre, axis=0, keepdims=True)
            r.cin[inside, cols] = d_pre

        for pair in range(heads // 2):
            cols = slice(pair * lanes, (pair + 1) * lanes)
            window = r.cin[around, cols]
            pre = conv_pre(window, taps[:, cols])
            sig = sigmoid(pre)
            xh = pre * sig
            step_e, to_end_e, into_e = (expand_tok(rows, sel, cols) for sel in (r.sel_step, r.sel_end, r.sel_into))
            xs = xh * step_e
            xsb = xs.astype(BF16)
            dyb = r.dy[rows, cols]
            dy = dyb.astype(F32)
            adj = r.end[:, cols]
            dye = dy * into_e
            d_c = d_c + dot3(dye, r.inc[c, :, cols], NT)
            d_b = d_b + dot3(xs * to_end_e, adj, NT)
            d_xs_inter = to_end_e * dot(b_mat, adj.astype(BF16))
            two = split(dyb)
            mixed = []
            for i, h in enumerate((2 * pair, 2 * pair + 1)):
                decay = jnp.exp(cumt[h : h + 1, :] - cum[:, h : h + 1] + mask)
                mixed.append((scores * decay).astype(BF16))
                d_scores = d_scores + dot(xsb, two[i], NT) * decay
            d_xs_intra = dot(jnp.concatenate(mixed, axis=1), jnp.concatenate(two, axis=0))
            d_xs = d_xs_intra + d_xs_inter
            collect = r.collect[cols, :]
            d_step_own = d_step_own + dot_left(xh * d_xs, collect)
            lost = skip[:, cols] * (dy * xh) + (xsb.astype(F32) * d_xs_intra + xs * d_xs_inter)
            d_cum = d_cum - dot_left(lost, collect)
            ended = jnp.sum(adj * r.inc[c + 1, :, cols], axis=0, keepdims=True)
            through = through + dot_left(ended, collect)
            r.g_skip[:, cols] += jnp.sum(dy * xh, axis=0, keepdims=True)
            r.end[:, cols] = r.kept[c, :, cols] * adj + dot(c_mat, dye.astype(BF16), TN)
            conv_grad(skip[:, cols] * dy + step_e * d_xs, window, pre, sig, cols)
        d_sb = d_scores.astype(BF16)
        d_b = d_b + dot(d_sb, c_mat)
        d_c = d_c + dot(d_sb, b_mat, TN)
        cols = slice(inner, channels)
        window = r.cin[around, cols]
        pre = conv_pre(window, taps[:, cols])
        conv_grad(jnp.concatenate([d_b, d_c], axis=1), window, pre, sigmoid(pre), cols)
        d_la = (dot_right(r.upper[...], d_cum) + through) * aux[:, 2:3]
        r.g_log[...] += jnp.sum(rate * step * d_la, axis=0, keepdims=True)
        d_v = (d_step_own + rate * d_la) * sigmoid(v)
        r.g_dt[...] += jnp.sum(d_v, axis=0, keepdims=True)
        r.dstep[rows, :] = d_v.astype(BF16)

    def project_back(c):
        rows = at(c)
        window = r.cin[pl.ds(pl.multiple_of(c * BLOCK + EDGE, EDGE), BLOCK + EDGE), :]
        d_in = taps[0:1, :] * window[:BLOCK]
        for k in range(1, n_taps):
            d_in = d_in + taps[k : k + 1, :] * window[k : k + BLOCK]
        d_val = d_in[:, :inner].astype(BF16)
        dstep = r.dstep[rows, :]
        normed = r.normed[rows, :]
        r.gw_value[...] += dot(normed, d_val, TN)
        r.pack[0:heads, :] += dot(dstep, normed, TN)
        d_part = dot(r.dz[rows, :], r.wg[...], NT) + dot(d_val, r.wv[...], NT) + dot(dstep, r.ws[...])
        scatter_sent(OUT, 6 * c, out_block(c))
        r.parts[c, :, :width] = d_part.astype(BF16)
        r.parts[c, :, width:] = d_in[:, inner:].astype(BF16)
        scatter_1(PART, 6 * c, part_block(c), r.part_in)

    def part_block(c):
        half = slab // 2
        return lambda h, i: r.parts.at[c, pl.ds(pl.multiple_of(h * slab + i * half, half), half)]

    def combine(c):
        scatter_2(PART, 6 * c, part_block(c), r.part_in)

    def slab_of(c):
        return lambda h: r.normed.at[pl.ds(pl.multiple_of(c * BLOCK + h * slab, slab), slab)]

    def slab_half(c):
        half = slab // 2
        return lambda h, i: r.normed.at[pl.ds(pl.multiple_of(c * BLOCK + h * slab + i * half, half), half)]

    def forward(c):
        gather_2(GRAD, 4 * c, slab_of(c), slab_half(c))

    def own_slab(c):
        return pl.ds(pl.multiple_of(c * BLOCK + head * slab, slab), slab)

    def finish(c):
        rows = own_slab(c)
        total = jnp.concatenate(scatter_3(PART, 6 * c, part_block(c), r.part_in), axis=0)
        x = r.x[rows, :].astype(F32)
        norm = lax.rsqrt(jnp.mean(x * x, axis=1, keepdims=True) + EPS)
        xr = x * norm
        d_bc = total[:, width:].astype(BF16)
        d_normed = total[:, :width] + dot(d_bc, r.wbc[...], NT)
        r.gw_bc[...] += dot(r.normed[rows, :], d_bc, TN)
        r.g_norm[...] += jnp.sum(d_normed * xr, axis=0, keepdims=True)
        q = d_normed * gain
        d_x = norm * q - xr * (norm * norm * jnp.mean(q * x, axis=1, keepdims=True))
        cot = jnp.concatenate([r.cot_all[k, rows, :] for k in range(nh)], axis=1)
        r.normed[rows, :] = (d_x + cot.astype(F32)).astype(BF16)
        gather_1(GRAD, 4 * c, slab_of(c))

    def add_residual(c):
        cols = pl.ds(pl.multiple_of(head * part, part), part)
        half = BLOCK // 2
        for i, total in enumerate(scatter_3(OUT, 6 * c, out_block(c), r.out_in)):
            rows = pl.ds(pl.multiple_of(c * BLOCK + i * half, half), half)
            scaled = r.tok[rows, RMS : RMS + 1] * total
            r.block_out[rows, :] = (scaled + r.x[rows, cols].astype(F32)).astype(BF16)

    def reverse(t):
        c = blocks - 1 - t
        back(c)

        @pl.when(t == 0)
        def _():
            total_b(WO, r.gw_out)
            total_b(WG, r.gw_gate)
            r.gw_value[...] = jnp.zeros_like(r.gw_value)

        @pl.when(t >= 1)
        def _():
            add_residual(c)
            project_back(c)

        @pl.when(t >= 2)
        def _():
            combine(c + 1)

        @pl.when(t == 2)
        def _():
            total_c(WO)
            total_c(WG)

        @pl.when(t >= LAG)
        def _():
            finish(c + LAG - 1)

        @pl.when(t == 4)
        def _():
            total_d(WO)
            total_d(WG)

    repeat(blocks, reverse)

    first_rows = r.cin.at[pl.ds(EDGE, EDGE)]
    last_rows = r.cin.at[pl.ds(EDGE + tokens, EDGE)]
    link(EDGES, 0, SEQ_AXIS, -1, first_rows, last_rows).start()
    order = [*range(blocks - 2, -1, -1), blocks - 1]
    waiting = order[max(blocks - LAG, 0) :]
    add_residual(blocks - 1)
    combine(0)
    came(EDGES, 0, SEQ_AXIS, 1, last_rows)

    @pl.when(seq == ns - 1)
    def _():
        r.cin[EDGE + tokens :, :] = jnp.zeros((EDGE, channels), F32)

    project_back(blocks - 1)
    total_a(WV, r.gw_value).start()
    r.pack[9 : 9 + n_taps + 1, :channels] = r.g_conv[: n_taps + 1, :]
    r.pack[14:15, :inner] = r.g_gain[...]
    r.pack[15:16, 0:heads] = r.g_dt[...]
    r.pack[15:16, 128 : 128 + heads] = r.g_log[...]
    r.pack[15:16, 256 : 256 + heads] = dot_left(r.g_skip[...], r.collect[...])
    for c in waiting[:-2]:
        finish(c)
    total_b(WV, r.gw_value)
    finish(0)
    combine(blocks - 1)
    for c in order[:-2]:
        forward(c)
    finish(blocks - 1)

    r.pack[8:9, :] = r.g_norm[...]
    quarter = width // nh
    r.bc_out[...] = r.gw_bc[...].astype(BF16)
    r.pack_out[...] = r.pack[8:16, :]
    for o in range(1, nh):
        rows = pl.ds(pl.multiple_of(other(HEAD_AXIS, o) * quarter, quarter), quarter)
        link(BC, o - 1, HEAD_AXIS, o, r.bc_out.at[rows], r.bc_in[o - 1]).start()
        link(PACK1, o - 1, HEAD_AXIS, o, r.pack_out, r.pack1_in.at[o - 1]).start()
    for o in range(1, nh):
        came(PACK1, o - 1, HEAD_AXIS, -o, r.pack1_in.at[o - 1])
        r.pack[8:9, :] += r.pack1_in[o - 1, 0:1, :]
        r.pack[9 : 9 + n_taps + 1, inner:channels] += r.pack1_in[o - 1, 1 : 2 + n_taps, inner:channels]
    link(PACK2, 0, DP_AXIS, 1, r.pack, r.pack2_in).start()
    rows = pl.ds(pl.multiple_of(head * quarter, quarter), quarter)
    mine = r.gw_bc[rows, :]
    for o in range(1, nh):
        came(BC, o - 1, HEAD_AXIS, -o, r.bc_in[o - 1])
        mine = mine + r.bc_in[o - 1][...].astype(F32)
    r.gw_q[...] = mine
    total_a(WQ, r.gw_q).start()
    came(PACK2, 0, DP_AXIS, 1, r.pack2_in)
    link(PACK2, 0, DP_AXIS, 1, r.pack, r.pack2_in).wait_send()
    r.pack[...] += r.pack2_in[...]
    for o in range(1, ns):
        link(PACK3, o - 1, SEQ_AXIS, o, r.pack, r.pack3_in.at[o - 1]).start()
    for c in order[-2:]:
        forward(c)
    total_b(WQ, r.gw_q)
    total_c(WV)
    total_c(WQ)
    total_d(WV)
    total_d(WQ)
    total_e(WQ)
    for o in range(nh):
        rows = pl.ds(pl.multiple_of(other(HEAD_AXIS, o) * quarter, quarter), quarter)
        if o == 0:
            r.bc_sum[rows, :] = r.wq_sum[...].astype(BF16)
            mine = r.bc_sum.at[rows]
        else:
            link(BCG, o - 1, HEAD_AXIS, o, mine, mine).start()
    total = r.pack[...]
    for o in range(1, ns):
        came(PACK3, o - 1, SEQ_AXIS, -o, r.pack3_in.at[o - 1])
        total = total + r.pack3_in[o - 1]
    r.small[...] = total
    total_e(WO)
    total_e(WG)
    total_e(WV)
    for o in range(1, nh):
        rows = pl.ds(pl.multiple_of(other(HEAD_AXIS, -o) * quarter, quarter), quarter)
        came(BCG, o - 1, HEAD_AXIS, -o, r.bc_sum.at[rows])
        sent(BCG, o - 1, HEAD_AXIS, o, mine)
        rows = pl.ds(pl.multiple_of(other(HEAD_AXIS, o) * quarter, quarter), quarter)
        sent(BC, o - 1, HEAD_AXIS, o, r.bc_out.at[rows])
        sent(PACK1, o - 1, HEAD_AXIS, o, r.pack_out)
    for o in range(1, ns):
        sent(PACK3, o - 1, SEQ_AXIS, o, r.pack)
        if direct:
            sent(BACK, o - 1, SEQ_AXIS, o, r.back_out)
            sent(CARRY, o - 1, SEQ_AXIS, o, r.carry)
    sent(HALO, 0, SEQ_AXIS, 1, x_tail)
    sent(HALO, 1, SEQ_AXIS, 1, r.doc_out)
    sent(EDGES, 0, SEQ_AXIS, -1, first_rows)

    @pl.when(seq < ns - 1)
    def _():
        for pair in range(pairs):
            sent(ENDS, pair, SEQ_AXIS, 1, r.end_out.at[pair])

    def drain(c):
        for o in range(1, nh):
            sent(SUM, c * (nh - 1) + o - 1, HEAD_AXIS, o, r.sum_out.at[c])
        scatter_sent(PART, 6 * c, part_block(c))
        gather_3(GRAD, 4 * c, slab_of(c), slab_half(c))

    repeat(blocks, drain)
    done = pltpu.make_async_copy(r.normed, r.grad_in, r.load.at[0])
    done.start()
    done.wait()


def write_kernel(n, *refs):
    small = refs[n]
    for source, target in zip(refs[:n], refs[n + 1 :]):
        target[...] = source[...].astype(target.dtype)
    norm, step, conv_v, conv_b, dt, log, skip, gain = refs[2 * n + 1 :]
    inner, heads, taps = conv_v.shape[1], dt.shape[1], conv_v.shape[0]

    @pl.when(pl.program_id(0) == 0)
    def _():
        norm[...] = small[8:9, :]
        step[...] = small[0:heads, :]
        conv_v[...] = small[9 : 9 + taps, :inner]
        conv_b[...] = small[9 : 9 + taps, inner : inner + conv_b.shape[1]]
        dt[...] = small[15:16, 0:heads]
        log[...] = small[15:16, 128 : 128 + heads]
        skip[...] = small[15:16, 256 : 256 + heads]
        gain[...] = small[14:15, :inner]


def on_device(
    hidden_in, doc_ids, norm_gain, w_gate, w_value, w_bc, w_step, conv_value, conv_bc, dt_bias, a_log, d_skip,
    out_gain, w_out, cotangent,
):
    x, cot = hidden_in[0], cotangent[0]
    tokens, width = x.shape
    inner, heads = w_gate.shape[1], w_step.shape[1]
    bc_width, head_dim = w_bc.shape[1], inner // heads
    state = bc_width // 2
    channels = inner + bc_width
    blocks = tokens // BLOCK
    nh, ns = lax.axis_size(HEAD_AXIS), lax.axis_size(SEQ_AXIS)
    part, slab = width // nh, BLOCK // nh
    n_taps = conv_value.shape[0] - 1
    vmem, hbm = pltpu.VMEM, pl.ANY
    inbox = ns - 1 if ns <= DIRECT else 1
    inputs = dict(
        x=x, cot=cot, docs=doc_ids, gain=norm_gain[None], wg=w_gate, wv=w_value, wbc=w_bc,
        ws=w_step.T, wo=w_out, cv=conv_value, cb=conv_bc, dtb=dt_bias[None], alog=a_log[None],
        dskip=d_skip[None], og=out_gain[None],
    )
    outputs = dict(
        block_out=((tokens, part), BF16),
        grad_in=((tokens, width), BF16),
        wg_sum=(w_gate.shape, BF16),
        wv_sum=(w_value.shape, BF16),
        wo_sum=(w_out.shape, BF16),
        bc_sum=(w_bc.shape, BF16),
        small=((16, width), F32),
    )
    scratch = dict(
        cot_all=vmem((nh, tokens, part), BF16),
        halo_x=vmem((TAIL, width), BF16),
        doc_out=vmem((8, 128), F32),
        doc_in=vmem((8, 128), F32),
        doc_prev=vmem((8, 128), F32),
        upper=vmem((BLOCK, BLOCK), BF16),
        eye=vmem((BLOCK, BLOCK), BF16),
        spread=vmem((heads, inner), BF16),
        collect=vmem((inner, heads), BF16),
        normed=vmem((tokens, width), BF16),
        z=vmem((tokens, inner), F32),
        cin=vmem((EDGE + tokens + EDGE, channels), F32),
        y=vmem((tokens, inner), F32),
        xs=vmem((tokens, inner), BF16),
        dy=vmem((tokens, inner), BF16),
        b=vmem((tokens, state), BF16),
        c=vmem((tokens, state), F32),
        tok=vmem((tokens, 128), F32),
        cumt=vmem((heads, tokens), F32),
        dstep=vmem((tokens, heads), BF16),
        inc=vmem((blocks + 1, state, inner), F32),
        kept=vmem((blocks, 1, inner), F32),
        end=vmem((state, inner), F32),
        own=vmem((heads // 2, state, 2 * head_dim), F32),
        end_out=vmem((heads // 2, state, 2 * head_dim), F32),
        end_in=vmem((heads // 2, state, 2 * head_dim), F32),
        carry_part=vmem((heads // 2, 1, 2 * head_dim), F32),
        sel_step=vmem((128, inner), BF16),
        sel_end=vmem((128, inner), BF16),
        sel_into=vmem((128, inner), BF16),
        back_out=vmem((state, inner), BF16),
        back_in=vmem((inbox, state, inner), BF16),
        carry=vmem((1, inner), F32),
        carry_in=vmem((inbox, 1, inner), F32),
        prod=vmem((1, inner), F32),
        sum_out=vmem((blocks, 8, BLOCK), F32),
        sum_in=vmem((blocks * (nh - 1), 8, BLOCK), F32),
        parts=vmem((blocks, BLOCK, width + bc_width), BF16),
        out_in=vmem((blocks * 6, BLOCK // 2, part), BF16),
        part_in=vmem((blocks * 6, slab // 2, width + bc_width), BF16),
        gw_out=vmem(w_out.shape, F32),
        wq_sum=vmem((width // nh, bc_width), F32),
        dz=vmem((tokens, inner), BF16),
        g_gain=vmem((1, inner), F32),
        g_dt=vmem((1, heads), F32),
        g_log=vmem((1, heads), F32),
        g_skip=vmem((1, inner), F32),
        g_conv=vmem((8, channels), F32),
        g_norm=vmem((1, width), F32),
        pack=vmem((16, width), F32),
        pack_out=vmem((8, width), F32),
        pack1_in=vmem((nh - 1, 8, width), F32),
        pack2_in=vmem((16, width), F32),
        pack3_in=vmem((ns - 1, 16, width), F32),
        load=pltpu.SemaphoreType.DMA((1,)),
    )
    for name, (rows, cols), kind in (
        (WO, (inner, width // 2), BF16), (WG, (width // 2, inner), BF16), (WV, (width // 2, inner), BF16),
        (WQ, (width // nh, state), F32),
    ):
        if name != WV:
            scratch[name + "_pair"] = vmem((rows, cols), F32)
            scratch[name + "_mine"] = vmem((rows, cols), kind)
        scratch[name + "_in"] = vmem((ns - 1, rows // ns, cols), kind)
    counts = dict(
        cot=4, halo=2, ends=heads // 2, carry=ns - 1, back=ns - 1, sum=blocks * (nh - 1), out=blocks * 6,
        part=blocks * 6, grad=blocks * 4, edge=1, bc=nh - 1, bcg=nh - 1, pack1=nh - 1, pack2=1, pack3=ns - 1,
    )
    for name in (WO, WG, WV, WQ):
        counts |= {name + "a": 1, name + "b": ns - 1, name + "c": ns - 1, name + "d": ns}
    for name, n in counts.items():
        scratch[name + "_s"] = pltpu.SemaphoreType.DMA((n,))
        scratch[name + "_r"] = pltpu.SemaphoreType.DMA((n,))
    names = [*inputs, *outputs, *scratch]

    def run(*refs):
        r = types.SimpleNamespace(**dict(zip(names, refs)))
        quarter = width // nh
        r.gw_gate = r.gw_value = r.z.at[pl.ds(0, width)]
        r.wv_pair = r.z.at[pl.ds(width, width // 2)]
        r.gw_bc = r.y.at[pl.ds(0, width), pl.ds(0, bc_width)]
        r.gw_q = r.y.at[pl.ds(width, quarter), pl.ds(0, bc_width)]
        r.bc_out = r.xs.at[pl.ds(0, width), pl.ds(0, bc_width)]
        r.wv_mine = r.xs.at[pl.ds(width, width // 2)]
        r.bc_in = [r.dz.at[pl.ds(o * quarter, quarter), pl.ds(0, bc_width)] for o in range(nh - 1)]
        kernel(r)

    block_out, grad_in, g_gate, g_value, g_out, g_bc, small = pl.pallas_call(
        run,
        out_shape=[jax.ShapeDtypeStruct(*o) for o in outputs.values()],
        in_specs=[pl.BlockSpec(memory_space=hbm if name == "cot" else vmem) for name in inputs],
        out_specs=[pl.BlockSpec(memory_space=hbm if name == "grad_in" else vmem) for name in outputs],
        scratch_shapes=list(scratch.values()),
        compiler_params=pltpu.CompilerParams(
            collective_id=0, has_side_effects=True, vmem_limit_bytes=VMEM_LIMIT
        ),
        name="block",
    )(*inputs.values())
    steps = 8
    grads = (block_out, grad_in, g_gate, g_value, g_out, g_bc)
    kinds = (BF16, BF16, F32, F32, F32, F32)
    tiny = ((1, width), (heads, width), (n_taps + 1, inner), (n_taps + 1, bc_width), (1, heads), (1, heads), (1, heads),
            (1, inner))

    def split_rows(a):
        return pl.BlockSpec((a.shape[0] // steps, a.shape[1]), lambda i: (i, 0))

    def whole(dims):
        return pl.BlockSpec(dims, lambda i: (0, 0))

    outs = pl.pallas_call(
        functools.partial(write_kernel, len(grads)),
        grid=(steps,),
        in_specs=[*map(split_rows, grads), whole(small.shape)],
        out_specs=[*map(split_rows, grads), *map(whole, tiny)],
        out_shape=[jax.ShapeDtypeStruct(a.shape, k) for a, k in zip(grads, kinds)]
        + [jax.ShapeDtypeStruct(dims, F32) for dims in tiny],
        compiler_params=pltpu.CompilerParams(vmem_limit_bytes=VMEM_LIMIT),
        name="write",
    )(*grads, small)
    block_out, grad_in, g_gate, g_value, g_out, g_bc, g_norm, g_step, g_cv, g_cb, g_dt, g_log, g_skip, g_gain = outs
    return (
        block_out[None], grad_in[None], g_norm[0], g_gate, g_value, g_bc, g_step.T, g_cv, g_cb, g_dt[0], g_log[0],
        g_skip[0], g_gain[0], g_out,
    )


def solution(mesh):
    return jax.shard_map(
        on_device,
        mesh=mesh,
        in_specs=(
            P(DP_AXIS, SEQ_AXIS, None),
            P(DP_AXIS, SEQ_AXIS),
            P(),
            P(None, HEAD_AXIS),
            P(None, HEAD_AXIS),
            P(),
            P(None, HEAD_AXIS),
            P(None, HEAD_AXIS),
            P(),
            P(HEAD_AXIS),
            P(HEAD_AXIS),
            P(HEAD_AXIS),
            P(HEAD_AXIS),
            P(HEAD_AXIS, None),
            P(DP_AXIS, SEQ_AXIS, HEAD_AXIS),
        ),
        out_specs=(
            P(DP_AXIS, SEQ_AXIS, HEAD_AXIS),
            P(DP_AXIS, SEQ_AXIS, None),
            P(),
            P(None, HEAD_AXIS),
            P(None, HEAD_AXIS),
            P(),
            P(None, HEAD_AXIS),
            P(None, HEAD_AXIS),
            P(),
            P(HEAD_AXIS),
            P(HEAD_AXIS),
            P(HEAD_AXIS),
            P(HEAD_AXIS),
            P(HEAD_AXIS, None),
        ),
        check_vma=False,
    )
```

```python
import functools
import types

import jax
import jax.numpy as jnp
from jax import lax
from jax.experimental import pallas as pl
from jax.experimental.pallas import tpu as pltpu
from jax.sharding import PartitionSpec as P

BLOCK = 256
EDGE = 8
TAIL = 16
EPS = 1e-05
NEG = -1e30
F32 = jnp.float32
BF16 = jnp.bfloat16
NN = (((1,), (0,)), ((), ()))
NT = (((1,), (1,)), ((), ()))
TN = (((0,), (0,)), ((), ()))
MESH = pl.DeviceIdType.MESH
CUM, AUX, DYY, STEP, TO_END, INTO, RMS = 8, 16, 24, 32, 40, 48, 56
LAG = 4
HEAD_AXIS, SEQ_AXIS, DP_AXIS = "head", "seq", "dp"
COT, HALO, ENDS, NORM, BACK, SUM, OUT, PART, GRAD, EDGES, BC, BCG, PACK1 = (
    "cot", "halo", "ends", "norm", "back", "sum", "out", "part", "grad", "edge", "bc", "bcg", "pack1"
)
WO, WG, WV, WQ, WP = "wo", "wg", "wv", "wq", "wp"
PIECES = {WO: 4, WG: 4, WV: 4, WQ: 1, WP: 1}
VMEM_LIMIT = 63 * 1024 * 1024


def dot(a, b, dims=NN):
    return lax.dot_general(a, b, dims, preferred_element_type=F32)


def halves(v):
    hi = v.astype(BF16)
    return hi, (v - hi.astype(F32)).astype(BF16)


def dot_left(v, m, dims=NN):
    hi, lo = halves(v)
    return dot(hi, m, dims) + dot(lo, m, dims)


def dot_right(m, v, dims=NN):
    hi, lo = halves(v)
    return dot(m, hi, dims) + dot(m, lo, dims)


def dot3(a, b, dims=NN):
    (ah, al), (bh, bl) = halves(a), halves(b)
    return dot(ah, bh, dims) + (dot(al, bh, dims) + dot(ah, bl, dims))


def score_pair(c, b, first):
    hi, lo = halves(c)
    cc, bb = jnp.concatenate([hi, lo], axis=1), jnp.concatenate([b, b], axis=1)
    return dot(cc, bb, NT) if first else dot(bb, cc, NT)


def sigmoid(v):
    return 0.5 * jnp.tanh(0.5 * v) + 0.5


def softplus(v):
    return jnp.maximum(v, 0.0) + jnp.log1p(jnp.exp(-jnp.abs(v)))


def iota(shape, axis):
    return lax.broadcasted_iota(jnp.int32, shape, axis)


def in_norm(x, gain):
    r = lax.rsqrt(jnp.mean(x * x, axis=1, keepdims=True) + EPS)
    return (x * r * gain).astype(BF16)


def repeat(n, body):
    def run(i, carry):
        body(i)
        return carry

    lax.fori_loop(0, n, run, 0)


def kernel(r):
    nh, ns = lax.axis_size(HEAD_AXIS), lax.axis_size(SEQ_AXIS)
    head, seq, dp = lax.axis_index(HEAD_AXIS), lax.axis_index(SEQ_AXIS), lax.axis_index(DP_AXIS)
    me = {HEAD_AXIS: head, SEQ_AXIS: seq, DP_AXIS: dp}
    count = {HEAD_AXIS: nh, SEQ_AXIS: ns, DP_AXIS: 2}
    tokens, width = r.x.shape
    inner, heads = r.wg.shape[1], r.ws.shape[0]
    state = r.wbc.shape[1] // 2
    channels = inner + 2 * state
    blocks, part, slab = tokens // BLOCK, width // nh, BLOCK // nh
    inner_all = inner * nh
    n_taps = r.cv.shape[0] - 1
    lanes = 2 * (inner // heads)

    def at(c):
        return pl.ds(pl.multiple_of(c * BLOCK, BLOCK), BLOCK)

    left, upper_half = lax.rem(head, 2), lax.div(head, 2)
    square = [head, 2 * upper_half + 1 - left, 2 * (1 - upper_half) + left, nh - 1 - head]

    def other(axis, o):
        if axis == HEAD_AXIS:
            return square[abs(o)]
        return lax.rem(me[axis] + o + count[axis], count[axis])

    def link(name, index, axis, o, src, dst):
        return pltpu.make_async_remote_copy(
            src_ref=src,
            dst_ref=dst,
            send_sem=getattr(r, name + "_s").at[index],
            recv_sem=getattr(r, name + "_r").at[index],
            device_id={axis: other(axis, o)},
            device_id_type=MESH,
        )

    def sent(name, index, axis, o, src):
        link(name, index, axis, o, src, src).wait_send()

    def came(name, index, axis, o, dst):
        link(name, index, axis, o, dst, dst).wait_recv()

    def gather_1(name, base, view):
        for o in (1, 2):
            link(name, base + o - 1, HEAD_AXIS, o, view(head), view(head)).start()

    def gather_2(name, base, view, half):
        for o in (1, 2):
            came(name, base + o - 1, HEAD_AXIS, o, view(square[o]))
            piece = half(square[o], o - 1)
            link(name, base + 1 + o, HEAD_AXIS, 3 - o, piece, piece).start()

    def gather_3(name, base, view, half):
        for o in (1, 2):
            came(name, base + 1 + o, HEAD_AXIS, 3 - o, half(square[3], o - 1))
            sent(name, base + o - 1, HEAD_AXIS, o, view(head))
            sent(name, base + 1 + o, HEAD_AXIS, 3 - o, half(square[o], o - 1))

    def scatter_1(name, base, block, inbox):
        for o in (1, 2):
            link(name, base + 2 * o - 2, HEAD_AXIS, o, block(square[o], o - 1), inbox.at[base + 2 * o - 2]).start()
            link(name, base + 2 * o - 1, HEAD_AXIS, o, block(square[3], o - 1), inbox.at[base + 2 * o - 1]).start()

    def scatter_2(name, base, block, inbox):
        for o in (1, 2):
            index = base + 2 * o - 1
            came(name, index, HEAD_AXIS, o, inbox.at[index])
            mine = block(square[3 - o], o - 1)
            mine[...] = (mine[...].astype(F32) + inbox[index].astype(F32)).astype(BF16)
            link(name, base + 3 + o, HEAD_AXIS, 3 - o, mine, inbox.at[base + 3 + o]).start()

    def scatter_3(name, base, block, inbox):
        totals = []
        for o in (1, 2):
            total = block(head, o - 1)[...].astype(F32)
            for index, by in ((base + 2 * o - 2, o), (base + 3 + o, 3 - o)):
                came(name, index, HEAD_AXIS, by, inbox.at[index])
                total = total + inbox[index].astype(F32)
            totals.append(total)
        return totals

    def scatter_sent(name, base, block):
        for o in (1, 2):
            sent(name, base + 2 * o - 2, HEAD_AXIS, o, block(square[o], o - 1))
            sent(name, base + 2 * o - 1, HEAD_AXIS, o, block(square[3], o - 1))
            sent(name, base + 3 + o, HEAD_AXIS, 3 - o, block(square[3 - o], o - 1))

    own = pltpu.make_async_copy(r.cot, r.cot_all.at[head], r.load.at[0])
    own.start()
    row, col = iota((BLOCK, BLOCK), 0), iota((BLOCK, BLOCK), 1)
    r.upper[...] = (row <= col).astype(BF16)
    r.eye[...] = (row == col).astype(BF16)
    dim = inner // heads
    r.spread[...] = (iota((heads, inner), 1) // dim == iota((heads, inner), 0)).astype(BF16)
    r.collect[...] = (iota((inner, heads), 0) // dim == iota((inner, heads), 1)).astype(BF16)
    for sel, lane in ((r.sel_step, STEP), (r.sel_end, TO_END), (r.sel_into, INTO)):
        sel[...] = (iota((128, inner), 1) // dim + lane == iota((128, inner), 0)).astype(BF16)
    r.tok[...] = jnp.zeros_like(r.tok)
    r.doc_out[...] = jnp.broadcast_to(r.docs[0:1, tokens - 1 : tokens].astype(F32), r.doc_out.shape)
    barrier = pltpu.get_barrier_semaphore()
    for axis in (HEAD_AXIS, SEQ_AXIS, DP_AXIS):
        for o in range(1, count[axis]):
            pl.semaphore_signal(barrier, inc=1, device_id={axis: other(axis, o)}, device_id_type=MESH)
    pl.semaphore_wait(barrier, nh + ns + 2 - 3)
    own.wait()

    def cot_of(h):
        return r.cot_all.at[h]

    def cot_half(h, i):
        return r.cot_all.at[h, pl.ds(i * (tokens // 2), tokens // 2)]

    gather_1(COT, 0, cot_of)
    x_tail = r.x.at[pl.ds(tokens - TAIL, TAIL)]
    link(HALO, 0, SEQ_AXIS, 1, x_tail, r.halo_x).start()
    link(HALO, 1, SEQ_AXIS, 1, r.doc_out, r.doc_in).start()

    taps = jnp.concatenate([r.cv[...], r.cb[...]], axis=1)
    rate = -jnp.exp(r.alog[...])
    skip = dot_left(r.dskip[...], r.spread[...])
    gain, out_gain = r.gain[...], r.og[...]

    def conv_pre(window, taps):
        pre = taps[n_taps : n_taps + 1, :] + taps[0:1, :] * window[EDGE:]
        for k in range(1, n_taps):
            pre = pre + taps[k : k + 1, :] * window[EDGE - k : EDGE - k + BLOCK]
        return pre

    def doc_row(c):
        return r.docs[0:1, at(c)].astype(F32)

    def expand(v):
        return dot_left(v, r.spread[...])

    def expand_tok(rows, sel, cols=slice(None)):
        return dot_left(r.tok[rows, :], sel[:, cols])

    def project(c):
        rows = at(c)
        normed = in_norm(r.x[rows, :].astype(F32), gain)
        r.normed[rows, :] = normed
        inside = pl.ds(pl.multiple_of(c * BLOCK + EDGE, EDGE), BLOCK)
        r.cin[inside, :inner] = dot(normed, r.wv[...])
        r.cin[inside, inner:] = dot(normed, r.wbc[...])
        r.tok[rows, 0:heads] = dot(normed, r.ws[...], NT) + r.dtb[...]

    repeat(blocks, project)

    came(HALO, 0, SEQ_AXIS, -1, r.halo_x)
    came(HALO, 1, SEQ_AXIS, -1, r.doc_in)
    opened = jnp.where(seq == 0, 0.0, 1.0)
    edge = in_norm(r.halo_x[...].astype(F32), gain)
    r.cin[0:EDGE, :inner] = dot(edge, r.wv[...])[TAIL - EDGE :] * opened
    r.cin[0:EDGE, inner:] = dot(edge, r.wbc[...])[TAIL - EDGE :] * opened
    r.doc_prev[...] = jnp.where(seq == 0, -1.0, r.doc_in[...])

    r.carry[...] = jnp.ones_like(r.carry)

    def steps(c):
        rows = at(c)
        around = pl.ds(pl.multiple_of(c * BLOCK, BLOCK), BLOCK + EDGE)
        pre = conv_pre(r.cin[around, inner:], taps[:, inner:])
        u = pre * sigmoid(pre)
        r.b[rows, :] = u[:, :state].astype(BF16)
        r.c[rows, :] = u[:, state:]
        docs = doc_row(c)
        prev = r.doc_prev[0:1, 0:1]
        before = jnp.concatenate([prev, docs[:, : BLOCK - 1]], axis=1)
        ends = docs[:, BLOCK - 1 :]
        marks = [docs, (docs == prev).astype(F32), (docs == before).astype(F32), (docs == ends).astype(F32)]
        marks = jnp.concatenate(marks + [jnp.zeros((4, BLOCK), F32)], axis=0).astype(BF16)
        aux = dot(r.eye[...], marks, NT)
        r.tok[rows, AUX : AUX + 8] = aux
        step = softplus(r.tok[rows, 0:heads])
        la = rate * step
        la_hi, la_lo = halves(la)
        cum = dot(r.upper[...], la_hi, TN) + dot(r.upper[...], la_lo, TN)
        r.cumt[:, at(c)] = dot(la_hi, r.upper[...], TN) + dot(la_lo, r.upper[...], TN)
        total = cum[BLOCK - 1 :, :]
        r.tok[rows, CUM : CUM + heads] = cum
        r.tok[rows, STEP : STEP + heads] = step
        r.tok[rows, TO_END : TO_END + heads] = jnp.exp(total - cum) * aux[:, 3:4]
        r.tok[rows, INTO : INTO + heads] = jnp.exp(cum) * aux[:, 1:2]
        kept = expand(jnp.exp(total) * (ends == prev).astype(F32))
        r.kept[c] = kept
        r.carry[...] = r.carry[...] * kept
        r.doc_prev[...] = jnp.broadcast_to(ends, r.doc_prev.shape)

    repeat(blocks, steps)

    pairs = heads // 2
    for pair in range(pairs):
        r.carry_part[pair] = r.carry[:, pair * lanes : (pair + 1) * lanes]
    r.own[...] = jnp.zeros_like(r.own)

    def relay(turn):
        pair = turn - 2 * seq

        @pl.when(jnp.logical_and(pair >= 0, pair < pairs))
        def _():
            @pl.when(seq > 0)
            def _():
                came(ENDS, pair, SEQ_AXIS, -1, r.end_in.at[pair])

            into = jnp.where(seq > 0, r.end_in[pair], 0.0)
            r.end_out[pair] = r.carry_part[pair] * into + r.own[pair]
            r.own[pair] = into

            @pl.when(seq < ns - 1)
            def _():
                link(ENDS, pair, SEQ_AXIS, 1, r.end_out.at[pair], r.end_in.at[pair]).start()

    for pair in range(pairs):
        cols = slice(pair * lanes, (pair + 1) * lanes)

        def own_states(c, pair=pair, cols=cols):
            rows = at(c)
            around = pl.ds(pl.multiple_of(c * BLOCK, BLOCK), BLOCK + EDGE)
            pre = conv_pre(r.cin[around, cols], taps[:, cols])
            xh = pre * sigmoid(pre)
            xs = xh * expand_tok(rows, r.sel_step, cols)
            r.xs[rows, cols] = xs.astype(BF16)
            r.y[rows, cols] = skip[:, cols] * xh
            inc = dot(r.b[rows, :], (xs * expand_tok(rows, r.sel_end, cols)).astype(BF16), TN)
            r.inc[c, :, cols] = inc
            r.own[pair] = r.kept[c, :, cols] * r.own[pair] + inc

        repeat(blocks, own_states)
        relay(pair)

    gather_2(COT, 0, cot_of, cot_half)

    def relay_back(turn):
        distance = ns - 1 - seq
        pair = turn - 2 * distance

        @pl.when(jnp.logical_and(distance > 0, jnp.logical_and(pair >= 0, pair < pairs)))
        def _():
            came(BACK, pair, SEQ_AXIS, 1, r.back_in.at[pair])
            into = r.back_in[pair].astype(F32)
            r.back_out[pair] = (r.carry_part[pair] * into + r.own[pair]).astype(BF16)
            r.own[pair] = into

            @pl.when(seq > 0)
            def _():
                link(BACK, pair, SEQ_AXIS, -1, r.back_out.at[pair], r.back_in.at[pair]).start()

    first = iota((BLOCK, lanes), 1) < lanes // 2

    def split(pair):
        zero = jnp.zeros_like(pair)
        return jnp.where(first, pair, zero), jnp.where(first, zero, pair)

    def intra(c):
        rows = at(c)
        cum, cumt = r.tok[rows, CUM : CUM + heads], r.cumt[:, at(c)]
        mask = jnp.where((row >= col) & (r.tok[rows, AUX : AUX + 1] == doc_row(c)), 0.0, NEG)
        scores = score_pair(r.c[rows, :], r.b[rows, :], True)
        for pair in range(heads // 2):
            cols = slice(pair * lanes, (pair + 1) * lanes)
            mixed = []
            for h in (2 * pair, 2 * pair + 1):
                decay = jnp.exp(cum[:, h : h + 1] - cumt[h : h + 1, :] + mask)
                mixed.append((scores * decay).astype(BF16))
            two = jnp.concatenate(split(r.xs[rows, cols]), axis=0)
            r.y[rows, cols] += dot(jnp.concatenate(mixed, axis=1), two)
        r.z[rows, :] = dot(r.normed[rows, :], r.wg[...])
        relay(pairs + c)

    repeat(blocks, intra)

    if 2 * (ns - 1) > blocks:
        repeat(2 * (ns - 1) - blocks, lambda i: relay(pairs + blocks + i))
    for pair in range(pairs):
        r.end[:, pair * lanes : (pair + 1) * lanes] = r.own[pair]
    gather_3(COT, 0, cot_of, cot_half)

    def dgn_of(rows):
        total = dot(r.cot_all[0, rows, :], r.wo[:, :part], NT)
        for k in range(1, nh):
            total = total + dot(r.cot_all[k, rows, :], r.wo[:, k * part : (k + 1) * part], NT)
        return total

    ones = jnp.ones((8, inner), BF16)

    def sums(c):
        rows = at(c)
        si = r.end[...]
        r.end[...] = r.kept[c] * si + r.inc[c]
        r.inc[c] = si
        into = expand_tok(rows, r.sel_into)
        y = r.y[rows, :] + into * dot3(r.c[rows, :], si)
        r.y[rows, :] = y
        z = r.z[rows, :]
        g = y * (z * sigmoid(z))
        squares = dot_right(ones, g * g, NT)
        products = dot_right(ones, dgn_of(rows) * out_gain * g, NT)
        r.sum_out[c] = jnp.concatenate([squares[0:1], products[0:1], jnp.zeros((6, BLOCK), F32)], axis=0)
        for o in range(1, nh):
            index = c * (nh - 1) + o - 1
            link(SUM, index, HEAD_AXIS, o, r.sum_out.at[c], r.sum_in.at[index]).start()
        r.parts[c, :, :width] = dot((g * out_gain).astype(BF16), r.wo[...]).astype(BF16)
        scatter_1(OUT, 6 * c, out_block(c), r.out_in)

    def out_block(c):
        half = BLOCK // 2
        return lambda h, i: r.parts.at[c, pl.ds(i * half, half), pl.ds(pl.multiple_of(h * part, part), part)]

    repeat(blocks, sums)
    r.inc[blocks] = r.end[...]

    r.end[...] = jnp.zeros_like(r.end)
    r.prod[...] = jnp.ones_like(r.prod)
    r.pack[...] = jnp.zeros_like(r.pack)
    r.g_gain[...] = jnp.zeros_like(r.g_gain)

    def gate(c):
        rows = at(c)
        scatter_2(OUT, 6 * c, out_block(c), r.out_in)
        total = r.sum_out[c]
        for o in range(1, nh):
            index = c * (nh - 1) + o - 1
            came(SUM, index, HEAD_AXIS, -o, r.sum_in.at[index])
            total = total + r.sum_in[index]
        both = dot_right(r.eye[...], total, NT)
        y, z = r.y[rows, :], r.z[rows, :]
        dgn = dgn_of(rows)
        sig = sigmoid(z)
        act = z * sig
        g = y * act
        rms = lax.rsqrt(both[:, 0:1] / inner_all + EPS)
        r.tok[rows, RMS : RMS + 1] = rms
        gr = g * rms
        r.xs[rows, :] = (gr * out_gain).astype(BF16)
        r.g_gain[...] += jnp.sum(dgn * gr, axis=0, keepdims=True)
        dg = rms * (dgn * out_gain) - g * (rms * rms * rms * both[:, 1:2] / inner_all)
        dy = dg * act
        dyb = dy.astype(BF16)
        r.dy[rows, :] = dyb
        r.tok[rows, DYY : DYY + heads] = dot_left(dyb.astype(F32) * y, r.collect[...])
        r.dz[rows, :] = (dg * y * (sig * (1.0 + z * (1.0 - sig)))).astype(BF16)
        into = expand_tok(rows, r.sel_into)
        r.end[...] += r.prod[...] * dot(r.c[rows, :].astype(BF16), (dy * into).astype(BF16), TN)
        r.prod[...] = r.prod[...] * r.kept[c]

    repeat(blocks, gate)

    for pair in range(pairs):
        r.own[pair] = r.end[:, pair * lanes : (pair + 1) * lanes]

    @pl.when(seq == ns - 1)
    def _():
        for pair in range(pairs):
            r.back_out[pair] = r.own[pair].astype(BF16)
            link(BACK, pair, SEQ_AXIS, -1, r.back_out.at[pair], r.back_in.at[pair]).start()
        r.own[...] = jnp.zeros_like(r.own)

    r.gw_out[...] = jnp.zeros_like(r.gw_out)
    r.gw_gate[...] = jnp.zeros_like(r.gw_gate)

    def weight_grads(c):
        rows = at(c)
        gn = r.xs[rows, :]
        for k in range(nh):
            r.gw_out[:, k * part : (k + 1) * part] += dot(gn, r.cot_all[k, rows, :], TN)
        r.gw_gate[...] += dot(r.normed[rows, :], r.dz[rows, :], TN)
        relay_back(c)

    repeat(blocks, weight_grads)

    def ref(name, kind):
        return getattr(r, name + kind)

    def half_of(name, source, core):
        if name in (WO, WQ):
            half = source.shape[1] // 2
            return source.at[:, pl.ds(pl.multiple_of(core * half, half), half)]
        half = source.shape[0] // 2
        return source.at[pl.ds(pl.multiple_of(core * half, half), half)]

    near = seq < ns // 2
    depth, last = jnp.where(near, seq, ns - 1 - seq), ns // 2 - 1
    inward = jnp.where(near, 1, -1)

    def piece_of(name, half, j):
        rows = half.shape[0] // PIECES[name]
        return half.at[pl.ds(j * rows, rows)]

    def result(name, core, j):
        return piece_of(name, half_of(name, ref(name, "_sum"), core), j)

    def total_a(name, source):
        return link(name + "a", 0, DP_AXIS, 1, half_of(name, source, 1 - dp), ref(name, "_pair"))

    def total_b(name, source):
        total_a(name, source).wait_send()
        came(name + "a", 0, DP_AXIS, 1, ref(name, "_pair"))
        mine = ref(name, "_mine")
        mine[...] = (half_of(name, source, dp)[...] + ref(name, "_pair")[...]).astype(mine.dtype)

        @pl.when(depth == 0)
        def _():
            for j in range(PIECES[name]):
                link(name + "b", j, SEQ_AXIS, inward, piece_of(name, mine, j), ref(name, "_in").at[j]).start()

    def total_c(name):
        @pl.when(depth > 0)
        def _():
            for j in range(PIECES[name]):
                came(name + "b", j, SEQ_AXIS, -inward, ref(name, "_in").at[j])
                mine = piece_of(name, ref(name, "_mine"), j)
                mine[...] = (mine[...].astype(F32) + ref(name, "_in")[j].astype(F32)).astype(mine.dtype)

                @pl.when(depth < last)
                def _():
                    link(name + "b", j, SEQ_AXIS, inward, mine, ref(name, "_in").at[j]).start()

                @pl.when(depth == last)
                def _():
                    link(name + "c", j, SEQ_AXIS, inward, mine, result(name, dp, j)).start()

    def total_d(name):
        for j in range(PIECES[name]):
            total = result(name, dp, j)

            @pl.when(depth == last)
            def _():
                came(name + "c", j, SEQ_AXIS, inward, total)
                mine = piece_of(name, ref(name, "_mine"), j)
                total[...] = (mine[...].astype(F32) + total[...].astype(F32)).astype(mine.dtype)

            @pl.when(depth < last)
            def _():
                came(name + "f", j, SEQ_AXIS, inward, total)

            @pl.when(depth > 0)
            def _():
                link(name + "f", j, SEQ_AXIS, -inward, total, total).start()

            link(name + "d", j, DP_AXIS, 1, total, total).start()

    def total_e(name):
        for j in range(PIECES[name]):
            total, mine = result(name, dp, j), piece_of(name, ref(name, "_mine"), j)
            came(name + "d", j, DP_AXIS, 1, result(name, 1 - dp, j))
            sent(name + "d", j, DP_AXIS, 1, total)

            @pl.when(depth < last)
            def _():
                sent(name + "b", j, SEQ_AXIS, inward, mine)

            @pl.when(depth == last)
            def _():
                sent(name + "c", j, SEQ_AXIS, inward, mine)

            @pl.when(depth > 0)
            def _():
                sent(name + "f", j, SEQ_AXIS, -inward, total)

    total_a(WO, r.gw_out).start()
    total_a(WG, r.gw_gate).start()

    if 2 * (ns - 1) + pairs > blocks:
        repeat(2 * (ns - 1) + pairs - blocks, lambda i: relay_back(blocks + i))
    for pair in range(pairs):
        r.end[:, pair * lanes : (pair + 1) * lanes] = r.own[pair]
    r.g_dt[...] = jnp.zeros_like(r.g_dt)
    r.g_log[...] = jnp.zeros_like(r.g_log)
    r.g_skip[...] = jnp.zeros_like(r.g_skip)
    r.g_conv[...] = jnp.zeros_like(r.g_conv)
    r.gw_bc[...] = jnp.zeros_like(r.gw_bc)
    r.g_norm[...] = jnp.zeros_like(r.g_norm)

    def back(c):
        rows = at(c)
        around = pl.ds(pl.multiple_of(c * BLOCK, BLOCK), BLOCK + EDGE)
        inside = pl.ds(pl.multiple_of(c * BLOCK + EDGE, EDGE), BLOCK)
        b_mat, c_full = r.b[rows, :], r.c[rows, :]
        c_mat = c_full.astype(BF16)
        v = r.tok[rows, 0:heads]
        step = r.tok[rows, STEP : STEP + heads]
        cum, cumt, aux = r.tok[rows, CUM : CUM + heads], r.cumt[:, at(c)], r.tok[rows, AUX : AUX + 8]
        mask = jnp.where((row <= col) & (aux[:, 0:1] == doc_row(c)), 0.0, NEG)
        scores = score_pair(c_full, b_mat, False)
        d_scores = jnp.zeros((BLOCK, BLOCK), F32)
        d_b = jnp.zeros((BLOCK, state), F32)
        d_c = jnp.zeros((BLOCK, state), F32)
        d_step_own = jnp.zeros((BLOCK, heads), F32)
        d_cum = r.tok[rows, DYY : DYY + heads]
        through = jnp.zeros((1, heads), F32)

        def conv_grad(d_u, window, pre, sig, cols):
            d_pre = d_u * (sig * (1.0 + pre * (1.0 - sig)))
            for k in range(n_taps):
                shifted = window[EDGE - k : EDGE - k + BLOCK]
                r.g_conv[k : k + 1, cols] += jnp.sum(d_pre * shifted, axis=0, keepdims=True)
            r.g_conv[n_taps : n_taps + 1, cols] += jnp.sum(d_pre, axis=0, keepdims=True)
            r.cin[inside, cols] = d_pre

        for pair in range(heads // 2):
            cols = slice(pair * lanes, (pair + 1) * lanes)
            window = r.cin[around, cols]
            pre = conv_pre(window, taps[:, cols])
            sig = sigmoid(pre)
            xh = pre * sig
            step_e, to_end_e, into_e = (expand_tok(rows, sel, cols) for sel in (r.sel_step, r.sel_end, r.sel_into))
            xs = xh * step_e
            xsb = xs.astype(BF16)
            dyb = r.dy[rows, cols]
            dy = dyb.astype(F32)
            adj = r.end[:, cols]
            dye = dy * into_e
            d_c = d_c + dot3(dye, r.inc[c, :, cols], NT)
            d_b = d_b + dot3(xs * to_end_e, adj, NT)
            d_xs_inter = to_end_e * dot(b_mat, adj.astype(BF16))
            two = split(dyb)
            mixed = []
            for i, h in enumerate((2 * pair, 2 * pair + 1)):
                decay = jnp.exp(cumt[h : h + 1, :] - cum[:, h : h + 1] + mask)
                mixed.append((scores * decay).astype(BF16))
                d_scores = d_scores + dot(xsb, two[i], NT) * decay
            d_xs_intra = dot(jnp.concatenate(mixed, axis=1), jnp.concatenate(two, axis=0))
            d_xs = d_xs_intra + d_xs_inter
            collect = r.collect[cols, :]
            d_step_own = d_step_own + dot_left(xh * d_xs, collect)
            lost = skip[:, cols] * (dy * xh) + (xsb.astype(F32) * d_xs_intra + xs * d_xs_inter)
            d_cum = d_cum - dot_left(lost, collect)
            ended = jnp.sum(adj * r.inc[c + 1, :, cols], axis=0, keepdims=True)
            through = through + dot_left(ended, collect)
            r.g_skip[:, cols] += jnp.sum(dy * xh, axis=0, keepdims=True)
            r.end[:, cols] = r.kept[c, :, cols] * adj + dot(c_mat, dye.astype(BF16), TN)
            conv_grad(skip[:, cols] * dy + step_e * d_xs, window, pre, sig, cols)
        d_sb = d_scores.astype(BF16)
        d_b = d_b + dot(d_sb, c_mat)
        d_c = d_c + dot(d_sb, b_mat, TN)
        cols = slice(inner, channels)
        window = r.cin[around, cols]
        pre = conv_pre(window, taps[:, cols])
        conv_grad(jnp.concatenate([d_b, d_c], axis=1), window, pre, sigmoid(pre), cols)
        d_la = (dot_right(r.upper[...], d_cum) + through) * aux[:, 2:3]
        r.g_log[...] += jnp.sum(rate * step * d_la, axis=0, keepdims=True)
        d_v = (d_step_own + rate * d_la) * sigmoid(v)
        r.g_dt[...] += jnp.sum(d_v, axis=0, keepdims=True)
        r.dstep[rows, :] = d_v.astype(BF16)

    def project_back(c):
        rows = at(c)
        window = r.cin[pl.ds(pl.multiple_of(c * BLOCK + EDGE, EDGE), BLOCK + EDGE), :]
        d_in = taps[0:1, :] * window[:BLOCK]
        for k in range(1, n_taps):
            d_in = d_in + taps[k : k + 1, :] * window[k : k + BLOCK]
        d_inb = d_in.astype(BF16)
        d_val = d_inb[:, :inner]
        dstep = r.dstep[rows, :]
        normed = r.normed[rows, :]
        grads = dot(normed, d_inb, TN)
        r.gw_value[...] += grads[:, :inner]
        r.gw_bc[...] += grads[:, inner:]
        r.pack[0:heads, :] += dot(dstep, normed, TN)
        d_part = dot(r.dz[rows, :], r.wg[...], NT) + dot(d_val, r.wv[...], NT) + dot(dstep, r.ws[...])
        scatter_sent(OUT, 6 * c, out_block(c))
        r.parts[c, :, :width] = d_part.astype(BF16)
        r.parts[c, :, width:] = d_inb[:, inner:]
        scatter_1(PART, 6 * c, part_block(c), r.part_in)

    def part_block(c):
        half = slab // 2
        return lambda h, i: r.parts.at[c, pl.ds(pl.multiple_of(h * slab + i * half, half), half)]

    def combine(c):
        scatter_2(PART, 6 * c, part_block(c), r.part_in)

    def slab_of(c):
        return lambda h: r.normed.at[pl.ds(pl.multiple_of(c * BLOCK + h * slab, slab), slab)]

    def slab_half(c):
        half = slab // 2
        return lambda h, i: r.normed.at[pl.ds(pl.multiple_of(c * BLOCK + h * slab + i * half, half), half)]

    def forward(c):
        gather_2(GRAD, 4 * c, slab_of(c), slab_half(c))

    def own_slab(c):
        return pl.ds(pl.multiple_of(c * BLOCK + head * slab, slab), slab)

    def finish(c):
        rows = own_slab(c)
        total = jnp.concatenate(scatter_3(PART, 6 * c, part_block(c), r.part_in), axis=0)
        x = r.x[rows, :].astype(F32)
        norm = lax.rsqrt(jnp.mean(x * x, axis=1, keepdims=True) + EPS)
        xr = x * norm
        d_bc = total[:, width:].astype(BF16)
        d_normed = total[:, :width] + dot(d_bc, r.wbc[...], NT)
        r.g_norm[...] += jnp.sum(d_normed * xr, axis=0, keepdims=True)
        q = d_normed * gain
        d_x = norm * q - xr * (norm * norm * jnp.mean(q * x, axis=1, keepdims=True))
        cot = jnp.concatenate([r.cot_all[k, rows, :] for k in range(nh)], axis=1)
        r.normed[rows, :] = (d_x + cot.astype(F32)).astype(BF16)
        gather_1(GRAD, 4 * c, slab_of(c))

    def add_residual(c):
        cols = pl.ds(pl.multiple_of(head * part, part), part)
        half = BLOCK // 2
        for i, total in enumerate(scatter_3(OUT, 6 * c, out_block(c), r.out_in)):
            rows = pl.ds(pl.multiple_of(c * BLOCK + i * half, half), half)
            scaled = r.tok[rows, RMS : RMS + 1] * total
            r.block_out[rows, :] = (scaled + r.x[rows, cols].astype(F32)).astype(BF16)

    def reverse(t):
        c = blocks - 1 - t
        back(c)

        @pl.when(t == 0)
        def _():
            total_b(WO, r.gw_out)
            total_b(WG, r.gw_gate)
            r.gw_value[...] = jnp.zeros_like(r.gw_value)

        @pl.when(t >= 1)
        def _():
            add_residual(c)
            project_back(c)

        @pl.when(t >= 2)
        def _():
            combine(c + 1)

        @pl.when(t == 2)
        def _():
            total_c(WO)

        @pl.when(t >= LAG)
        def _():
            finish(c + LAG - 1)

        @pl.when(t == 4)
        def _():
            total_c(WG)
            total_d(WO)

    repeat(blocks, reverse)

    first_rows = r.cin.at[pl.ds(EDGE, EDGE)]
    last_rows = r.cin.at[pl.ds(EDGE + tokens, EDGE)]
    link(EDGES, 0, SEQ_AXIS, -1, first_rows, last_rows).start()
    order = [*range(blocks - 2, -1, -1), blocks - 1]
    waiting = order[max(blocks - LAG, 0) :]
    add_residual(blocks - 1)
    combine(0)
    came(EDGES, 0, SEQ_AXIS, 1, last_rows)

    @pl.when(seq == ns - 1)
    def _():
        r.cin[EDGE + tokens :, :] = jnp.zeros((EDGE, channels), F32)

    project_back(blocks - 1)
    total_a(WV, r.gw_value).start()

    quarter = width // nh

    def quarter_of(whole, h):
        return whole.at[pl.ds(pl.multiple_of(h * quarter, quarter), quarter)]

    r.pack[9 : 9 + n_taps + 1, :channels] = r.g_conv[: n_taps + 1, :]
    r.pack[14:15, :inner] = r.g_gain[...]
    r.pack[15:16, 0:heads] = r.g_dt[...]
    r.pack[15:16, 128 : 128 + heads] = r.g_log[...]
    r.pack[15:16, 256 : 256 + heads] = dot_left(r.g_skip[...], r.collect[...])
    r.bc_out[...] = r.gw_bc[...].astype(BF16)
    r.pack_out[...] = r.pack[8:16, :]
    for o in range(1, nh):
        link(PACK1, o - 1, HEAD_AXIS, o, r.pack_out, r.pack1_in.at[o - 1]).start()
        link(BC, o - 1, HEAD_AXIS, o, quarter_of(r.bc_out, square[o]), r.bc_in[o - 1]).start()
    for c in waiting[:-2]:
        finish(c)
    total_b(WV, r.gw_value)
    total_d(WG)
    for o in range(1, nh):
        came(PACK1, o - 1, HEAD_AXIS, -o, r.pack1_in.at[o - 1])
        r.pack[9 : 9 + n_taps + 1, inner:channels] += r.pack1_in[o - 1, 1 : 2 + n_taps, inner:channels]
    total_a(WP, r.pack).start()
    finish(0)
    combine(blocks - 1)
    mine = quarter_of(r.gw_bc, head)[...]
    for o in range(1, nh):
        came(BC, o - 1, HEAD_AXIS, -o, r.bc_in[o - 1])
        mine = mine + r.bc_in[o - 1][...].astype(F32)
    r.gw_q[...] = mine
    total_a(WQ, r.gw_q).start()
    total_c(WV)
    total_b(WP, r.pack)
    total_b(WQ, r.gw_q)
    for c in order[:2]:
        forward(c)
    total_c(WP)
    total_c(WQ)
    finish(blocks - 1)
    for o in range(1, nh):
        link(NORM, o - 1, HEAD_AXIS, o, r.g_norm, r.norm_in.at[o - 1]).start()
    for c in order[2:-2]:
        forward(c)
    total_d(WV)
    total_d(WP)
    total_d(WQ)
    total = r.g_norm[...]
    for o in range(1, nh):
        came(NORM, o - 1, HEAD_AXIS, -o, r.norm_in.at[o - 1])
        total = total + r.norm_in[o - 1]
    r.norm_out[0] = total
    link(NORM, nh - 1, DP_AXIS, 1, r.norm_out.at[0], r.norm_in.at[nh - 1]).start()
    forward(0)
    total_e(WQ)
    mine = quarter_of(r.bc_sum, head)
    mine[...] = r.wq_sum[...].astype(BF16)
    for o in range(1, nh):
        link(BCG, o - 1, HEAD_AXIS, o, mine, mine).start()
    came(NORM, nh - 1, DP_AXIS, 1, r.norm_in.at[nh - 1])
    total = r.norm_out[0] + r.norm_in[nh - 1]
    r.norm_out[1] = total
    for o in range(1, ns):
        link(NORM, nh + o - 1, SEQ_AXIS, o, r.norm_out.at[1], r.norm_in.at[nh + o - 1]).start()
    forward(blocks - 1)
    for name in (WO, WG, WV, WP):
        total_e(name)

    r.norm_all[seq] = total
    for o in range(1, ns):
        came(NORM, nh + o - 1, SEQ_AXIS, -o, r.norm_in.at[nh + o - 1])
        r.norm_all[other(SEQ_AXIS, -o)] = r.norm_in[nh + o - 1]
    total = r.norm_all[0]
    for k in range(1, ns):
        total = total + r.norm_all[k]
    r.norm_sum[...] = total
    for o in range(1, nh):
        came(BCG, o - 1, HEAD_AXIS, -o, quarter_of(r.bc_sum, square[o]))
        sent(BCG, o - 1, HEAD_AXIS, o, mine)
        sent(BC, o - 1, HEAD_AXIS, o, quarter_of(r.bc_out, square[o]))
        sent(PACK1, o - 1, HEAD_AXIS, o, r.pack_out)
        sent(NORM, o - 1, HEAD_AXIS, o, r.g_norm)
    sent(NORM, nh - 1, DP_AXIS, 1, r.norm_out.at[0])
    for o in range(1, ns):
        sent(NORM, nh + o - 1, SEQ_AXIS, o, r.norm_out.at[1])
    sent(HALO, 0, SEQ_AXIS, 1, x_tail)
    sent(HALO, 1, SEQ_AXIS, 1, r.doc_out)
    sent(EDGES, 0, SEQ_AXIS, -1, first_rows)

    @pl.when(seq > 0)
    def _():
        for pair in range(pairs):
            sent(BACK, pair, SEQ_AXIS, -1, r.back_out.at[pair])

    @pl.when(seq < ns - 1)
    def _():
        for pair in range(pairs):
            sent(ENDS, pair, SEQ_AXIS, 1, r.end_out.at[pair])

    def drain(c):
        for o in range(1, nh):
            sent(SUM, c * (nh - 1) + o - 1, HEAD_AXIS, o, r.sum_out.at[c])
        scatter_sent(PART, 6 * c, part_block(c))
        gather_3(GRAD, 4 * c, slab_of(c), slab_half(c))

    repeat(blocks, drain)
    done = pltpu.make_async_copy(r.normed, r.grad_in, r.load.at[0])
    done.start()
    done.wait()


def write_kernel(n, *refs):
    small, norm_sum = refs[n : n + 2]
    for source, target in zip(refs[:n], refs[n + 2 :]):
        target[...] = source[...].astype(target.dtype)
    norm, step, conv_v, conv_b, dt, log, skip, gain = refs[2 * n + 2 :]
    inner, heads, taps = conv_v.shape[1], dt.shape[1], conv_v.shape[0]

    @pl.when(pl.program_id(0) == 0)
    def _():
        norm[...] = norm_sum[...]
        step[...] = small[0:heads, :]
        conv_v[...] = small[9 : 9 + taps, :inner]
        conv_b[...] = small[9 : 9 + taps, inner : inner + conv_b.shape[1]]
        dt[...] = small[15:16, 0:heads]
        log[...] = small[15:16, 128 : 128 + heads]
        skip[...] = small[15:16, 256 : 256 + heads]
        gain[...] = small[14:15, :inner]


def on_device(
    hidden_in, doc_ids, norm_gain, w_gate, w_value, w_bc, w_step, conv_value, conv_bc, dt_bias, a_log, d_skip,
    out_gain, w_out, cotangent,
):
    x, cot = hidden_in[0], cotangent[0]
    tokens, width = x.shape
    inner, heads = w_gate.shape[1], w_step.shape[1]
    bc_width, head_dim = w_bc.shape[1], inner // heads
    state = bc_width // 2
    channels = inner + bc_width
    blocks = tokens // BLOCK
    nh, ns = lax.axis_size(HEAD_AXIS), lax.axis_size(SEQ_AXIS)
    part, slab = width // nh, BLOCK // nh
    n_taps = conv_value.shape[0] - 1
    vmem, hbm = pltpu.VMEM, pl.ANY
    inputs = dict(
        x=x, cot=cot, docs=doc_ids, gain=norm_gain[None], wg=w_gate, wv=w_value, wbc=w_bc,
        ws=w_step.T, wo=w_out, cv=conv_value, cb=conv_bc, dtb=dt_bias[None], alog=a_log[None],
        dskip=d_skip[None], og=out_gain[None],
    )
    outputs = dict(
        block_out=((tokens, part), BF16),
        grad_in=((tokens, width), BF16),
        wg_sum=(w_gate.shape, BF16),
        wv_sum=(w_value.shape, BF16),
        wo_sum=(w_out.shape, BF16),
        bc_sum=(w_bc.shape, BF16),
        wp_sum=((16, width), F32),
        norm_sum=((1, width), F32),
    )
    scratch = dict(
        cot_all=vmem((nh, tokens, part), BF16),
        halo_x=vmem((TAIL, width), BF16),
        doc_out=vmem((8, 128), F32),
        doc_in=vmem((8, 128), F32),
        doc_prev=vmem((8, 128), F32),
        upper=vmem((BLOCK, BLOCK), BF16),
        eye=vmem((BLOCK, BLOCK), BF16),
        spread=vmem((heads, inner), BF16),
        collect=vmem((inner, heads), BF16),
        normed=vmem((tokens, width), BF16),
        z=vmem((tokens, inner), F32),
        cin=vmem((EDGE + tokens + EDGE, channels), F32),
        y=vmem((tokens, inner), F32),
        xs=vmem((tokens, inner), BF16),
        dy=vmem((tokens, inner), BF16),
        b=vmem((tokens, state), BF16),
        c=vmem((tokens, state), F32),
        tok=vmem((tokens, 128), F32),
        cumt=vmem((heads, tokens), F32),
        dstep=vmem((tokens, heads), BF16),
        inc=vmem((blocks + 1, state, inner), F32),
        kept=vmem((blocks, 1, inner), F32),
        end=vmem((state, inner), F32),
        own=vmem((heads // 2, state, 2 * head_dim), F32),
        end_out=vmem((heads // 2, state, 2 * head_dim), F32),
        end_in=vmem((heads // 2, state, 2 * head_dim), F32),
        carry_part=vmem((heads // 2, 1, 2 * head_dim), F32),
        sel_step=vmem((128, inner), BF16),
        sel_end=vmem((128, inner), BF16),
        sel_into=vmem((128, inner), BF16),
        back_out=vmem((heads // 2, state, 2 * head_dim), BF16),
        norm_in=vmem((nh + ns - 1, 1, width), F32),
        norm_out=vmem((2, 1, width), F32),
        norm_all=vmem((ns, 1, width), F32),
        back_in=vmem((heads // 2, state, 2 * head_dim), BF16),
        carry=vmem((1, inner), F32),
        prod=vmem((1, inner), F32),
        sum_out=vmem((blocks, 8, BLOCK), F32),
        sum_in=vmem((blocks * (nh - 1), 8, BLOCK), F32),
        parts=vmem((blocks, BLOCK, width + bc_width), BF16),
        out_in=vmem((blocks * 6, BLOCK // 2, part), BF16),
        part_in=vmem((blocks * 6, slab // 2, width + bc_width), BF16),
        gw_out=vmem(w_out.shape, F32),
        wq_sum=vmem((width // nh, bc_width), F32),
        dz=vmem((tokens, inner), BF16),
        g_gain=vmem((1, inner), F32),
        g_dt=vmem((1, heads), F32),
        g_log=vmem((1, heads), F32),
        g_skip=vmem((1, inner), F32),
        g_conv=vmem((8, channels), F32),
        g_norm=vmem((1, width), F32),
        pack=vmem((16, width), F32),
        pack_out=vmem((8, width), F32),
        pack1_in=vmem((nh - 1, 8, width), F32),
        load=pltpu.SemaphoreType.DMA((1,)),
    )
    for name, (rows, cols), kind in (
        (WO, (inner, width // 2), BF16), (WG, (width // 2, inner), BF16), (WV, (width // 2, inner), BF16),
        (WQ, (width // nh, state), F32), (WP, (8, width), F32),
    ):
        if name != WV:
            scratch[name + "_pair"] = vmem((rows, cols), F32)
            scratch[name + "_mine"] = vmem((rows, cols), kind)
        scratch[name + "_in"] = vmem((PIECES[name], rows // PIECES[name], cols), kind)
    counts = dict(
        cot=4, halo=2, ends=heads // 2, back=heads // 2, norm=nh + ns - 1, sum=blocks * (nh - 1), out=blocks * 6,
        part=blocks * 6, grad=blocks * 4, edge=1, bc=nh - 1, bcg=nh - 1, pack1=nh - 1,
    )
    for name, n in PIECES.items():
        counts |= {name + "a": 1, name + "b": n, name + "c": n, name + "d": n, name + "f": n}
    for name, n in counts.items():
        scratch[name + "_s"] = pltpu.SemaphoreType.DMA((n,))
        scratch[name + "_r"] = pltpu.SemaphoreType.DMA((n,))
    names = [*inputs, *outputs, *scratch]

    def run(*refs):
        r = types.SimpleNamespace(**dict(zip(names, refs)))
        quarter = width // nh
        r.gw_gate = r.gw_value = r.z.at[pl.ds(0, width)]
        r.wv_pair = r.z.at[pl.ds(width, width // 2)]
        r.gw_bc = r.y.at[pl.ds(0, width), pl.ds(0, bc_width)]
        r.gw_q = r.y.at[pl.ds(width, quarter), pl.ds(0, bc_width)]
        r.bc_out = r.xs.at[pl.ds(0, width), pl.ds(0, bc_width)]
        r.wv_mine = r.xs.at[pl.ds(width, width // 2)]
        r.bc_in = [r.dz.at[pl.ds(o * quarter, quarter), pl.ds(0, bc_width)] for o in range(nh - 1)]
        kernel(r)

    block_out, grad_in, g_gate, g_value, g_out, g_bc, small, norm = pl.pallas_call(
        run,
        out_shape=[jax.ShapeDtypeStruct(*o) for o in outputs.values()],
        in_specs=[pl.BlockSpec(memory_space=hbm if name == "cot" else vmem) for name in inputs],
        out_specs=[pl.BlockSpec(memory_space=hbm if name == "grad_in" else vmem) for name in outputs],
        scratch_shapes=list(scratch.values()),
        compiler_params=pltpu.CompilerParams(
            collective_id=0, has_side_effects=True, vmem_limit_bytes=VMEM_LIMIT
        ),
        name="block",
    )(*inputs.values())
    steps = 8
    grads = (block_out, grad_in, g_gate, g_value, g_out, g_bc)
    kinds = (BF16, BF16, F32, F32, F32, F32)
    tiny = ((1, width), (heads, width), (n_taps + 1, inner), (n_taps + 1, bc_width), (1, heads), (1, heads), (1, heads),
            (1, inner))

    def split_rows(a):
        return pl.BlockSpec((a.shape[0] // steps, a.shape[1]), lambda i: (i, 0))

    def whole(dims):
        return pl.BlockSpec(dims, lambda i: (0, 0))

    outs = pl.pallas_call(
        functools.partial(write_kernel, len(grads)),
        grid=(steps,),
        in_specs=[*map(split_rows, grads), whole(small.shape), whole(norm.shape)],
        out_specs=[*map(split_rows, grads), *map(whole, tiny)],
        out_shape=[jax.ShapeDtypeStruct(a.shape, k) for a, k in zip(grads, kinds)]
        + [jax.ShapeDtypeStruct(dims, F32) for dims in tiny],
        compiler_params=pltpu.CompilerParams(vmem_limit_bytes=VMEM_LIMIT),
        name="write",
    )(*grads, small, norm)
    block_out, grad_in, g_gate, g_value, g_out, g_bc, g_norm, g_step, g_cv, g_cb, g_dt, g_log, g_skip, g_gain = outs
    return (
        block_out[None], grad_in[None], g_norm[0], g_gate, g_value, g_bc, g_step.T, g_cv, g_cb, g_dt[0], g_log[0],
        g_skip[0], g_gain[0], g_out,
    )


def solution(mesh):
    return jax.shard_map(
        on_device,
        mesh=mesh,
        in_specs=(
            P(DP_AXIS, SEQ_AXIS, None),
            P(DP_AXIS, SEQ_AXIS),
            P(),
            P(None, HEAD_AXIS),
            P(None, HEAD_AXIS),
            P(),
            P(None, HEAD_AXIS),
            P(None, HEAD_AXIS),
            P(),
            P(HEAD_AXIS),
            P(HEAD_AXIS),
            P(HEAD_AXIS),
            P(HEAD_AXIS),
            P(HEAD_AXIS, None),
            P(DP_AXIS, SEQ_AXIS, HEAD_AXIS),
        ),
        out_specs=(
            P(DP_AXIS, SEQ_AXIS, HEAD_AXIS),
            P(DP_AXIS, SEQ_AXIS, None),
            P(),
            P(None, HEAD_AXIS),
            P(None, HEAD_AXIS),
            P(),
            P(None, HEAD_AXIS),
            P(None, HEAD_AXIS),
            P(),
            P(HEAD_AXIS),
            P(HEAD_AXIS),
            P(HEAD_AXIS),
            P(HEAD_AXIS),
            P(HEAD_AXIS, None),
        ),
        check_vma=False,
    )
```

```python
import functools
import types

import jax
import jax.numpy as jnp
from jax import lax
from jax.experimental import pallas as pl
from jax.experimental.pallas import tpu as pltpu
from jax.sharding import PartitionSpec as P

BLOCK = 256
EDGE = 8
TAIL = 16
EPS = 1e-05
NEG = -1e30
F32 = jnp.float32
BF16 = jnp.bfloat16
NN = (((1,), (0,)), ((), ()))
NT = (((1,), (1,)), ((), ()))
TN = (((0,), (0,)), ((), ()))
MESH = pl.DeviceIdType.MESH
CUM, AUX, DYY, STEP, TO_END, INTO, RMS = 8, 16, 24, 32, 40, 48, 56
LAG = 4
HEAD_AXIS, SEQ_AXIS, DP_AXIS = "head", "seq", "dp"
COT, HALO, ENDS, NORM, BACK, SUM, OUT, PART, GRAD, EDGES, BC, BCG, PACK1 = (
    "cot", "halo", "ends", "norm", "back", "sum", "out", "part", "grad", "edge", "bc", "bcg", "pack1"
)
WO, WG, WV, WQ, WP = "wo", "wg", "wv", "wq", "wp"
PIECES = {WO: 4, WG: 4, WV: 8, WQ: 1, WP: 1}
LOADED = ("x_hbm", "cot", "wg_hbm", "wv_hbm", "wbc_hbm", "wo_hbm")
VMEM_LIMIT = 63 * 1024 * 1024


def dot(a, b, dims=NN):
    return lax.dot_general(a, b, dims, preferred_element_type=F32)


def halves(v):
    hi = v.astype(BF16)
    return hi, (v - hi.astype(F32)).astype(BF16)


def dot_left(v, m, dims=NN):
    hi, lo = halves(v)
    return dot(hi, m, dims) + dot(lo, m, dims)


def dot_right(m, v, dims=NN):
    hi, lo = halves(v)
    return dot(m, hi, dims) + dot(m, lo, dims)


def both(v, axis=1):
    return jnp.concatenate(halves(v), axis=axis)


def dot3(a, b, dims=NN):
    (ah, al), (bh, bl) = halves(a), halves(b)
    return dot(
        jnp.concatenate([ah, al, ah], axis=1), jnp.concatenate([bh, bh, bl], axis=dims[0][1][0]), dims
    )


def score_pair(c, b, first):
    hi, lo = halves(c)
    cc, bb = jnp.concatenate([hi, lo], axis=1), jnp.concatenate([b, b], axis=1)
    return dot(cc, bb, NT) if first else dot(bb, cc, NT)


def sigmoid(v):
    return 0.5 * jnp.tanh(0.5 * v) + 0.5


def softplus(v):
    return jnp.maximum(v, 0.0) + jnp.log1p(jnp.exp(-jnp.abs(v)))


def iota(shape, axis):
    return lax.broadcasted_iota(jnp.int32, shape, axis)


def in_norm(x, gain):
    r = lax.rsqrt(jnp.mean(x * x, axis=1, keepdims=True) + EPS)
    return (x * r * gain).astype(BF16)


def repeat(n, body):
    def run(i, carry):
        body(i)
        return carry

    lax.fori_loop(0, n, run, 0)


def kernel(r):
    nh, ns = lax.axis_size(HEAD_AXIS), lax.axis_size(SEQ_AXIS)
    head, seq, dp = lax.axis_index(HEAD_AXIS), lax.axis_index(SEQ_AXIS), lax.axis_index(DP_AXIS)
    me = {HEAD_AXIS: head, SEQ_AXIS: seq, DP_AXIS: dp}
    count = {HEAD_AXIS: nh, SEQ_AXIS: ns, DP_AXIS: 2}
    tokens, width = r.x.shape
    inner, heads = r.wg.shape[1], r.ws.shape[0]
    state = r.wbc.shape[1] // 2
    channels = inner + 2 * state
    blocks, part, slab = tokens // BLOCK, width // nh, BLOCK // nh
    inner_all = inner * nh
    n_taps = r.cv.shape[0] - 1
    lanes = 2 * (inner // heads)

    def at(c):
        return pl.ds(pl.multiple_of(c * BLOCK, BLOCK), BLOCK)

    left, upper_half = lax.rem(head, 2), lax.div(head, 2)
    square = [head, 2 * upper_half + 1 - left, 2 * (1 - upper_half) + left, nh - 1 - head]

    def other(axis, o):
        if axis == HEAD_AXIS:
            return square[abs(o)]
        return lax.rem(me[axis] + o + count[axis], count[axis])

    def link(name, index, axis, o, src, dst):
        return pltpu.make_async_remote_copy(
            src_ref=src,
            dst_ref=dst,
            send_sem=getattr(r, name + "_s").at[index],
            recv_sem=getattr(r, name + "_r").at[index],
            device_id={axis: other(axis, o)},
            device_id_type=MESH,
        )

    def sent(name, index, axis, o, src):
        link(name, index, axis, o, src, src).wait_send()

    def came(name, index, axis, o, dst):
        link(name, index, axis, o, dst, dst).wait_recv()

    def gather_1(name, base, view):
        for o in (1, 2):
            link(name, base + o - 1, HEAD_AXIS, o, view(head), view(head)).start()

    def gather_2(name, base, view, half):
        for o in (1, 2):
            came(name, base + o - 1, HEAD_AXIS, o, view(square[o]))
            piece = half(square[o], o - 1)
            link(name, base + 1 + o, HEAD_AXIS, 3 - o, piece, piece).start()

    def gather_3(name, base, view, half):
        for o in (1, 2):
            came(name, base + 1 + o, HEAD_AXIS, 3 - o, half(square[3], o - 1))
            sent(name, base + o - 1, HEAD_AXIS, o, view(head))
            sent(name, base + 1 + o, HEAD_AXIS, 3 - o, half(square[o], o - 1))

    def scatter_1(name, base, block, inbox):
        for o in (1, 2):
            link(name, base + 2 * o - 2, HEAD_AXIS, o, block(square[o], o - 1), inbox.at[base + 2 * o - 2]).start()
            link(name, base + 2 * o - 1, HEAD_AXIS, o, block(square[3], o - 1), inbox.at[base + 2 * o - 1]).start()

    def scatter_2(name, base, block, inbox):
        for o in (1, 2):
            index = base + 2 * o - 1
            came(name, index, HEAD_AXIS, o, inbox.at[index])
            mine = block(square[3 - o], o - 1)
            mine[...] = (mine[...].astype(F32) + inbox[index].astype(F32)).astype(BF16)
            link(name, base + 3 + o, HEAD_AXIS, 3 - o, mine, inbox.at[base + 3 + o]).start()

    def scatter_3(name, base, block, inbox):
        totals = []
        for o in (1, 2):
            total = block(head, o - 1)[...].astype(F32)
            for index, by in ((base + 2 * o - 2, o), (base + 3 + o, 3 - o)):
                came(name, index, HEAD_AXIS, by, inbox.at[index])
                total = total + inbox[index].astype(F32)
            totals.append(total)
        return totals

    def scatter_sent(name, base, block):
        for o in (1, 2):
            sent(name, base + 2 * o - 2, HEAD_AXIS, o, block(square[o], o - 1))
            sent(name, base + 2 * o - 1, HEAD_AXIS, o, block(square[3], o - 1))
            sent(name, base + 3 + o, HEAD_AXIS, 3 - o, block(square[3 - o], o - 1))

    def cot_of(h):
        return r.cot_all.at[:, pl.ds(pl.multiple_of(h * part, part), part)]

    def cot_half(h, i):
        return r.cot_all.at[pl.ds(i * (tokens // 2), tokens // 2), pl.ds(pl.multiple_of(h * part, part), part)]

    moves = ((r.x_hbm, r.x), (r.wv_hbm, r.wv), (r.wbc_hbm, r.wbc), (r.cot, cot_of(head)), (r.wg_hbm, r.wg), (r.wo_hbm, r.wo))
    loads = [pltpu.make_async_copy(*move, r.load.at[i]) for i, move in enumerate(moves)]
    for load in loads:
        load.start()
    row, col = iota((BLOCK, BLOCK), 0), iota((BLOCK, BLOCK), 1)
    r.upper[...] = (row <= col).astype(BF16)
    r.eye[...] = (row == col).astype(BF16)
    dim = inner // heads
    r.spread[...] = (iota((heads, inner), 1) // dim == iota((heads, inner), 0)).astype(BF16)
    r.collect[...] = (iota((inner, heads), 0) // dim == iota((inner, heads), 1)).astype(BF16)
    for sel, lane in ((r.sel_step, STEP), (r.sel_end, TO_END), (r.sel_into, INTO)):
        sel[...] = (iota((256, inner), 1) // dim + lane == lax.rem(iota((256, inner), 0), 128)).astype(BF16)
    r.tok[...] = jnp.zeros_like(r.tok)
    r.doc_out[...] = jnp.broadcast_to(r.docs[0:1, tokens - 1 : tokens].astype(F32), r.doc_out.shape)
    barrier = pltpu.get_barrier_semaphore()
    for axis in (HEAD_AXIS, SEQ_AXIS, DP_AXIS):
        for o in range(1, count[axis]):
            pl.semaphore_signal(barrier, inc=1, device_id={axis: other(axis, o)}, device_id_type=MESH)
    pl.semaphore_wait(barrier, nh + ns + 2 - 3)
    for load in loads[:4]:
        load.wait()
    gather_1(COT, 0, cot_of)
    x_tail = r.x.at[pl.ds(tokens - TAIL, TAIL)]
    link(HALO, 0, SEQ_AXIS, 1, x_tail, r.halo_x).start()
    link(HALO, 1, SEQ_AXIS, 1, r.doc_out, r.doc_in).start()

    taps = jnp.concatenate([r.cv[...], r.cb[...]], axis=1)
    rate = -jnp.exp(r.alog[...])
    same = iota((heads, heads), 0) == iota((heads, heads), 1)
    rate_col = jnp.sum(jnp.where(same, rate, 0.0), axis=1, keepdims=True)
    skip = dot_left(r.dskip[...], r.spread[...])
    gain, out_gain = r.gain[...], r.og[...]

    def conv_pre(window, taps):
        pre = taps[n_taps : n_taps + 1, :] + taps[0:1, :] * window[EDGE:]
        for k in range(1, n_taps):
            pre = pre + taps[k : k + 1, :] * window[EDGE - k : EDGE - k + BLOCK]
        return pre

    def doc_row(c):
        return r.docs[0:1, at(c)].astype(F32)

    def expand_tok(marks, sel, cols=slice(None)):
        return dot(marks, sel[:, cols])

    def project(c):
        rows = at(c)
        normed = in_norm(r.x[rows, :].astype(F32), gain)
        r.normed[rows, :] = normed
        inside = pl.ds(pl.multiple_of(c * BLOCK + EDGE, EDGE), BLOCK)
        r.cin[inside, :inner] = dot(normed, r.wv[...])
        r.cin[inside, inner:] = dot(normed, r.wbc[...])
        r.tok[rows, 0:heads] = dot(normed, r.ws[...], NT) + r.dtb[...]

    repeat(blocks, project)

    came(HALO, 0, SEQ_AXIS, -1, r.halo_x)
    came(HALO, 1, SEQ_AXIS, -1, r.doc_in)
    opened = jnp.where(seq == 0, 0.0, 1.0)
    edge = in_norm(r.halo_x[...].astype(F32), gain)
    r.cin[0:EDGE, :inner] = dot(edge, r.wv[...])[TAIL - EDGE :] * opened
    r.cin[0:EDGE, inner:] = dot(edge, r.wbc[...])[TAIL - EDGE :] * opened
    r.doc_prev[...] = jnp.where(seq == 0, -1.0, r.doc_in[...])

    r.carry[...] = jnp.ones_like(r.carry)

    def steps(c):
        rows = at(c)
        around = pl.ds(pl.multiple_of(c * BLOCK, BLOCK), BLOCK + EDGE)
        pre = conv_pre(r.cin[around, inner:], taps[:, inner:])
        u = pre * sigmoid(pre)
        r.b[rows, :] = u[:, :state].astype(BF16)
        r.c[rows, :] = u[:, state:]
        docs = doc_row(c)
        prev = r.doc_prev[0:1, 0:1]
        before = jnp.concatenate([prev, docs[:, : BLOCK - 1]], axis=1)
        ends = docs[:, BLOCK - 1 :]
        marks = [docs, (docs == prev).astype(F32), (docs == before).astype(F32), (docs == ends).astype(F32)]
        vt = r.tok[rows, :].T[0:heads]
        step = softplus(vt)
        la_hi, la_lo = halves(rate_col * step)
        cum = dot(la_hi, r.upper[...]) + dot(la_lo, r.upper[...])
        r.cumt[:, at(c)] = cum
        total = cum[:, BLOCK - 1 :]
        columns = [vt, cum, *marks, jnp.zeros((12, BLOCK), F32), step, jnp.exp(total - cum) * marks[3]]
        columns += [jnp.exp(cum) * marks[1], jnp.zeros((72, BLOCK), F32)]
        r.tok[rows, :] = jnp.concatenate(columns, axis=0).T
        held = jnp.exp(total) * (ends == prev).astype(F32)
        kept = jnp.sum(r.spread[...].astype(F32) * held, axis=0, keepdims=True)
        r.kept[c] = kept
        r.carry[...] = r.carry[...] * kept
        r.doc_prev[...] = jnp.broadcast_to(ends, r.doc_prev.shape)

    repeat(blocks, steps)

    pairs = heads // 2
    for pair in range(pairs):
        r.carry_part[pair] = r.carry[:, pair * lanes : (pair + 1) * lanes]
    r.own[...] = jnp.zeros_like(r.own)

    def relay(turn):
        pair = turn - 2 * seq

        @pl.when(jnp.logical_and(pair >= 0, pair < pairs))
        def _():
            @pl.when(seq > 0)
            def _():
                came(ENDS, pair, SEQ_AXIS, -1, r.end_in.at[pair])

            into = jnp.where(seq > 0, r.end_in[pair], 0.0)
            r.end_out[pair] = r.carry_part[pair] * into + r.own[pair]
            r.own[pair] = into

            @pl.when(seq < ns - 1)
            def _():
                link(ENDS, pair, SEQ_AXIS, 1, r.end_out.at[pair], r.end_in.at[pair]).start()

    for pair in range(pairs):
        cols = slice(pair * lanes, (pair + 1) * lanes)

        def own_states(c, pair=pair, cols=cols):
            rows = at(c)
            around = pl.ds(pl.multiple_of(c * BLOCK, BLOCK), BLOCK + EDGE)
            pre = conv_pre(r.cin[around, cols], taps[:, cols])
            xh = pre * sigmoid(pre)
            marks = both(r.tok[rows, :])
            xs = xh * expand_tok(marks, r.sel_step, cols)
            r.xs[rows, cols] = xs.astype(BF16)
            r.y[rows, cols] = skip[:, cols] * xh
            inc = dot(r.b[rows, :], (xs * expand_tok(marks, r.sel_end, cols)).astype(BF16), TN)
            r.inc[c, :, cols] = inc
            r.own[pair] = r.kept[c, :, cols] * r.own[pair] + inc

        repeat(blocks // 2, lambda i, body=own_states: (body(2 * i), body(2 * i + 1)))
        relay(pair)

    gather_2(COT, 0, cot_of, cot_half)

    def relay_back(turn):
        distance = ns - 1 - seq
        pair = turn - 2 * distance

        @pl.when(jnp.logical_and(distance > 0, jnp.logical_and(pair >= 0, pair < pairs)))
        def _():
            came(BACK, pair, SEQ_AXIS, 1, r.back_in.at[pair])
            into = r.back_in[pair].astype(F32)
            r.back_out[pair] = (r.carry_part[pair] * into + r.own[pair]).astype(BF16)
            r.own[pair] = into

            @pl.when(seq > 0)
            def _():
                link(BACK, pair, SEQ_AXIS, -1, r.back_out.at[pair], r.back_in.at[pair]).start()

    first = iota((BLOCK, lanes), 1) < lanes // 2

    def split(pair):
        zero = jnp.zeros_like(pair)
        return jnp.where(first, pair, zero), jnp.where(first, zero, pair)

    def intra(c):
        rows = at(c)
        cum, cumt = r.tok[rows, CUM : CUM + heads], r.cumt[:, at(c)]
        mask = jnp.where((row >= col) & (r.tok[rows, AUX : AUX + 1] == doc_row(c)), 0.0, NEG)
        scores = score_pair(r.c[rows, :], r.b[rows, :], True)
        for pair in range(heads // 2):
            cols = slice(pair * lanes, (pair + 1) * lanes)
            mixed = []
            for h in (2 * pair, 2 * pair + 1):
                decay = jnp.exp(cum[:, h : h + 1] - cumt[h : h + 1, :] + mask)
                mixed.append((scores * decay).astype(BF16))
            two = jnp.concatenate(split(r.xs[rows, cols]), axis=0)
            r.y[rows, cols] += dot(jnp.concatenate(mixed, axis=1), two)
        r.z[rows, :] = dot(r.normed[rows, :], r.wg[...])
        relay(pairs + c)

    loads[4].wait()
    repeat(blocks, intra)
    loads[5].wait()

    if 2 * (ns - 1) > blocks:
        repeat(2 * (ns - 1) - blocks, lambda i: relay(pairs + blocks + i))
    for pair in range(pairs):
        r.end[:, pair * lanes : (pair + 1) * lanes] = r.own[pair]
    gather_3(COT, 0, cot_of, cot_half)

    def dgn_of(rows):
        return dot(r.cot_all[rows, :], r.wo[...], NT)

    lane8 = iota((BLOCK, 8), 1)

    def sums(c):
        rows = at(c)
        si = r.end[...]
        r.end[...] = r.kept[c] * si + r.inc[c]
        r.inc[c] = si
        into = expand_tok(both(r.tok[rows, :]), r.sel_into)
        y = r.y[rows, :] + into * dot3(r.c[rows, :], si)
        r.y[rows, :] = y
        z = r.z[rows, :]
        g = y * (z * sigmoid(z))
        squares = jnp.sum(g * g, axis=1, keepdims=True)
        products = jnp.sum(dgn_of(rows) * out_gain * g, axis=1, keepdims=True)
        cols_hi, cols_lo = halves(jnp.where(lane8 == 0, squares, jnp.where(lane8 == 1, products, 0.0)))
        r.sum_out[c] = dot(cols_hi, r.eye[...], TN) + dot(cols_lo, r.eye[...], TN)
        for o in range(1, nh):
            index = c * (nh - 1) + o - 1
            link(SUM, index, HEAD_AXIS, o, r.sum_out.at[c], r.sum_in.at[index]).start()
        r.parts[c, :, :width] = dot((g * out_gain).astype(BF16), r.wo[...]).astype(BF16)
        scatter_1(OUT, 6 * c, out_block(c), r.out_in)

    def out_block(c):
        half = BLOCK // 2
        return lambda h, i: r.parts.at[c, pl.ds(i * half, half), pl.ds(pl.multiple_of(h * part, part), part)]

    repeat(blocks, sums)
    r.inc[blocks] = r.end[...]

    r.end[...] = jnp.zeros_like(r.end)
    r.prod[...] = jnp.ones_like(r.prod)
    r.pack[...] = jnp.zeros_like(r.pack)
    r.g_gain[...] = jnp.zeros_like(r.g_gain)

    def gate(c):
        rows = at(c)
        total = r.sum_out[c]
        for o in range(1, nh):
            index = c * (nh - 1) + o - 1
            came(SUM, index, HEAD_AXIS, -o, r.sum_in.at[index])
            total = total + r.sum_in[index]
        shares = dot_right(r.eye[...], total, NT)
        y, z = r.y[rows, :], r.z[rows, :]
        dgn = dgn_of(rows)
        sig = sigmoid(z)
        act = z * sig
        g = y * act
        rms = lax.rsqrt(shares[:, 0:1] / inner_all + EPS)
        r.tok[rows, RMS : RMS + 1] = rms
        gr = g * rms
        r.xs[rows, :] = (gr * out_gain).astype(BF16)
        r.g_gain[...] += jnp.sum(dgn * gr, axis=0, keepdims=True)
        dg = rms * (dgn * out_gain) - g * (rms * rms * rms * shares[:, 1:2] / inner_all)
        dy = dg * act
        dyb = dy.astype(BF16)
        r.dy[rows, :] = dyb
        r.dz[rows, :] = (dg * y * (sig * (1.0 + z * (1.0 - sig)))).astype(BF16)
        into = expand_tok(both(r.tok[rows, :]), r.sel_into)
        r.end[...] += r.prod[...] * dot(r.c[rows, :].astype(BF16), (dy * into).astype(BF16), TN)
        r.prod[...] = r.prod[...] * r.kept[c]

    repeat(blocks, gate)

    for pair in range(pairs):
        r.own[pair] = r.end[:, pair * lanes : (pair + 1) * lanes]

    @pl.when(seq == ns - 1)
    def _():
        for pair in range(pairs):
            r.back_out[pair] = r.own[pair].astype(BF16)
            link(BACK, pair, SEQ_AXIS, -1, r.back_out.at[pair], r.back_in.at[pair]).start()
        r.own[...] = jnp.zeros_like(r.own)

    r.gw_out[...] = jnp.zeros_like(r.gw_out)
    r.gw_gate[...] = jnp.zeros_like(r.gw_gate)

    def weight_grads(i):
        rows = pl.ds(pl.multiple_of(i * 2 * BLOCK, 2 * BLOCK), 2 * BLOCK)
        r.gw_out[...] += dot(r.xs[rows, :], r.cot_all[rows, :], TN)
        scatter_2(OUT, 12 * i, out_block(2 * i), r.out_in)
        relay_back(2 * i)
        r.gw_gate[...] += dot(r.normed[rows, :], r.dz[rows, :], TN)
        r.tok[rows, DYY : DYY + heads] = dot_left(r.dy[rows, :].astype(F32) * r.y[rows, :], r.collect[...])
        scatter_2(OUT, 12 * i + 6, out_block(2 * i + 1), r.out_in)
        relay_back(2 * i + 1)

    repeat(blocks // 2, weight_grads)

    def add_residual(c):
        cols = pl.ds(pl.multiple_of(head * part, part), part)
        half = BLOCK // 2
        for i, total in enumerate(scatter_3(OUT, 6 * c, out_block(c), r.out_in)):
            rows = pl.ds(pl.multiple_of(c * BLOCK + i * half, half), half)
            scaled = r.tok[rows, RMS : RMS + 1] * total
            r.block_out[rows, :] = (scaled + r.x[rows, cols].astype(F32)).astype(BF16)

    def ref(name, kind):
        return getattr(r, name + kind)

    def half_of(name, source, core):
        if name == WO:
            half = source.shape[1] // 2
            return source.at[:, pl.ds(pl.multiple_of(core * half, half), half)]
        half = source.shape[0] // 2
        return source.at[pl.ds(pl.multiple_of(core * half, half), half)]

    near = seq < ns // 2
    depth, last = jnp.where(near, seq, ns - 1 - seq), ns // 2 - 1
    inward = jnp.where(near, 1, -1)

    def piece_of(name, half, j):
        rows = half.shape[0] // PIECES[name]
        return half.at[pl.ds(j * rows, rows)]

    def result(name, core, j):
        whole = ref(name, "_sum")
        return piece_of(name, whole if name == WQ else half_of(name, whole, core), j)

    def total_a(name, source):
        return link(name + "a", 0, DP_AXIS, 1, half_of(name, source, 1 - dp), ref(name, "_pair"))

    def total_b(name, source):
        total_a(name, source).wait_send()
        came(name + "a", 0, DP_AXIS, 1, ref(name, "_pair"))
        mine = ref(name, "_mine")
        mine[...] = (half_of(name, source, dp)[...] + ref(name, "_pair")[...]).astype(mine.dtype)

        start_inward(name)

    def start_inward(name):
        mine = ref(name, "_mine")

        @pl.when(depth == 0)
        def _():
            for j in range(PIECES[name]):
                link(name + "b", j, SEQ_AXIS, inward, piece_of(name, mine, j), ref(name, "_in").at[j]).start()

    def total_c(name, pieces=None):
        @pl.when(depth > 0)
        def _():
            for j in pieces or range(PIECES[name]):
                came(name + "b", j, SEQ_AXIS, -inward, ref(name, "_in").at[j])
                mine = piece_of(name, ref(name, "_mine"), j)
                mine[...] = (mine[...].astype(F32) + ref(name, "_in")[j].astype(F32)).astype(mine.dtype)

                @pl.when(depth < last)
                def _():
                    link(name + "b", j, SEQ_AXIS, inward, mine, ref(name, "_in").at[j]).start()

                @pl.when(depth == last)
                def _():
                    link(name + "c", j, SEQ_AXIS, inward, mine, result(name, dp, j)).start()

    def total_d(name, middle, pieces=None):
        for j in pieces or range(PIECES[name]):
            total = result(name, dp, j)

            @pl.when(depth == last if middle else depth < last)
            def _():
                if middle:
                    came(name + "c", j, SEQ_AXIS, inward, total)
                    mine = piece_of(name, ref(name, "_mine"), j)
                    total[...] = (mine[...].astype(F32) + total[...].astype(F32)).astype(mine.dtype)
                else:
                    came(name + "f", j, SEQ_AXIS, inward, total)

                @pl.when(depth > 0)
                def _():
                    link(name + "f", j, SEQ_AXIS, -inward, total, total).start()

                if name != WQ:
                    link(name + "d", j, DP_AXIS, 1, total, total).start()

    def total_e(name):
        for j in range(PIECES[name]):
            total, mine = result(name, dp, j), piece_of(name, ref(name, "_mine"), j)
            if name != WQ:
                came(name + "d", j, DP_AXIS, 1, result(name, 1 - dp, j))
                sent(name + "d", j, DP_AXIS, 1, total)

            @pl.when(depth < last)
            def _():
                sent(name + "b", j, SEQ_AXIS, inward, mine)

            @pl.when(depth == last)
            def _():
                sent(name + "c", j, SEQ_AXIS, inward, mine)

            @pl.when(depth > 0)
            def _():
                sent(name + "f", j, SEQ_AXIS, -inward, total)

    total_a(WO, r.gw_out).start()
    total_a(WG, r.gw_gate).start()

    repeat(blocks // 2, add_residual)
    if 2 * (ns - 1) + pairs > blocks:
        repeat(2 * (ns - 1) + pairs - blocks, lambda i: relay_back(blocks + i))
    for pair in range(pairs):
        r.end[:, pair * lanes : (pair + 1) * lanes] = r.own[pair]
    r.g_dt[...] = jnp.zeros_like(r.g_dt)
    r.g_log[...] = jnp.zeros_like(r.g_log)
    r.g_skip[...] = jnp.zeros_like(r.g_skip)
    r.g_conv[...] = jnp.zeros_like(r.g_conv)
    r.gw_bc[...] = jnp.zeros_like(r.gw_bc)
    r.g_norm[...] = jnp.zeros_like(r.g_norm)

    def back(c):
        rows = at(c)
        around = pl.ds(pl.multiple_of(c * BLOCK, BLOCK), BLOCK + EDGE)
        inside = pl.ds(pl.multiple_of(c * BLOCK + EDGE, EDGE), BLOCK)
        b_mat, c_full = r.b[rows, :], r.c[rows, :]
        c_mat = c_full.astype(BF16)
        v = r.tok[rows, 0:heads]
        step = r.tok[rows, STEP : STEP + heads]
        cum, cumt, aux = r.tok[rows, CUM : CUM + heads], r.cumt[:, at(c)], r.tok[rows, AUX : AUX + 8]
        mask = jnp.where((row <= col) & (aux[:, 0:1] == doc_row(c)), 0.0, NEG)
        scores = score_pair(c_full, b_mat, False)
        marks = both(r.tok[rows, :])
        d_scores = jnp.zeros((BLOCK, BLOCK), F32)
        d_b = jnp.zeros((BLOCK, state), F32)
        d_c = jnp.zeros((BLOCK, state), F32)
        d_step_own = jnp.zeros((BLOCK, heads), F32)
        d_cum = r.tok[rows, DYY : DYY + heads]
        through = jnp.zeros((1, heads), F32)

        def conv_grad(d_u, window, pre, sig, cols):
            d_pre = d_u * (sig * (1.0 + pre * (1.0 - sig)))
            for k in range(n_taps):
                shifted = window[EDGE - k : EDGE - k + BLOCK]
                r.g_conv[k : k + 1, cols] += jnp.sum(d_pre * shifted, axis=0, keepdims=True)
            r.g_conv[n_taps : n_taps + 1, cols] += jnp.sum(d_pre, axis=0, keepdims=True)
            r.cin[inside, cols] = d_pre

        for pair in range(heads // 2):
            cols = slice(pair * lanes, (pair + 1) * lanes)
            window = r.cin[around, cols]
            pre = conv_pre(window, taps[:, cols])
            sig = sigmoid(pre)
            xh = pre * sig
            step_e, to_end_e, into_e = (expand_tok(marks, sel, cols) for sel in (r.sel_step, r.sel_end, r.sel_into))
            xs = xh * step_e
            xsb = xs.astype(BF16)
            dyb = r.dy[rows, cols]
            dy = dyb.astype(F32)
            adj = r.end[:, cols]
            dye = dy * into_e
            d_c = d_c + dot3(dye, r.inc[c, :, cols], NT)
            d_b = d_b + dot3(xs * to_end_e, adj, NT)
            d_xs_inter = to_end_e * dot(b_mat, adj.astype(BF16))
            two = split(dyb)
            mixed = []
            for i, h in enumerate((2 * pair, 2 * pair + 1)):
                decay = jnp.exp(cumt[h : h + 1, :] - cum[:, h : h + 1] + mask)
                mixed.append((scores * decay).astype(BF16))
                d_scores = d_scores + dot(xsb, two[i], NT) * decay
            d_xs_intra = dot(jnp.concatenate(mixed, axis=1), jnp.concatenate(two, axis=0))
            d_xs = d_xs_intra + d_xs_inter
            collect = jnp.concatenate([r.collect[cols, :]] * 2, axis=0)
            d_step_own = d_step_own + dot(both(xh * d_xs), collect)
            lost = skip[:, cols] * (dy * xh) + (xsb.astype(F32) * d_xs_intra + xs * d_xs_inter)
            d_cum = d_cum - dot(both(lost), collect)
            ended = jnp.sum(adj * r.inc[c + 1, :, cols], axis=0, keepdims=True)
            through = through + dot(both(ended), collect)
            r.g_skip[:, cols] += jnp.sum(dy * xh, axis=0, keepdims=True)
            r.end[:, cols] = r.kept[c, :, cols] * adj + dot(c_mat, dye.astype(BF16), TN)
            conv_grad(skip[:, cols] * dy + step_e * d_xs, window, pre, sig, cols)
        d_sb = d_scores.astype(BF16)
        d_b = d_b + dot(d_sb, c_mat)
        d_c = d_c + dot(d_sb, b_mat, TN)
        cols = slice(inner, channels)
        window = r.cin[around, cols]
        pre = conv_pre(window, taps[:, cols])
        conv_grad(jnp.concatenate([d_b, d_c], axis=1), window, pre, sigmoid(pre), cols)
        d_la = (dot_right(r.upper[...], d_cum) + through) * aux[:, 2:3]
        r.g_log[...] += jnp.sum(rate * step * d_la, axis=0, keepdims=True)
        d_v = (d_step_own + rate * d_la) * sigmoid(v)
        r.g_dt[...] += jnp.sum(d_v, axis=0, keepdims=True)
        r.dstep[rows, :] = d_v.astype(BF16)

    def project_back(c):
        rows = at(c)
        window = r.cin[pl.ds(pl.multiple_of(c * BLOCK + EDGE, EDGE), BLOCK + EDGE), :]
        d_in = taps[0:1, :] * window[:BLOCK]
        for k in range(1, n_taps):
            d_in = d_in + taps[k : k + 1, :] * window[k : k + BLOCK]
        d_inb = d_in.astype(BF16)
        d_val = d_inb[:, :inner]
        dstep = r.dstep[rows, :]
        normed = r.normed[rows, :]
        grads = dot(normed, d_inb, TN)
        r.gw_value[...] += grads[:, :inner]
        r.gw_bc[...] += grads[:, inner:]
        r.pack[0:heads, :] += dot(dstep, normed, TN)
        d_part = dot(r.dz[rows, :], r.wg[...], NT) + dot(d_val, r.wv[...], NT) + dot(dstep, r.ws[...])
        scatter_sent(OUT, 6 * c, out_block(c))
        r.parts[c, :, :width] = d_part.astype(BF16)
        r.parts[c, :, width:] = d_inb[:, inner:]
        scatter_1(PART, 6 * c, part_block(c), r.part_in)

    def part_block(c):
        half = slab // 2
        return lambda h, i: r.parts.at[c, pl.ds(pl.multiple_of(h * slab + i * half, half), half)]

    def combine(c):
        scatter_2(PART, 6 * c, part_block(c), r.part_in)

    def slab_of(c):
        return lambda h: r.normed.at[pl.ds(pl.multiple_of(c * BLOCK + h * slab, slab), slab)]

    def slab_half(c):
        half = slab // 2
        return lambda h, i: r.normed.at[pl.ds(pl.multiple_of(c * BLOCK + h * slab + i * half, half), half)]

    def forward(c):
        gather_2(GRAD, 4 * c, slab_of(c), slab_half(c))

    def own_slab(c):
        return pl.ds(pl.multiple_of(c * BLOCK + head * slab, slab), slab)

    def finish(c):
        rows = own_slab(c)
        total = jnp.concatenate(scatter_3(PART, 6 * c, part_block(c), r.part_in), axis=0)
        x = r.x[rows, :].astype(F32)
        norm = lax.rsqrt(jnp.mean(x * x, axis=1, keepdims=True) + EPS)
        xr = x * norm
        d_bc = total[:, width:].astype(BF16)
        d_normed = total[:, :width] + dot(d_bc, r.wbc[...], NT)
        r.g_norm[...] += jnp.sum(d_normed * xr, axis=0, keepdims=True)
        q = d_normed * gain
        d_x = norm * q - xr * (norm * norm * jnp.mean(q * x, axis=1, keepdims=True))
        r.normed[rows, :] = (d_x + r.cot_all[rows, :].astype(F32)).astype(BF16)
        gather_1(GRAD, 4 * c, slab_of(c))

    def reverse(t):
        c = blocks - 1 - t
        back(c)

        @pl.when(t == 0)
        def _():
            total_b(WO, r.gw_out)
            total_b(WG, r.gw_gate)
            r.gw_value[...] = jnp.zeros_like(r.gw_value)

        @pl.when(t < blocks - blocks // 2)
        def _():
            add_residual(c)

        @pl.when(t >= 1)
        def _():
            project_back(c)

        @pl.when(t >= 2)
        def _():
            combine(c + 1)

        @pl.when(t == 2)
        def _():
            total_c(WO)

        @pl.when(t >= LAG)
        def _():
            finish(c + LAG - 1)

        @pl.when(t >= LAG + 2)
        def _():
            forward(c + LAG + 1)

        @pl.when(t == 4)
        def _():
            total_c(WG)
            total_d(WO, True)

    repeat(blocks, reverse)

    first_rows = r.cin.at[pl.ds(EDGE, EDGE)]
    last_rows = r.cin.at[pl.ds(EDGE + tokens, EDGE)]
    link(EDGES, 0, SEQ_AXIS, -1, first_rows, last_rows).start()
    order = [*range(blocks - 2, -1, -1), blocks - 1]
    unfinished, unsent = order[blocks - LAG :], order[max(blocks - LAG - 2, 0) :]
    came(EDGES, 0, SEQ_AXIS, 1, last_rows)

    @pl.when(seq == ns - 1)
    def _():
        r.cin[EDGE + tokens :, :] = jnp.zeros((EDGE, channels), F32)

    project_back(blocks - 1)
    total_a(WV, r.gw_value).start()

    half_rows = width // 2
    quarter = half_rows // nh

    def bc_rows(whole, core, h):
        return whole.at[pl.ds(pl.multiple_of(core * half_rows + h * quarter, quarter), quarter)]

    def half_bc(core):
        return r.gw_bc.at[pl.ds(pl.multiple_of(core * half_rows, half_rows), half_rows)]

    link(BC, nh - 1, DP_AXIS, 1, half_bc(1 - dp), r.bc_pair).start()
    r.pack[9 : 9 + n_taps + 1, :channels] = r.g_conv[: n_taps + 1, :]
    r.pack[14:15, :inner] = r.g_gain[...]
    r.pack[15:16, 0:heads] = r.g_dt[...]
    r.pack[15:16, 128 : 128 + heads] = r.g_log[...]
    r.pack[15:16, 256 : 256 + heads] = dot_left(r.g_skip[...], r.collect[...])
    r.pack_out[...] = r.pack[8:16, :]
    for o in range(1, nh):
        link(PACK1, o - 1, HEAD_AXIS, o, r.pack_out, r.pack1_in.at[o - 1]).start()
    total_d(WG, True)
    total_b(WV, r.gw_value)
    came(BC, nh - 1, DP_AXIS, 1, r.bc_pair)
    r.bc_out[...] = (half_bc(dp)[...] + r.bc_pair[...]).astype(BF16)
    for o in range(1, nh):
        link(BC, o - 1, HEAD_AXIS, o, bc_rows(r.bc_out, 0, square[o]), r.bc_in.at[o - 1]).start()
    combine(0)
    forward(unsent[0])
    finish(unfinished[0])
    total_c(WV, (0, 1))
    for o in range(1, nh):
        came(PACK1, o - 1, HEAD_AXIS, -o, r.pack1_in.at[o - 1])
        r.pack[9 : 9 + n_taps + 1, inner:channels] += r.pack1_in[o - 1, 1 : 2 + n_taps, inner:channels]
    total_a(WP, r.pack).start()
    combine(blocks - 1)
    total_c(WV, (2, 3))
    total_d(WV, True, (0, 1))
    for c in unfinished[1:-1]:
        finish(c)
    forward(unsent[1])
    total_c(WV, (4, 5))
    total_d(WV, True, (2, 3))
    mine = bc_rows(r.bc_out, 0, head)[...].astype(F32)
    for o in range(1, nh):
        came(BC, o - 1, HEAD_AXIS, -o, r.bc_in.at[o - 1])
        mine = mine + r.bc_in[o - 1].astype(F32)
    r.wq_mine[...] = mine.astype(BF16)
    start_inward(WQ)
    total_b(WP, r.pack)
    total_c(WV, (6, 7))
    total_d(WV, True, (4, 5))
    total_d(WO, False)
    total_d(WG, False)
    finish(blocks - 1)
    for o in range(1, nh):
        link(NORM, o - 1, HEAD_AXIS, o, r.g_norm, r.norm_in.at[o - 1]).start()
    total_d(WV, True, (6, 7))
    total_c(WP)
    total_c(WQ)
    for c in unsent[2:-1]:
        forward(c)
    total_d(WP, True)
    total_d(WQ, True)
    total_d(WV, False)
    total = r.g_norm[...]
    for o in range(1, nh):
        came(NORM, o - 1, HEAD_AXIS, -o, r.norm_in.at[o - 1])
        total = total + r.norm_in[o - 1]
    r.norm_out[0] = total
    link(NORM, nh - 1, DP_AXIS, 1, r.norm_out.at[0], r.norm_in.at[nh - 1]).start()
    forward(blocks - 1)
    total_d(WP, False)
    total_d(WQ, False)
    total_e(WQ)
    mine = bc_rows(r.bc_sum, dp, head)
    mine[...] = r.wq_sum[...]
    for o in range(1, nh):
        link(BCG, o - 1, HEAD_AXIS, o, mine, mine).start()
    link(BCG, nh - 1, DP_AXIS, 1, mine, mine).start()
    came(NORM, nh - 1, DP_AXIS, 1, r.norm_in.at[nh - 1])
    total = r.norm_out[0] + r.norm_in[nh - 1]
    r.norm_out[1] = total
    for o in range(1, ns):
        link(NORM, nh + o - 1, SEQ_AXIS, o, r.norm_out.at[1], r.norm_in.at[nh + o - 1]).start()
    for name in (WO, WG, WV, WP):
        total_e(name)

    r.norm_all[seq] = total
    for o in range(1, ns):
        came(NORM, nh + o - 1, SEQ_AXIS, -o, r.norm_in.at[nh + o - 1])
        r.norm_all[other(SEQ_AXIS, -o)] = r.norm_in[nh + o - 1]
    total = r.norm_all[0]
    for k in range(1, ns):
        total = total + r.norm_all[k]
    r.norm_sum[...] = total
    for o in range(1, nh):
        theirs = bc_rows(r.bc_sum, dp, square[o])
        came(BCG, o - 1, HEAD_AXIS, -o, theirs)
        link(BCG, nh - 1 + o, DP_AXIS, 1, theirs, theirs).start()
        sent(BCG, o - 1, HEAD_AXIS, o, mine)
        sent(BC, o - 1, HEAD_AXIS, o, bc_rows(r.bc_out, 0, square[o]))
        sent(PACK1, o - 1, HEAD_AXIS, o, r.pack_out)
        sent(NORM, o - 1, HEAD_AXIS, o, r.g_norm)
    for o in range(nh):
        came(BCG, nh - 1 + o, DP_AXIS, 1, bc_rows(r.bc_sum, 1 - dp, square[o]))
        sent(BCG, nh - 1 + o, DP_AXIS, 1, bc_rows(r.bc_sum, dp, square[o]))
    sent(BC, nh - 1, DP_AXIS, 1, half_bc(1 - dp))
    sent(NORM, nh - 1, DP_AXIS, 1, r.norm_out.at[0])
    for o in range(1, ns):
        sent(NORM, nh + o - 1, SEQ_AXIS, o, r.norm_out.at[1])
    sent(HALO, 0, SEQ_AXIS, 1, x_tail)
    sent(HALO, 1, SEQ_AXIS, 1, r.doc_out)
    sent(EDGES, 0, SEQ_AXIS, -1, first_rows)

    @pl.when(seq > 0)
    def _():
        for pair in range(pairs):
            sent(BACK, pair, SEQ_AXIS, -1, r.back_out.at[pair])

    @pl.when(seq < ns - 1)
    def _():
        for pair in range(pairs):
            sent(ENDS, pair, SEQ_AXIS, 1, r.end_out.at[pair])

    def drain(c):
        for o in range(1, nh):
            sent(SUM, c * (nh - 1) + o - 1, HEAD_AXIS, o, r.sum_out.at[c])
        scatter_sent(PART, 6 * c, part_block(c))
        gather_3(GRAD, 4 * c, slab_of(c), slab_half(c))
        store(c).start()

    def store(c):
        return pltpu.make_async_copy(r.normed.at[at(c)], r.grad_in.at[at(c)], r.stored.at[c])

    repeat(blocks, drain)
    repeat(blocks, lambda c: store(c).wait())


def write_kernel(n, *refs):
    small, norm_sum = refs[n : n + 2]
    for source, target in zip(refs[:n], refs[n + 2 :]):
        target[...] = source[...].astype(target.dtype)
    norm, step, conv_v, conv_b, dt, log, skip, gain = refs[2 * n + 2 :]
    inner, heads, taps = conv_v.shape[1], dt.shape[1], conv_v.shape[0]

    @pl.when(pl.program_id(0) == 0)
    def _():
        norm[...] = norm_sum[...]
        step[...] = small[0:heads, :]
        conv_v[...] = small[9 : 9 + taps, :inner]
        conv_b[...] = small[9 : 9 + taps, inner : inner + conv_b.shape[1]]
        dt[...] = small[15:16, 0:heads]
        log[...] = small[15:16, 128 : 128 + heads]
        skip[...] = small[15:16, 256 : 256 + heads]
        gain[...] = small[14:15, :inner]


def on_device(
    hidden_in, doc_ids, norm_gain, w_gate, w_value, w_bc, w_step, conv_value, conv_bc, dt_bias, a_log, d_skip,
    out_gain, w_out, cotangent,
):
    x, cot = hidden_in[0], cotangent[0]
    tokens, width = x.shape
    inner, heads = w_gate.shape[1], w_step.shape[1]
    bc_width, head_dim = w_bc.shape[1], inner // heads
    state = bc_width // 2
    channels = inner + bc_width
    blocks = tokens // BLOCK
    nh, ns = lax.axis_size(HEAD_AXIS), lax.axis_size(SEQ_AXIS)
    part, slab = width // nh, BLOCK // nh
    n_taps = conv_value.shape[0] - 1
    vmem, hbm = pltpu.VMEM, pl.ANY
    inputs = dict(
        x_hbm=x, cot=cot, docs=doc_ids, gain=norm_gain[None], wg_hbm=w_gate, wv_hbm=w_value, wbc_hbm=w_bc,
        ws=w_step.T, wo_hbm=w_out, cv=conv_value, cb=conv_bc, dtb=dt_bias[None], alog=a_log[None],
        dskip=d_skip[None], og=out_gain[None],
    )
    outputs = dict(
        block_out=((tokens, part), BF16),
        grad_in=((tokens, width), BF16),
        wg_sum=(w_gate.shape, BF16),
        wv_sum=(w_value.shape, BF16),
        wo_sum=(w_out.shape, BF16),
        bc_sum=(w_bc.shape, BF16),
        wp_sum=((16, width), F32),
        norm_sum=((1, width), F32),
    )
    scratch = dict(
        x=vmem((tokens, width), BF16),
        wg=vmem(w_gate.shape, BF16),
        wv=vmem(w_value.shape, BF16),
        wbc=vmem(w_bc.shape, BF16),
        wo=vmem(w_out.shape, BF16),
        bc_in=vmem((nh - 1, width // 2 // nh, bc_width), BF16),
        cot_all=vmem((tokens, width), BF16),
        halo_x=vmem((TAIL, width), BF16),
        doc_out=vmem((8, 128), F32),
        doc_in=vmem((8, 128), F32),
        doc_prev=vmem((8, 128), F32),
        upper=vmem((BLOCK, BLOCK), BF16),
        eye=vmem((BLOCK, BLOCK), BF16),
        spread=vmem((heads, inner), BF16),
        collect=vmem((inner, heads), BF16),
        normed=vmem((tokens, width), BF16),
        z=vmem((tokens, inner), F32),
        cin=vmem((EDGE + tokens + EDGE, channels), F32),
        y=vmem((tokens, inner), F32),
        xs=vmem((tokens, inner), BF16),
        dy=vmem((tokens, inner), BF16),
        b=vmem((tokens, state), BF16),
        c=vmem((tokens, state), F32),
        tok=vmem((tokens, 128), F32),
        cumt=vmem((heads, tokens), F32),
        dstep=vmem((tokens, heads), BF16),
        inc=vmem((blocks + 1, state, inner), F32),
        kept=vmem((blocks, 1, inner), F32),
        end=vmem((state, inner), F32),
        own=vmem((heads // 2, state, 2 * head_dim), F32),
        end_out=vmem((heads // 2, state, 2 * head_dim), F32),
        end_in=vmem((heads // 2, state, 2 * head_dim), F32),
        carry_part=vmem((heads // 2, 1, 2 * head_dim), F32),
        sel_step=vmem((256, inner), BF16),
        sel_end=vmem((256, inner), BF16),
        sel_into=vmem((256, inner), BF16),
        back_out=vmem((heads // 2, state, 2 * head_dim), BF16),
        norm_in=vmem((nh + ns - 1, 1, width), F32),
        norm_out=vmem((2, 1, width), F32),
        norm_all=vmem((ns, 1, width), F32),
        back_in=vmem((heads // 2, state, 2 * head_dim), BF16),
        carry=vmem((1, inner), F32),
        prod=vmem((1, inner), F32),
        sum_out=vmem((blocks, 8, BLOCK), F32),
        sum_in=vmem((blocks * (nh - 1), 8, BLOCK), F32),
        parts=vmem((blocks, BLOCK, width + bc_width), BF16),
        out_in=vmem((blocks * 6, BLOCK // 2, part), BF16),
        part_in=vmem((blocks * 6, slab // 2, width + bc_width), BF16),
        gw_out=vmem(w_out.shape, F32),
        wq_sum=vmem((width // 2 // nh, bc_width), BF16),
        dz=vmem((tokens, inner), BF16),
        g_gain=vmem((1, inner), F32),
        g_dt=vmem((1, heads), F32),
        g_log=vmem((1, heads), F32),
        g_skip=vmem((1, inner), F32),
        g_conv=vmem((8, channels), F32),
        g_norm=vmem((1, width), F32),
        pack=vmem((16, width), F32),
        pack_out=vmem((8, width), F32),
        pack1_in=vmem((nh - 1, 8, width), F32),
        load=pltpu.SemaphoreType.DMA((6,)),
        stored=pltpu.SemaphoreType.DMA((blocks,)),
    )
    for name, (rows, cols), kind in (
        (WO, (inner, width // 2), BF16), (WG, (width // 2, inner), BF16), (WV, (width // 2, inner), BF16),
        (WQ, (width // 2 // nh, bc_width), BF16), (WP, (8, width), F32),
    ):
        if name not in (WV, WQ):
            scratch[name + "_pair"] = vmem((rows, cols), F32)
        if name != WV:
            scratch[name + "_mine"] = vmem((rows, cols), kind)
        scratch[name + "_in"] = vmem((PIECES[name], rows // PIECES[name], cols), kind)
    counts = dict(
        cot=4, halo=2, ends=heads // 2, back=heads // 2, norm=nh + ns - 1, sum=blocks * (nh - 1), out=blocks * 6,
        part=blocks * 6, grad=blocks * 4, edge=1, bc=nh, bcg=2 * nh - 1, pack1=nh - 1,
    )
    for name, n in PIECES.items():
        counts |= {name + "a": 1, name + "b": n, name + "c": n, name + "d": n, name + "f": n}
    for name, n in counts.items():
        scratch[name + "_s"] = pltpu.SemaphoreType.DMA((n,))
        scratch[name + "_r"] = pltpu.SemaphoreType.DMA((n,))
    names = [*inputs, *outputs, *scratch]

    def run(*refs):
        r = types.SimpleNamespace(**dict(zip(names, refs)))
        r.gw_gate = r.gw_value = r.z.at[pl.ds(0, width)]
        r.wv_pair = r.z.at[pl.ds(width, width // 2)]
        r.gw_bc = r.y.at[pl.ds(0, width), pl.ds(0, bc_width)]
        r.bc_pair = r.y.at[pl.ds(width, width // 2), pl.ds(0, bc_width)]
        r.bc_out = r.xs.at[pl.ds(0, width // 2), pl.ds(0, bc_width)]
        r.wv_mine = r.xs.at[pl.ds(width, width // 2)]
        kernel(r)

    block_out, grad_in, g_gate, g_value, g_out, g_bc, small, norm = pl.pallas_call(
        run,
        out_shape=[jax.ShapeDtypeStruct(*o) for o in outputs.values()],
        in_specs=[pl.BlockSpec(memory_space=hbm if name in LOADED else vmem) for name in inputs],
        out_specs=[pl.BlockSpec(memory_space=hbm if name == "grad_in" else vmem) for name in outputs],
        scratch_shapes=list(scratch.values()),
        compiler_params=pltpu.CompilerParams(
            collective_id=0, has_side_effects=True, vmem_limit_bytes=VMEM_LIMIT
        ),
        name="block",
    )(*inputs.values())
    steps = 8
    grads = (block_out, grad_in, g_gate, g_value, g_out, g_bc)
    kinds = (BF16, BF16, F32, F32, F32, F32)
    tiny = ((1, width), (heads, width), (n_taps + 1, inner), (n_taps + 1, bc_width), (1, heads), (1, heads), (1, heads),
            (1, inner))

    def split_rows(a):
        return pl.BlockSpec((a.shape[0] // steps, a.shape[1]), lambda i: (i, 0))

    def whole(dims):
        return pl.BlockSpec(dims, lambda i: (0, 0))

    outs = pl.pallas_call(
        functools.partial(write_kernel, len(grads)),
        grid=(steps,),
        in_specs=[*map(split_rows, grads), whole(small.shape), whole(norm.shape)],
        out_specs=[*map(split_rows, grads), *map(whole, tiny)],
        out_shape=[jax.ShapeDtypeStruct(a.shape, k) for a, k in zip(grads, kinds)]
        + [jax.ShapeDtypeStruct(dims, F32) for dims in tiny],
        compiler_params=pltpu.CompilerParams(vmem_limit_bytes=VMEM_LIMIT),
        name="write",
    )(*grads, small, norm)
    block_out, grad_in, g_gate, g_value, g_out, g_bc, g_norm, g_step, g_cv, g_cb, g_dt, g_log, g_skip, g_gain = outs
    return (
        block_out[None], grad_in[None], g_norm[0], g_gate, g_value, g_bc, g_step.T, g_cv, g_cb, g_dt[0], g_log[0],
        g_skip[0], g_gain[0], g_out,
    )


def solution(mesh):
    return jax.shard_map(
        on_device,
        mesh=mesh,
        in_specs=(
            P(DP_AXIS, SEQ_AXIS, None),
            P(DP_AXIS, SEQ_AXIS),
            P(),
            P(None, HEAD_AXIS),
            P(None, HEAD_AXIS),
            P(),
            P(None, HEAD_AXIS),
            P(None, HEAD_AXIS),
            P(),
            P(HEAD_AXIS),
            P(HEAD_AXIS),
            P(HEAD_AXIS),
            P(HEAD_AXIS),
            P(HEAD_AXIS, None),
            P(DP_AXIS, SEQ_AXIS, HEAD_AXIS),
        ),
        out_specs=(
            P(DP_AXIS, SEQ_AXIS, HEAD_AXIS),
            P(DP_AXIS, SEQ_AXIS, None),
            P(),
            P(None, HEAD_AXIS),
            P(None, HEAD_AXIS),
            P(),
            P(None, HEAD_AXIS),
            P(None, HEAD_AXIS),
            P(),
            P(HEAD_AXIS),
            P(HEAD_AXIS),
            P(HEAD_AXIS),
            P(HEAD_AXIS),
            P(HEAD_AXIS, None),
        ),
        check_vma=False,
    )
```

```python
import functools
import types

import jax
import jax.numpy as jnp
from jax import lax
from jax.experimental import pallas as pl
from jax.experimental.pallas import tpu as pltpu
from jax.sharding import PartitionSpec as P

BLOCK = 256
EDGE = 8
TAIL = 16
EPS = 1e-05
NEG = -1e30
F32 = jnp.float32
BF16 = jnp.bfloat16
NN = (((1,), (0,)), ((), ()))
NT = (((1,), (1,)), ((), ()))
TN = (((0,), (0,)), ((), ()))
MESH = pl.DeviceIdType.MESH
CUM, AUX, DYY, STEP, TO_END, INTO, RMS = 8, 16, 24, 32, 40, 48, 56
LAG = 3
EARLY = 2
HEAD_AXIS, SEQ_AXIS, DP_AXIS = "head", "seq", "dp"
COT, HALO, ENDS, NORM, BACK, SUM, OUT, PART, GRAD, EDGES, BC, BCG, PACK1 = (
    "cot", "halo", "ends", "norm", "back", "sum", "out", "part", "grad", "edge", "bc", "bcg", "pack1"
)
WO, WG, WV, WQ, WP = "wo", "wg", "wv", "wq", "wp"
PIECES = {WO: 4, WG: 4, WV: 8, WQ: 1, WP: 1}
LOADED = ("x_hbm", "cot", "wg_hbm", "wv_hbm", "wbc_hbm", "wo_hbm")
VMEM_LIMIT = 63 * 1024 * 1024


def dot(a, b, dims=NN):
    return lax.dot_general(a, b, dims, preferred_element_type=F32)


def halves(v):
    hi = v.astype(BF16)
    return hi, (v - hi.astype(F32)).astype(BF16)


def dot_left(v, m, dims=NN):
    hi, lo = halves(v)
    return dot(hi, m, dims) + dot(lo, m, dims)


def dot_right(m, v, dims=NN):
    hi, lo = halves(v)
    return dot(m, hi, dims) + dot(m, lo, dims)


def both(v, axis=1):
    return jnp.concatenate(halves(v), axis=axis)


def dot3(a, b, dims=NN):
    (ah, al), (bh, bl) = halves(a), halves(b)
    return dot(
        jnp.concatenate([ah, al, ah], axis=1), jnp.concatenate([bh, bh, bl], axis=dims[0][1][0]), dims
    )


def score_pair(c, b, first):
    hi, lo = halves(c)
    cc, bb = jnp.concatenate([hi, lo], axis=1), jnp.concatenate([b, b], axis=1)
    return dot(cc, bb, NT) if first else dot(bb, cc, NT)


def sigmoid(v):
    return 0.5 * jnp.tanh(0.5 * v) + 0.5


def softplus(v):
    return jnp.maximum(v, 0.0) + jnp.log1p(jnp.exp(-jnp.abs(v)))


def iota(shape, axis):
    return lax.broadcasted_iota(jnp.int32, shape, axis)


def in_norm(x, gain):
    r = lax.rsqrt(jnp.mean(x * x, axis=1, keepdims=True) + EPS)
    return (x * r * gain).astype(BF16)


def repeat(n, body):
    def run(i, carry):
        body(i)
        return carry

    lax.fori_loop(0, n, run, 0)


def kernel(r):
    nh, ns = lax.axis_size(HEAD_AXIS), lax.axis_size(SEQ_AXIS)
    head, seq, dp = lax.axis_index(HEAD_AXIS), lax.axis_index(SEQ_AXIS), lax.axis_index(DP_AXIS)
    me = {HEAD_AXIS: head, SEQ_AXIS: seq, DP_AXIS: dp}
    count = {HEAD_AXIS: nh, SEQ_AXIS: ns, DP_AXIS: 2}
    tokens, width = r.x.shape
    inner, heads = r.wg.shape[1], r.ws.shape[0]
    state = r.wbc.shape[1] // 2
    channels = inner + 2 * state
    blocks, part, slab = tokens // BLOCK, width // nh, BLOCK // nh
    inner_all = inner * nh
    n_taps = r.cv.shape[0] - 1
    lanes = 2 * (inner // heads)

    def at(c):
        return pl.ds(pl.multiple_of(c * BLOCK, BLOCK), BLOCK)

    left, upper_half = lax.rem(head, 2), lax.div(head, 2)
    square = [head, 2 * upper_half + 1 - left, 2 * (1 - upper_half) + left, nh - 1 - head]

    def other(axis, o):
        if axis == HEAD_AXIS:
            return square[abs(o)]
        return lax.rem(me[axis] + o + count[axis], count[axis])

    def link(name, index, axis, o, src, dst):
        return pltpu.make_async_remote_copy(
            src_ref=src,
            dst_ref=dst,
            send_sem=getattr(r, name + "_s").at[index],
            recv_sem=getattr(r, name + "_r").at[index],
            device_id={axis: other(axis, o)},
            device_id_type=MESH,
        )

    def sent(name, index, axis, o, src):
        link(name, index, axis, o, src, src).wait_send()

    def came(name, index, axis, o, dst):
        link(name, index, axis, o, dst, dst).wait_recv()

    def gather_1(name, base, view):
        for o in (1, 2):
            link(name, base + o - 1, HEAD_AXIS, o, view(head), view(head)).start()

    def gather_2(name, base, view, half):
        for o in (1, 2):
            came(name, base + o - 1, HEAD_AXIS, o, view(square[o]))
            piece = half(square[o], o - 1)
            link(name, base + 1 + o, HEAD_AXIS, 3 - o, piece, piece).start()

    def gather_3(name, base, view, half):
        for o in (1, 2):
            came(name, base + 1 + o, HEAD_AXIS, 3 - o, half(square[3], o - 1))
            sent(name, base + o - 1, HEAD_AXIS, o, view(head))
            sent(name, base + 1 + o, HEAD_AXIS, 3 - o, half(square[o], o - 1))

    def scatter_1(name, base, block, inbox):
        for o in (1, 2):
            link(name, base + 2 * o - 2, HEAD_AXIS, o, block(square[o], o - 1), inbox.at[base + 2 * o - 2]).start()
            link(name, base + 2 * o - 1, HEAD_AXIS, o, block(square[3], o - 1), inbox.at[base + 2 * o - 1]).start()

    def scatter_2(name, base, block, inbox):
        for o in (1, 2):
            index = base + 2 * o - 1
            came(name, index, HEAD_AXIS, o, inbox.at[index])
            mine = block(square[3 - o], o - 1)
            mine[...] = (mine[...].astype(F32) + inbox[index].astype(F32)).astype(BF16)
            link(name, base + 3 + o, HEAD_AXIS, 3 - o, mine, inbox.at[base + 3 + o]).start()

    def scatter_3(name, base, block, inbox):
        totals = []
        for o in (1, 2):
            total = block(head, o - 1)[...].astype(F32)
            for index, by in ((base + 2 * o - 2, o), (base + 3 + o, 3 - o)):
                came(name, index, HEAD_AXIS, by, inbox.at[index])
                total = total + inbox[index].astype(F32)
            totals.append(total)
        return totals

    def scatter_sent(name, base, block):
        for o in (1, 2):
            sent(name, base + 2 * o - 2, HEAD_AXIS, o, block(square[o], o - 1))
            sent(name, base + 2 * o - 1, HEAD_AXIS, o, block(square[3], o - 1))
            sent(name, base + 3 + o, HEAD_AXIS, 3 - o, block(square[3 - o], o - 1))

    def cot_of(h):
        return r.cot_all.at[:, pl.ds(pl.multiple_of(h * part, part), part)]

    def cot_half(h, i):
        return r.cot_all.at[pl.ds(i * (tokens // 2), tokens // 2), pl.ds(pl.multiple_of(h * part, part), part)]

    moves = ((r.x_hbm, r.x), (r.wv_hbm, r.wv), (r.wbc_hbm, r.wbc), (r.cot, cot_of(head)), (r.wg_hbm, r.wg), (r.wo_hbm, r.wo))
    loads = [pltpu.make_async_copy(*move, r.load.at[i]) for i, move in enumerate(moves)]
    for load in loads:
        load.start()
    row, col = iota((BLOCK, BLOCK), 0), iota((BLOCK, BLOCK), 1)
    r.upper[...] = (row <= col).astype(BF16)
    r.eye[...] = (row == col).astype(BF16)
    dim = inner // heads
    r.spread[...] = (iota((heads, inner), 1) // dim == iota((heads, inner), 0)).astype(BF16)
    r.collect[...] = (iota((inner, heads), 0) // dim == iota((inner, heads), 1)).astype(BF16)
    for sel, lane in ((r.sel_step, STEP), (r.sel_end, TO_END), (r.sel_into, INTO)):
        sel[...] = (iota((256, inner), 1) // dim + lane == lax.rem(iota((256, inner), 0), 128)).astype(BF16)
    r.tok[...] = jnp.zeros_like(r.tok)
    r.doc_out[...] = jnp.broadcast_to(r.docs[0:1, tokens - 1 : tokens].astype(F32), r.doc_out.shape)
    barrier = pltpu.get_barrier_semaphore()
    for axis in (HEAD_AXIS, SEQ_AXIS, DP_AXIS):
        for o in range(1, count[axis]):
            pl.semaphore_signal(barrier, inc=1, device_id={axis: other(axis, o)}, device_id_type=MESH)
    for load in loads[:3]:
        load.wait()
    gain, out_gain = r.gain[...], r.og[...]

    def project(c):
        rows = at(c)
        normed = in_norm(r.x[rows, :].astype(F32), gain)
        r.normed[rows, :] = normed
        inside = pl.ds(pl.multiple_of(c * BLOCK + EDGE, EDGE), BLOCK)
        r.cin[inside, :inner] = dot(normed, r.wv[...])
        r.cin[inside, inner:] = dot(normed, r.wbc[...])
        r.tok[rows, 0:heads] = dot(normed, r.ws[...], NT) + r.dtb[...]

    repeat(EARLY, project)
    pl.semaphore_wait(barrier, nh + ns + 2 - 3)
    loads[3].wait()
    gather_1(COT, 0, cot_of)
    x_tail = r.x.at[pl.ds(tokens - TAIL, TAIL)]
    link(HALO, 0, SEQ_AXIS, 1, x_tail, r.halo_x).start()
    link(HALO, 1, SEQ_AXIS, 1, r.doc_out, r.doc_in).start()
    repeat(blocks - EARLY, lambda i: project(EARLY + i))

    taps = jnp.concatenate([r.cv[...], r.cb[...]], axis=1)
    rate = -jnp.exp(r.alog[...])
    same = iota((heads, heads), 0) == iota((heads, heads), 1)
    rate_col = jnp.sum(jnp.where(same, rate, 0.0), axis=1, keepdims=True)
    skip = dot_left(r.dskip[...], r.spread[...])
    def conv_pre(window, taps):
        pre = taps[n_taps : n_taps + 1, :] + taps[0:1, :] * window[EDGE:]
        for k in range(1, n_taps):
            pre = pre + taps[k : k + 1, :] * window[EDGE - k : EDGE - k + BLOCK]
        return pre

    def doc_row(c):
        return r.docs[0:1, at(c)].astype(F32)

    def expand_tok(marks, sel, cols=slice(None)):
        return dot(marks, sel[:, cols])

    came(HALO, 0, SEQ_AXIS, -1, r.halo_x)
    came(HALO, 1, SEQ_AXIS, -1, r.doc_in)
    opened = jnp.where(seq == 0, 0.0, 1.0)
    edge = in_norm(r.halo_x[...].astype(F32), gain)
    r.cin[0:EDGE, :inner] = dot(edge, r.wv[...])[TAIL - EDGE :] * opened
    r.cin[0:EDGE, inner:] = dot(edge, r.wbc[...])[TAIL - EDGE :] * opened
    r.doc_prev[...] = jnp.where(seq == 0, -1.0, r.doc_in[...])

    r.carry[...] = jnp.ones_like(r.carry)

    def steps(c):
        rows = at(c)
        around = pl.ds(pl.multiple_of(c * BLOCK, BLOCK), BLOCK + EDGE)
        pre = conv_pre(r.cin[around, inner:], taps[:, inner:])
        u = pre * sigmoid(pre)
        r.b[rows, :] = u[:, :state].astype(BF16)
        r.c[rows, :] = u[:, state:]
        docs = doc_row(c)
        prev = r.doc_prev[0:1, 0:1]
        before = jnp.concatenate([prev, docs[:, : BLOCK - 1]], axis=1)
        ends = docs[:, BLOCK - 1 :]
        marks = [docs, (docs == prev).astype(F32), (docs == before).astype(F32), (docs == ends).astype(F32)]
        vt = r.tok[rows, :].T[0:heads]
        step = softplus(vt)
        la_hi, la_lo = halves(rate_col * step)
        cum = dot(la_hi, r.upper[...]) + dot(la_lo, r.upper[...])
        r.cumt[:, at(c)] = cum
        total = cum[:, BLOCK - 1 :]
        columns = [vt, cum, *marks, jnp.zeros((12, BLOCK), F32), step, jnp.exp(total - cum) * marks[3]]
        columns += [jnp.exp(cum) * marks[1], jnp.zeros((72, BLOCK), F32)]
        r.tok[rows, :] = jnp.concatenate(columns, axis=0).T
        held = jnp.exp(total) * (ends == prev).astype(F32)
        kept = jnp.sum(r.spread[...].astype(F32) * held, axis=0, keepdims=True)
        r.kept[c] = kept
        r.carry[...] = r.carry[...] * kept
        r.doc_prev[...] = jnp.broadcast_to(ends, r.doc_prev.shape)

    repeat(blocks, steps)

    pairs = heads // 2
    for pair in range(pairs):
        r.carry_part[pair] = r.carry[:, pair * lanes : (pair + 1) * lanes]
    r.own[...] = jnp.zeros_like(r.own)

    def relay(turn):
        pair = turn - 2 * seq

        @pl.when(jnp.logical_and(pair >= 0, pair < pairs))
        def _():
            @pl.when(seq > 0)
            def _():
                came(ENDS, pair, SEQ_AXIS, -1, r.end_in.at[pair])

            into = jnp.where(seq > 0, r.end_in[pair], 0.0)
            r.end_out[pair] = r.carry_part[pair] * into + r.own[pair]
            r.own[pair] = into

            @pl.when(seq < ns - 1)
            def _():
                link(ENDS, pair, SEQ_AXIS, 1, r.end_out.at[pair], r.end_in.at[pair]).start()

    for pair in range(pairs):
        cols = slice(pair * lanes, (pair + 1) * lanes)

        def own_states(c, pair=pair, cols=cols):
            rows = at(c)
            around = pl.ds(pl.multiple_of(c * BLOCK, BLOCK), BLOCK + EDGE)
            pre = conv_pre(r.cin[around, cols], taps[:, cols])
            xh = pre * sigmoid(pre)
            marks = both(r.tok[rows, :])
            xs = xh * expand_tok(marks, r.sel_step, cols)
            r.xs[rows, cols] = xs.astype(BF16)
            r.y[rows, cols] = skip[:, cols] * xh
            inc = dot(r.b[rows, :], (xs * expand_tok(marks, r.sel_end, cols)).astype(BF16), TN)
            r.inc[c, :, cols] = inc
            r.own[pair] = r.kept[c, :, cols] * r.own[pair] + inc

        repeat(blocks // 2, lambda i, body=own_states: (body(2 * i), body(2 * i + 1)))
        relay(pair)

    gather_2(COT, 0, cot_of, cot_half)

    def relay_back(turn):
        distance = ns - 1 - seq
        for i in range(2):
            pair = 2 * (turn - 2 * distance) + i

            @pl.when(jnp.logical_and(distance > 0, jnp.logical_and(pair >= 0, pair < pairs)))
            def _(pair=pair):
                came(BACK, pair, SEQ_AXIS, 1, r.back_in.at[pair])
                into = r.back_in[pair].astype(F32)
                r.back_out[pair] = (r.carry_part[pair] * into + r.own[pair]).astype(BF16)
                r.own[pair] = into

                @pl.when(seq > 0)
                def _():
                    link(BACK, pair, SEQ_AXIS, -1, r.back_out.at[pair], r.back_in.at[pair]).start()

    first = iota((BLOCK, lanes), 1) < lanes // 2

    def split(pair):
        zero = jnp.zeros_like(pair)
        return jnp.where(first, pair, zero), jnp.where(first, zero, pair)

    def intra(c):
        rows = at(c)
        cum, cumt = r.tok[rows, CUM : CUM + heads], r.cumt[:, at(c)]
        mask = jnp.where((row >= col) & (r.tok[rows, AUX : AUX + 1] == doc_row(c)), 0.0, NEG)
        scores = score_pair(r.c[rows, :], r.b[rows, :], True)
        for pair in range(heads // 2):
            cols = slice(pair * lanes, (pair + 1) * lanes)
            mixed = []
            for h in (2 * pair, 2 * pair + 1):
                decay = jnp.exp(cum[:, h : h + 1] - cumt[h : h + 1, :] + mask)
                mixed.append((scores * decay).astype(BF16))
            two = jnp.concatenate(split(r.xs[rows, cols]), axis=0)
            r.y[rows, cols] += dot(jnp.concatenate(mixed, axis=1), two)
        r.z[rows, :] = dot(r.normed[rows, :], r.wg[...])
        relay(pairs + c)

    loads[4].wait()
    repeat(blocks, intra)
    loads[5].wait()

    if 2 * (ns - 1) > blocks:
        repeat(2 * (ns - 1) - blocks, lambda i: relay(pairs + blocks + i))
    for pair in range(pairs):
        r.end[:, pair * lanes : (pair + 1) * lanes] = r.own[pair]
    gather_3(COT, 0, cot_of, cot_half)

    def dgn_of(rows):
        return dot(r.cot_all[rows, :], r.wo[...], NT)

    lane8 = iota((BLOCK, 8), 1)

    def sums(c):
        rows = at(c)
        si = r.end[...]
        r.end[...] = r.kept[c] * si + r.inc[c]
        r.inc[c] = si
        into = expand_tok(both(r.tok[rows, :]), r.sel_into)
        y = r.y[rows, :] + into * dot3(r.c[rows, :], si)
        r.y[rows, :] = y
        z = r.z[rows, :]
        g = y * (z * sigmoid(z))
        squares = jnp.sum(g * g, axis=1, keepdims=True)
        products = jnp.sum(dgn_of(rows) * out_gain * g, axis=1, keepdims=True)
        cols_hi, cols_lo = halves(jnp.where(lane8 == 0, squares, jnp.where(lane8 == 1, products, 0.0)))
        r.sum_out[c] = dot(cols_hi, r.eye[...], TN) + dot(cols_lo, r.eye[...], TN)
        for o in range(1, nh):
            index = c * (nh - 1) + o - 1
            link(SUM, index, HEAD_AXIS, o, r.sum_out.at[c], r.sum_in.at[index]).start()
        r.parts[c] = dot((g * out_gain).astype(BF16), r.wo[...]).astype(BF16)

    def out_block(c):
        half = BLOCK // 2
        return lambda h, i: r.parts.at[c, pl.ds(i * half, half), pl.ds(pl.multiple_of(h * part, part), part)]

    repeat(blocks // 2, lambda i: (sums(2 * i), sums(2 * i + 1)))
    r.inc[blocks] = r.end[...]

    r.end[...] = jnp.zeros_like(r.end)
    r.prod[...] = jnp.ones_like(r.prod)
    r.pack[...] = jnp.zeros_like(r.pack)
    r.g_gain[...] = jnp.zeros_like(r.g_gain)

    def gate(c):
        rows = at(c)
        total = r.sum_out[c]
        for o in range(1, nh):
            index = c * (nh - 1) + o - 1
            came(SUM, index, HEAD_AXIS, -o, r.sum_in.at[index])
            total = total + r.sum_in[index]
        scatter_1(OUT, 6 * c, out_block(c), r.out_in)
        shares = dot_right(r.eye[...], total, NT)
        y, z = r.y[rows, :], r.z[rows, :]
        dgn = dgn_of(rows)
        sig = sigmoid(z)
        act = z * sig
        g = y * act
        rms = lax.rsqrt(shares[:, 0:1] / inner_all + EPS)
        r.tok[rows, RMS : RMS + 1] = rms
        gr = g * rms
        r.xs[rows, :] = (gr * out_gain).astype(BF16)
        r.g_gain[...] += jnp.sum(dgn * gr, axis=0, keepdims=True)
        dg = rms * (dgn * out_gain) - g * (rms * rms * rms * shares[:, 1:2] / inner_all)
        dy = dg * act
        dyb = dy.astype(BF16)
        r.dy[rows, :] = dyb
        r.dz[rows, :] = (dg * y * (sig * (1.0 + z * (1.0 - sig)))).astype(BF16)
        into = expand_tok(both(r.tok[rows, :]), r.sel_into)
        part_state = dot(r.c[rows, :].astype(BF16), (dy * into).astype(BF16), TN)
        r.adj[c] = part_state.astype(BF16)
        r.end[...] += r.prod[...] * part_state
        r.prod[...] = r.prod[...] * r.kept[c]

    repeat(blocks // 2, lambda i: (gate(2 * i), gate(2 * i + 1)))

    for pair in range(pairs):
        r.own[pair] = r.end[:, pair * lanes : (pair + 1) * lanes]

    @pl.when(seq == ns - 1)
    def _():
        for pair in range(pairs):
            r.back_out[pair] = r.own[pair].astype(BF16)
            link(BACK, pair, SEQ_AXIS, -1, r.back_out.at[pair], r.back_in.at[pair]).start()
        r.own[...] = jnp.zeros_like(r.own)

    r.gw_out[...] = jnp.zeros_like(r.gw_out)
    r.gw_gate[...] = jnp.zeros_like(r.gw_gate)

    def weight_grads(i):
        rows = pl.ds(pl.multiple_of(i * 2 * BLOCK, 2 * BLOCK), 2 * BLOCK)
        r.gw_out[...] += dot(r.xs[rows, :], r.cot_all[rows, :], TN)
        relay_back(2 * i)
        r.gw_gate[...] += dot(r.normed[rows, :], r.dz[rows, :], TN)
        r.tok[rows, DYY : DYY + heads] = dot_left(r.dy[rows, :].astype(F32) * r.y[rows, :], r.collect[...])
        relay_back(2 * i + 1)

    repeat(blocks // 2, weight_grads)

    def add_residual(c):
        cols = pl.ds(pl.multiple_of(head * part, part), part)
        half = BLOCK // 2
        for i, total in enumerate(scatter_3(OUT, 6 * c, out_block(c), r.out_in)):
            rows = pl.ds(pl.multiple_of(c * BLOCK + i * half, half), half)
            scaled = r.tok[rows, RMS : RMS + 1] * total
            r.block_out[rows, :] = (scaled + r.x[rows, cols].astype(F32)).astype(BF16)

    def ref(name, kind):
        return getattr(r, name + kind)

    def half_of(name, source, core):
        if name == WO:
            half = source.shape[1] // 2
            return source.at[:, pl.ds(pl.multiple_of(core * half, half), half)]
        half = source.shape[0] // 2
        return source.at[pl.ds(pl.multiple_of(core * half, half), half)]

    near = seq < ns // 2
    depth, last = jnp.where(near, seq, ns - 1 - seq), ns // 2 - 1
    inward = jnp.where(near, 1, -1)

    def piece_of(name, half, j):
        rows = half.shape[0] // PIECES[name]
        return half.at[pl.ds(j * rows, rows)]

    def result(name, core, j):
        whole = ref(name, "_sum")
        return piece_of(name, whole if name == WQ else half_of(name, whole, core), j)

    def total_a(name, source):
        return link(name + "a", 0, DP_AXIS, 1, half_of(name, source, 1 - dp), ref(name, "_pair"))

    def total_b(name, source):
        total_a(name, source).wait_send()
        came(name + "a", 0, DP_AXIS, 1, ref(name, "_pair"))
        mine = ref(name, "_mine")
        mine[...] = (half_of(name, source, dp)[...] + ref(name, "_pair")[...]).astype(mine.dtype)

        start_inward(name)

    def start_inward(name):
        mine = ref(name, "_mine")

        @pl.when(depth == 0)
        def _():
            for j in range(PIECES[name]):
                link(name + "b", j, SEQ_AXIS, inward, piece_of(name, mine, j), ref(name, "_in").at[j]).start()

    def total_c(name, pieces=None):
        @pl.when(depth > 0)
        def _():
            for j in pieces or range(PIECES[name]):
                came(name + "b", j, SEQ_AXIS, -inward, ref(name, "_in").at[j])
                mine = piece_of(name, ref(name, "_mine"), j)
                mine[...] = (mine[...].astype(F32) + ref(name, "_in")[j].astype(F32)).astype(mine.dtype)

                @pl.when(depth < last)
                def _():
                    link(name + "b", j, SEQ_AXIS, inward, mine, ref(name, "_in").at[j]).start()

                @pl.when(depth == last)
                def _():
                    link(name + "c", j, SEQ_AXIS, inward, mine, result(name, dp, j)).start()

    def total_d(name, middle, pieces=None):
        for j in pieces or range(PIECES[name]):
            total = result(name, dp, j)

            @pl.when(depth == last if middle else depth < last)
            def _():
                if middle:
                    came(name + "c", j, SEQ_AXIS, inward, total)
                    mine = piece_of(name, ref(name, "_mine"), j)
                    total[...] = (mine[...].astype(F32) + total[...].astype(F32)).astype(mine.dtype)
                else:
                    came(name + "f", j, SEQ_AXIS, inward, total)

                @pl.when(depth > 0)
                def _():
                    link(name + "f", j, SEQ_AXIS, -inward, total, total).start()

                if name != WQ:
                    link(name + "d", j, DP_AXIS, 1, total, total).start()

    def total_e(name):
        for j in range(PIECES[name]):
            total, mine = result(name, dp, j), piece_of(name, ref(name, "_mine"), j)
            if name != WQ:
                came(name + "d", j, DP_AXIS, 1, result(name, 1 - dp, j))
                sent(name + "d", j, DP_AXIS, 1, total)

            @pl.when(depth < last)
            def _():
                sent(name + "b", j, SEQ_AXIS, inward, mine)

            @pl.when(depth == last)
            def _():
                sent(name + "c", j, SEQ_AXIS, inward, mine)

            @pl.when(depth > 0)
            def _():
                sent(name + "f", j, SEQ_AXIS, -inward, total)

    total_a(WO, r.gw_out).start()
    total_a(WG, r.gw_gate).start()

    if 2 * (ns - 1) + pairs // 2 > blocks:
        repeat(2 * (ns - 1) + pairs // 2 - blocks, lambda i: relay_back(blocks + i))
    for pair in range(pairs):
        r.end[:, pair * lanes : (pair + 1) * lanes] = r.own[pair]

    def chain(i):
        c = blocks - 1 - i
        here = r.end[...]
        r.end[...] = r.kept[c] * here + r.adj[c].astype(F32)
        r.adj[c] = here.astype(BF16)

    repeat(blocks, chain)
    repeat(blocks, lambda c: scatter_2(OUT, 6 * c, out_block(c), r.out_in))
    r.tail[...] = r.cin[0:EDGE, :]
    r.g_dt[...] = jnp.zeros_like(r.g_dt)
    r.g_log[...] = jnp.zeros_like(r.g_log)
    r.g_skip[...] = jnp.zeros_like(r.g_skip)
    r.g_conv[...] = jnp.zeros_like(r.g_conv)
    r.gw_bc[...] = jnp.zeros_like(r.gw_bc)
    r.g_norm[...] = jnp.zeros_like(r.g_norm)

    def back(c):
        rows = at(c)
        inside = pl.ds(pl.multiple_of(c * BLOCK + EDGE, EDGE), BLOCK)
        b_mat, c_full = r.b[rows, :], r.c[rows, :]
        c_mat = c_full.astype(BF16)
        v = r.tok[rows, 0:heads]
        step = r.tok[rows, STEP : STEP + heads]
        cum, cumt, aux = r.tok[rows, CUM : CUM + heads], r.cumt[:, at(c)], r.tok[rows, AUX : AUX + 8]
        mask = jnp.where((row <= col) & (aux[:, 0:1] == doc_row(c)), 0.0, NEG)
        scores = score_pair(c_full, b_mat, False)
        marks = both(r.tok[rows, :])
        d_scores = jnp.zeros((BLOCK, BLOCK), F32)
        d_b = jnp.zeros((BLOCK, state), F32)
        d_c = jnp.zeros((BLOCK, state), F32)
        d_step_own = jnp.zeros((BLOCK, heads), F32)
        d_cum = r.tok[rows, DYY : DYY + heads]
        through = jnp.zeros((1, heads), F32)

        def conv_grad(d_u, window, pre, sig, cols):
            d_pre = d_u * (sig * (1.0 + pre * (1.0 - sig)))
            for k in range(n_taps):
                shifted = window[EDGE - k : EDGE - k + BLOCK]
                r.g_conv[k : k + 1, cols] += jnp.sum(d_pre * shifted, axis=0, keepdims=True)
            r.g_conv[n_taps : n_taps + 1, cols] += jnp.sum(d_pre, axis=0, keepdims=True)
            r.tail[:, cols] = window[BLOCK:]
            r.cin[inside, cols] = d_pre

        def window_of(cols):
            return jnp.concatenate([r.tail[:, cols], r.cin[inside, cols]], axis=0)

        for pair in range(heads // 2):
            cols = slice(pair * lanes, (pair + 1) * lanes)
            window = window_of(cols)
            pre = conv_pre(window, taps[:, cols])
            sig = sigmoid(pre)
            xh = pre * sig
            step_e, to_end_e, into_e = (expand_tok(marks, sel, cols) for sel in (r.sel_step, r.sel_end, r.sel_into))
            xs = xh * step_e
            xsb = xs.astype(BF16)
            dyb = r.dy[rows, cols]
            dy = dyb.astype(F32)
            adjb = r.adj[c, :, cols]
            adj = adjb.astype(F32)
            dye = dy * into_e
            d_c = d_c + dot3(dye, r.inc[c, :, cols], NT)
            d_b = d_b + dot(both(xs * to_end_e), jnp.concatenate([adjb, adjb], axis=1), NT)
            d_xs_inter = to_end_e * dot(b_mat, adjb)
            two = split(dyb)
            mixed = []
            for i, h in enumerate((2 * pair, 2 * pair + 1)):
                decay = jnp.exp(cumt[h : h + 1, :] - cum[:, h : h + 1] + mask)
                mixed.append((scores * decay).astype(BF16))
                d_scores = d_scores + dot(xsb, two[i], NT) * decay
            d_xs_intra = dot(jnp.concatenate(mixed, axis=1), jnp.concatenate(two, axis=0))
            d_xs = d_xs_intra + d_xs_inter
            collect = jnp.concatenate([r.collect[cols, :]] * 2, axis=0)
            d_step_own = d_step_own + dot(both(xh * d_xs), collect)
            lost = skip[:, cols] * (dy * xh) + (xsb.astype(F32) * d_xs_intra + xs * d_xs_inter)
            d_cum = d_cum - dot(both(lost), collect)
            ended = jnp.sum(adj * r.inc[c + 1, :, cols], axis=0, keepdims=True)
            through = through + dot(both(ended), collect)
            r.g_skip[:, cols] += jnp.sum(dy * xh, axis=0, keepdims=True)
            conv_grad(skip[:, cols] * dy + step_e * d_xs, window, pre, sig, cols)
        d_sb = d_scores.astype(BF16)
        d_b = d_b + dot(d_sb, c_mat)
        d_c = d_c + dot(d_sb, b_mat, TN)
        cols = slice(inner, channels)
        window = window_of(cols)
        pre = conv_pre(window, taps[:, cols])
        conv_grad(jnp.concatenate([d_b, d_c], axis=1), window, pre, sigmoid(pre), cols)
        d_la = (dot_right(r.upper[...], d_cum) + through) * aux[:, 2:3]
        r.g_log[...] += jnp.sum(rate * step * d_la, axis=0, keepdims=True)
        d_v = (d_step_own + rate * d_la) * sigmoid(v)
        r.g_dt[...] += jnp.sum(d_v, axis=0, keepdims=True)
        r.dstep[rows, :] = d_v.astype(BF16)

    def project_back(c):
        rows = at(c)
        window = r.cin[pl.ds(pl.multiple_of(c * BLOCK + EDGE, EDGE), BLOCK + EDGE), :]
        d_in = taps[0:1, :] * window[:BLOCK]
        for k in range(1, n_taps):
            d_in = d_in + taps[k : k + 1, :] * window[k : k + BLOCK]
        d_inb = d_in.astype(BF16)
        d_val = d_inb[:, :inner]
        dstep = r.dstep[rows, :]
        normed = r.normed[rows, :]
        grads = dot(normed, d_inb, TN)
        r.gw_value[...] += grads[:, :inner]
        r.gw_bc[...] += grads[:, inner:]
        r.pack[0:heads, :] += dot(dstep, normed, TN)
        d_part = dot(r.dz[rows, :], r.wg[...], NT) + dot(d_val, r.wv[...], NT)
        d_part = d_part + dot(d_inb[:, inner:], r.wbc[...], NT) + dot(dstep, r.ws[...])
        scatter_sent(OUT, 6 * c, out_block(c))
        r.parts[c] = d_part.astype(BF16)
        scatter_1(PART, 6 * c, part_block(c), r.part_in)

    def part_block(c):
        half = slab // 2
        return lambda h, i: r.parts.at[c, pl.ds(pl.multiple_of(h * slab + i * half, half), half)]

    def combine(c):
        scatter_2(PART, 6 * c, part_block(c), r.part_in)

    def slab_of(c):
        return lambda h: r.normed.at[pl.ds(pl.multiple_of(c * BLOCK + h * slab, slab), slab)]

    def slab_half(c):
        half = slab // 2
        return lambda h, i: r.normed.at[pl.ds(pl.multiple_of(c * BLOCK + h * slab + i * half, half), half)]

    def forward(c):
        gather_2(GRAD, 4 * c, slab_of(c), slab_half(c))

    def own_slab(c):
        return pl.ds(pl.multiple_of(c * BLOCK + head * slab, slab), slab)

    def finish(c):
        rows = own_slab(c)
        total = jnp.concatenate(scatter_3(PART, 6 * c, part_block(c), r.part_in), axis=0)
        x = r.x[rows, :].astype(F32)
        norm = lax.rsqrt(jnp.mean(x * x, axis=1, keepdims=True) + EPS)
        xr = x * norm
        d_normed = total
        r.g_norm[...] += jnp.sum(d_normed * xr, axis=0, keepdims=True)
        q = d_normed * gain
        d_x = norm * q - xr * (norm * norm * jnp.mean(q * x, axis=1, keepdims=True))
        r.normed[rows, :] = (d_x + r.cot_all[rows, :].astype(F32)).astype(BF16)
        gather_1(GRAD, 4 * c, slab_of(c))

    first_rows = r.cin.at[pl.ds(EDGE, EDGE)]
    last_rows = r.cin.at[pl.ds(EDGE + tokens, EDGE)]

    def reverse(c):
        back(c)

        @pl.when(c == 0)
        def _():
            link(EDGES, 0, SEQ_AXIS, -1, first_rows, last_rows).start()
            total_b(WO, r.gw_out)
            total_b(WG, r.gw_gate)
            r.gw_value[...] = jnp.zeros_like(r.gw_value)

        add_residual(c)

        @pl.when(c >= 1)
        def _():
            project_back(c - 1)

        @pl.when(c >= 2)
        def _():
            combine(c - 2)

        @pl.when(c == 2)
        def _():
            total_c(WO)

        @pl.when(c >= LAG)
        def _():
            finish(c - LAG)

        @pl.when(c >= LAG + 2)
        def _():
            forward(c - LAG - 2)

        @pl.when(c == 4)
        def _():
            total_c(WG)
            total_d(WO, True)

    repeat(blocks, reverse)

    unfinished, unsent = [*range(blocks - LAG, blocks)], [*range(max(blocks - LAG - 2, 0), blocks)]
    came(EDGES, 0, SEQ_AXIS, 1, last_rows)

    @pl.when(seq == ns - 1)
    def _():
        r.cin[EDGE + tokens :, :] = jnp.zeros((EDGE, channels), F32)

    project_back(blocks - 1)
    total_a(WV, r.gw_value).start()

    half_rows = width // 2
    quarter = half_rows // nh

    def bc_rows(whole, core, h):
        return whole.at[pl.ds(pl.multiple_of(core * half_rows + h * quarter, quarter), quarter)]

    def half_bc(core):
        return r.gw_bc.at[pl.ds(pl.multiple_of(core * half_rows, half_rows), half_rows)]

    link(BC, nh - 1, DP_AXIS, 1, half_bc(1 - dp), r.bc_pair).start()
    r.pack[9 : 9 + n_taps + 1, :channels] = r.g_conv[: n_taps + 1, :]
    r.pack[14:15, :inner] = r.g_gain[...]
    r.pack[15:16, 0:heads] = r.g_dt[...]
    r.pack[15:16, 128 : 128 + heads] = r.g_log[...]
    r.pack[15:16, 256 : 256 + heads] = dot_left(r.g_skip[...], r.collect[...])
    r.pack_out[...] = r.pack[8:16, :]
    for o in range(1, nh):
        link(PACK1, o - 1, HEAD_AXIS, o, r.pack_out, r.pack1_in.at[o - 1]).start()
    total_d(WG, True)
    total_b(WV, r.gw_value)
    came(BC, nh - 1, DP_AXIS, 1, r.bc_pair)
    r.bc_out[...] = (half_bc(dp)[...] + r.bc_pair[...]).astype(BF16)
    for o in range(1, nh):
        link(BC, o - 1, HEAD_AXIS, o, bc_rows(r.bc_out, 0, square[o]), r.bc_in[o - 1]).start()
    combine(blocks - 2)
    forward(unsent[0])
    finish(unfinished[0])
    total_c(WV, (0, 1))
    for o in range(1, nh):
        came(PACK1, o - 1, HEAD_AXIS, -o, r.pack1_in.at[o - 1])
        r.pack[9 : 9 + n_taps + 1, inner:channels] += r.pack1_in[o - 1, 1 : 2 + n_taps, inner:channels]
    total_a(WP, r.pack).start()
    combine(blocks - 1)
    total_c(WV, (2, 3))
    total_d(WV, True, (0, 1))
    for c in unfinished[1:-1]:
        finish(c)
    forward(unsent[1])
    total_c(WV, (4, 5))
    total_d(WV, True, (2, 3))
    mine = bc_rows(r.bc_out, 0, head)[...].astype(F32)
    for o in range(1, nh):
        came(BC, o - 1, HEAD_AXIS, -o, r.bc_in[o - 1])
        mine = mine + r.bc_in[o - 1][...].astype(F32)
    r.wq_mine[...] = mine.astype(BF16)
    start_inward(WQ)
    total_b(WP, r.pack)
    total_c(WV, (6, 7))
    total_d(WV, True, (4, 5))
    total_d(WO, False)
    total_d(WG, False)
    finish(blocks - 1)
    for o in range(1, nh):
        link(NORM, o - 1, HEAD_AXIS, o, r.g_norm, r.norm_in.at[o - 1]).start()
    total_d(WV, True, (6, 7))
    total_c(WP)
    total_c(WQ)
    for c in unsent[2:-1]:
        forward(c)
    total_d(WP, True)
    total_d(WQ, True)
    total_d(WV, False)
    total = r.g_norm[...]
    for o in range(1, nh):
        came(NORM, o - 1, HEAD_AXIS, -o, r.norm_in.at[o - 1])
        total = total + r.norm_in[o - 1]
    r.norm_out[0] = total
    link(NORM, nh - 1, DP_AXIS, 1, r.norm_out.at[0], r.norm_in.at[nh - 1]).start()
    forward(blocks - 1)
    total_d(WP, False)
    total_d(WQ, False)
    total_e(WQ)
    mine = bc_rows(r.bc_sum, dp, head)
    mine[...] = r.wq_sum[...]
    for o in range(1, nh):
        link(BCG, o - 1, HEAD_AXIS, o, mine, mine).start()
    link(BCG, nh - 1, DP_AXIS, 1, mine, mine).start()
    came(NORM, nh - 1, DP_AXIS, 1, r.norm_in.at[nh - 1])
    total = r.norm_out[0] + r.norm_in[nh - 1]
    r.norm_out[1] = total
    for o in range(1, ns):
        link(NORM, nh + o - 1, SEQ_AXIS, o, r.norm_out.at[1], r.norm_in.at[nh + o - 1]).start()
    for name in (WO, WG, WV, WP):
        total_e(name)

    r.norm_all[seq] = total
    for o in range(1, ns):
        came(NORM, nh + o - 1, SEQ_AXIS, -o, r.norm_in.at[nh + o - 1])
        r.norm_all[other(SEQ_AXIS, -o)] = r.norm_in[nh + o - 1]
    total = r.norm_all[0]
    for k in range(1, ns):
        total = total + r.norm_all[k]
    r.norm_sum[...] = total
    for o in range(1, nh):
        theirs = bc_rows(r.bc_sum, dp, square[o])
        came(BCG, o - 1, HEAD_AXIS, -o, theirs)
        link(BCG, nh - 1 + o, DP_AXIS, 1, theirs, theirs).start()
        sent(BCG, o - 1, HEAD_AXIS, o, mine)
        sent(BC, o - 1, HEAD_AXIS, o, bc_rows(r.bc_out, 0, square[o]))
        sent(PACK1, o - 1, HEAD_AXIS, o, r.pack_out)
        sent(NORM, o - 1, HEAD_AXIS, o, r.g_norm)
    for o in range(nh):
        came(BCG, nh - 1 + o, DP_AXIS, 1, bc_rows(r.bc_sum, 1 - dp, square[o]))
        sent(BCG, nh - 1 + o, DP_AXIS, 1, bc_rows(r.bc_sum, dp, square[o]))
    sent(BC, nh - 1, DP_AXIS, 1, half_bc(1 - dp))
    sent(NORM, nh - 1, DP_AXIS, 1, r.norm_out.at[0])
    for o in range(1, ns):
        sent(NORM, nh + o - 1, SEQ_AXIS, o, r.norm_out.at[1])
    sent(HALO, 0, SEQ_AXIS, 1, x_tail)
    sent(HALO, 1, SEQ_AXIS, 1, r.doc_out)
    sent(EDGES, 0, SEQ_AXIS, -1, first_rows)

    @pl.when(seq > 0)
    def _():
        for pair in range(pairs):
            sent(BACK, pair, SEQ_AXIS, -1, r.back_out.at[pair])

    @pl.when(seq < ns - 1)
    def _():
        for pair in range(pairs):
            sent(ENDS, pair, SEQ_AXIS, 1, r.end_out.at[pair])

    def drain(c):
        for o in range(1, nh):
            sent(SUM, c * (nh - 1) + o - 1, HEAD_AXIS, o, r.sum_out.at[c])
        scatter_sent(PART, 6 * c, part_block(c))
        gather_3(GRAD, 4 * c, slab_of(c), slab_half(c))
        store(c).start()

    def store(c):
        return pltpu.make_async_copy(r.normed.at[at(c)], r.grad_in.at[at(c)], r.stored.at[c])

    repeat(blocks, drain)
    repeat(blocks, lambda c: store(c).wait())


def write_kernel(n, *refs):
    small, norm_sum = refs[n : n + 2]
    for source, target in zip(refs[:n], refs[n + 2 :]):
        target[...] = source[...].astype(target.dtype)
    norm, step, conv_v, conv_b, dt, log, skip, gain = refs[2 * n + 2 :]
    inner, heads, taps = conv_v.shape[1], dt.shape[1], conv_v.shape[0]

    @pl.when(pl.program_id(0) == 0)
    def _():
        norm[...] = norm_sum[...]
        step[...] = small[0:heads, :]
        conv_v[...] = small[9 : 9 + taps, :inner]
        conv_b[...] = small[9 : 9 + taps, inner : inner + conv_b.shape[1]]
        dt[...] = small[15:16, 0:heads]
        log[...] = small[15:16, 128 : 128 + heads]
        skip[...] = small[15:16, 256 : 256 + heads]
        gain[...] = small[14:15, :inner]


def on_device(
    hidden_in, doc_ids, norm_gain, w_gate, w_value, w_bc, w_step, conv_value, conv_bc, dt_bias, a_log, d_skip,
    out_gain, w_out, cotangent,
):
    x, cot = hidden_in[0], cotangent[0]
    tokens, width = x.shape
    inner, heads = w_gate.shape[1], w_step.shape[1]
    bc_width, head_dim = w_bc.shape[1], inner // heads
    state = bc_width // 2
    channels = inner + bc_width
    blocks = tokens // BLOCK
    nh, ns = lax.axis_size(HEAD_AXIS), lax.axis_size(SEQ_AXIS)
    part, slab = width // nh, BLOCK // nh
    n_taps = conv_value.shape[0] - 1
    vmem, hbm = pltpu.VMEM, pl.ANY
    inputs = dict(
        x_hbm=x, cot=cot, docs=doc_ids, gain=norm_gain[None], wg_hbm=w_gate, wv_hbm=w_value, wbc_hbm=w_bc,
        ws=w_step.T, wo_hbm=w_out, cv=conv_value, cb=conv_bc, dtb=dt_bias[None], alog=a_log[None],
        dskip=d_skip[None], og=out_gain[None],
    )
    outputs = dict(
        block_out=((tokens, part), BF16),
        grad_in=((tokens, width), BF16),
        wg_sum=(w_gate.shape, BF16),
        wv_sum=(w_value.shape, BF16),
        wo_sum=(w_out.shape, BF16),
        bc_sum=(w_bc.shape, BF16),
        wp_sum=((16, width), F32),
        norm_sum=((1, width), F32),
    )
    scratch = dict(
        x=vmem((tokens, width), BF16),
        wg=vmem(w_gate.shape, BF16),
        wv=vmem(w_value.shape, BF16),
        wbc=vmem(w_bc.shape, BF16),
        wo=vmem(w_out.shape, BF16),
        cot_all=vmem((tokens, width), BF16),
        halo_x=vmem((TAIL, width), BF16),
        doc_out=vmem((8, 128), F32),
        doc_in=vmem((8, 128), F32),
        doc_prev=vmem((8, 128), F32),
        upper=vmem((BLOCK, BLOCK), BF16),
        eye=vmem((BLOCK, BLOCK), BF16),
        spread=vmem((heads, inner), BF16),
        collect=vmem((inner, heads), BF16),
        normed=vmem((tokens, width), BF16),
        z=vmem((tokens, inner), F32),
        cin=vmem((EDGE + tokens + EDGE, channels), F32),
        y=vmem((tokens, inner), F32),
        xs=vmem((tokens, inner), BF16),
        dy=vmem((tokens, inner), BF16),
        b=vmem((tokens, state), BF16),
        c=vmem((tokens, state), F32),
        tok=vmem((tokens, 128), F32),
        cumt=vmem((heads, tokens), F32),
        dstep=vmem((tokens, heads), BF16),
        inc=vmem((blocks + 1, state, inner), F32),
        kept=vmem((blocks, 1, inner), F32),
        end=vmem((state, inner), F32),
        adj=vmem((blocks, state, inner), BF16),
        tail=vmem((EDGE, channels), F32),
        own=vmem((heads // 2, state, 2 * head_dim), F32),
        end_out=vmem((heads // 2, state, 2 * head_dim), F32),
        end_in=vmem((heads // 2, state, 2 * head_dim), F32),
        carry_part=vmem((heads // 2, 1, 2 * head_dim), F32),
        sel_step=vmem((256, inner), BF16),
        sel_end=vmem((256, inner), BF16),
        sel_into=vmem((256, inner), BF16),
        back_out=vmem((heads // 2, state, 2 * head_dim), BF16),
        norm_in=vmem((nh + ns - 1, 1, width), F32),
        norm_out=vmem((2, 1, width), F32),
        norm_all=vmem((ns, 1, width), F32),
        back_in=vmem((heads // 2, state, 2 * head_dim), BF16),
        carry=vmem((1, inner), F32),
        prod=vmem((1, inner), F32),
        sum_out=vmem((blocks, 8, BLOCK), F32),
        sum_in=vmem((blocks * (nh - 1), 8, BLOCK), F32),
        parts=vmem((blocks, BLOCK, width), BF16),
        out_in=vmem((blocks * 6, BLOCK // 2, part), BF16),
        part_in=vmem((blocks * 6, slab // 2, width), BF16),
        gw_out=vmem(w_out.shape, F32),
        wq_sum=vmem((width // 2 // nh, bc_width), BF16),
        dz=vmem((tokens, inner), BF16),
        g_gain=vmem((1, inner), F32),
        g_dt=vmem((1, heads), F32),
        g_log=vmem((1, heads), F32),
        g_skip=vmem((1, inner), F32),
        g_conv=vmem((8, channels), F32),
        g_norm=vmem((1, width), F32),
        pack=vmem((16, width), F32),
        pack_out=vmem((8, width), F32),
        pack1_in=vmem((nh - 1, 8, width), F32),
        load=pltpu.SemaphoreType.DMA((6,)),
        stored=pltpu.SemaphoreType.DMA((blocks,)),
    )
    for name, (rows, cols), kind in (
        (WO, (inner, width // 2), BF16), (WG, (width // 2, inner), BF16), (WV, (width // 2, inner), BF16),
        (WQ, (width // 2 // nh, bc_width), BF16), (WP, (8, width), F32),
    ):
        if name not in (WV, WQ):
            scratch[name + "_pair"] = vmem((rows, cols), F32)
        if name != WV:
            scratch[name + "_mine"] = vmem((rows, cols), kind)
        scratch[name + "_in"] = vmem((PIECES[name], rows // PIECES[name], cols), kind)
    counts = dict(
        cot=4, halo=2, ends=heads // 2, back=heads // 2, norm=nh + ns - 1, sum=blocks * (nh - 1), out=blocks * 6,
        part=blocks * 6, grad=blocks * 4, edge=1, bc=nh, bcg=2 * nh - 1, pack1=nh - 1,
    )
    for name, n in PIECES.items():
        counts |= {name + "a": 1, name + "b": n, name + "c": n, name + "d": n, name + "f": n}
    for name, n in counts.items():
        scratch[name + "_s"] = pltpu.SemaphoreType.DMA((n,))
        scratch[name + "_r"] = pltpu.SemaphoreType.DMA((n,))
    names = [*inputs, *outputs, *scratch]

    def run(*refs):
        r = types.SimpleNamespace(**dict(zip(names, refs)))
        r.gw_gate = r.gw_value = r.z.at[pl.ds(0, width)]
        r.wv_pair = r.z.at[pl.ds(width, width // 2)]
        r.gw_bc = r.y.at[pl.ds(0, width), pl.ds(0, bc_width)]
        r.bc_pair = r.y.at[pl.ds(width, width // 2), pl.ds(0, bc_width)]
        r.bc_out = r.xs.at[pl.ds(0, width // 2), pl.ds(0, bc_width)]
        free = [pl.ds(width // 2 + o * (width // 2 // nh), width // 2 // nh) for o in range(nh - 1)]
        r.bc_in = [r.xs.at[rows, pl.ds(0, bc_width)] for rows in free]
        r.wv_mine = r.xs.at[pl.ds(width, width // 2)]
        kernel(r)

    block_out, grad_in, g_gate, g_value, g_out, g_bc, small, norm = pl.pallas_call(
        run,
        out_shape=[jax.ShapeDtypeStruct(*o) for o in outputs.values()],
        in_specs=[pl.BlockSpec(memory_space=hbm if name in LOADED else vmem) for name in inputs],
        out_specs=[pl.BlockSpec(memory_space=hbm if name == "grad_in" else vmem) for name in outputs],
        scratch_shapes=list(scratch.values()),
        compiler_params=pltpu.CompilerParams(
            collective_id=0, has_side_effects=True, vmem_limit_bytes=VMEM_LIMIT
        ),
        name="block",
    )(*inputs.values())
    steps = 4
    grads = (block_out, grad_in, g_gate, g_value, g_out, g_bc)
    kinds = (BF16, BF16, F32, F32, F32, F32)
    tiny = ((1, width), (heads, width), (n_taps + 1, inner), (n_taps + 1, bc_width), (1, heads), (1, heads), (1, heads),
            (1, inner))

    def split_rows(a):
        return pl.BlockSpec((a.shape[0] // steps, a.shape[1]), lambda i: (i, 0))

    def whole(dims):
        return pl.BlockSpec(dims, lambda i: (0, 0))

    outs = pl.pallas_call(
        functools.partial(write_kernel, len(grads)),
        grid=(steps,),
        in_specs=[*map(split_rows, grads), whole(small.shape), whole(norm.shape)],
        out_specs=[*map(split_rows, grads), *map(whole, tiny)],
        out_shape=[jax.ShapeDtypeStruct(a.shape, k) for a, k in zip(grads, kinds)]
        + [jax.ShapeDtypeStruct(dims, F32) for dims in tiny],
        compiler_params=pltpu.CompilerParams(vmem_limit_bytes=VMEM_LIMIT),
        name="write",
    )(*grads, small, norm)
    block_out, grad_in, g_gate, g_value, g_out, g_bc, g_norm, g_step, g_cv, g_cb, g_dt, g_log, g_skip, g_gain = outs
    return (
        block_out[None], grad_in[None], g_norm[0], g_gate, g_value, g_bc, g_step.T, g_cv, g_cb, g_dt[0], g_log[0],
        g_skip[0], g_gain[0], g_out,
    )


def solution(mesh):
    return jax.shard_map(
        on_device,
        mesh=mesh,
        in_specs=(
            P(DP_AXIS, SEQ_AXIS, None),
            P(DP_AXIS, SEQ_AXIS),
            P(),
            P(None, HEAD_AXIS),
            P(None, HEAD_AXIS),
            P(),
            P(None, HEAD_AXIS),
            P(None, HEAD_AXIS),
            P(),
            P(HEAD_AXIS),
            P(HEAD_AXIS),
            P(HEAD_AXIS),
            P(HEAD_AXIS),
            P(HEAD_AXIS, None),
            P(DP_AXIS, SEQ_AXIS, HEAD_AXIS),
        ),
        out_specs=(
            P(DP_AXIS, SEQ_AXIS, HEAD_AXIS),
            P(DP_AXIS, SEQ_AXIS, None),
            P(),
            P(None, HEAD_AXIS),
            P(None, HEAD_AXIS),
            P(),
            P(None, HEAD_AXIS),
            P(None, HEAD_AXIS),
            P(),
            P(HEAD_AXIS),
            P(HEAD_AXIS),
            P(HEAD_AXIS),
            P(HEAD_AXIS),
            P(HEAD_AXIS, None),
        ),
        check_vma=False,
    )
```

```python
import functools
import types

import jax
import jax.numpy as jnp
from jax import lax
from jax.experimental import pallas as pl
from jax.experimental.pallas import tpu as pltpu
from jax.sharding import PartitionSpec as P

BLOCK = 256
EDGE = 8
TAIL = 16
EPS = 1e-05
NEG = -1e30
F32 = jnp.float32
BF16 = jnp.bfloat16
NN = (((1,), (0,)), ((), ()))
NT = (((1,), (1,)), ((), ()))
TN = (((0,), (0,)), ((), ()))
MESH = pl.DeviceIdType.MESH
CUM, AUX, DYY, STEP, TO_END, INTO, RMS = 8, 16, 24, 32, 40, 48, 56
LAG = 3
EARLY = 2
HEAD_AXIS, SEQ_AXIS, DP_AXIS = "head", "seq", "dp"
COT, HALO, ENDS, NORM, BACK, SUM, OUT, PART, GRAD, EDGES, BC, BCG, PACK1 = (
    "cot", "halo", "ends", "norm", "back", "sum", "out", "part", "grad", "edge", "bc", "bcg", "pack1"
)
WO, WG, WV, WQ, WP = "wo", "wg", "wv", "wq", "wp"
PIECES = {WO: 4, WG: 4, WV: 8, WQ: 1, WP: 1}
LOADED = ("x_hbm", "cot", "wg_hbm", "wv_hbm", "wbc_hbm", "wo_hbm")
VMEM_LIMIT = 63 * 1024 * 1024


def dot(a, b, dims=NN):
    return lax.dot_general(a, b, dims, preferred_element_type=F32)


def halves(v):
    hi = v.astype(BF16)
    return hi, (v - hi.astype(F32)).astype(BF16)


def dot_left(v, m, dims=NN):
    hi, lo = halves(v)
    return dot(hi, m, dims) + dot(lo, m, dims)


def dot_right(m, v, dims=NN):
    hi, lo = halves(v)
    return dot(m, hi, dims) + dot(m, lo, dims)


def both(v, axis=1):
    return jnp.concatenate(halves(v), axis=axis)


def dot3(a, b, dims=NN):
    (ah, al), (bh, bl) = halves(a), halves(b)
    return dot(
        jnp.concatenate([ah, al, ah], axis=1), jnp.concatenate([bh, bh, bl], axis=dims[0][1][0]), dims
    )


def score_pair(c, b, first):
    hi, lo = halves(c)
    cc, bb = jnp.concatenate([hi, lo], axis=1), jnp.concatenate([b, b], axis=1)
    return dot(cc, bb, NT) if first else dot(bb, cc, NT)


def sigmoid(v):
    return 0.5 * jnp.tanh(0.5 * v) + 0.5


def softplus(v):
    return jnp.maximum(v, 0.0) + jnp.log1p(jnp.exp(-jnp.abs(v)))


def iota(shape, axis):
    return lax.broadcasted_iota(jnp.int32, shape, axis)


def in_norm(x, gain):
    r = lax.rsqrt(jnp.mean(x * x, axis=1, keepdims=True) + EPS)
    return (x * r * gain).astype(BF16)


def repeat(n, body):
    def run(i, carry):
        body(i)
        return carry

    lax.fori_loop(0, n, run, 0)


def kernel(r):
    nh, ns = lax.axis_size(HEAD_AXIS), lax.axis_size(SEQ_AXIS)
    head, seq, dp = lax.axis_index(HEAD_AXIS), lax.axis_index(SEQ_AXIS), lax.axis_index(DP_AXIS)
    me = {HEAD_AXIS: head, SEQ_AXIS: seq, DP_AXIS: dp}
    count = {HEAD_AXIS: nh, SEQ_AXIS: ns, DP_AXIS: 2}
    tokens, width = r.x.shape
    inner, heads = r.wg.shape[1], r.ws.shape[0]
    state = r.wbc.shape[1] // 2
    channels = inner + 2 * state
    blocks, part, slab = tokens // BLOCK, width // nh, BLOCK // nh
    inner_all = inner * nh
    n_taps = r.cv.shape[0] - 1
    lanes = 2 * (inner // heads)

    def at(c):
        return pl.ds(pl.multiple_of(c * BLOCK, BLOCK), BLOCK)

    left, upper_half = lax.rem(head, 2), lax.div(head, 2)
    square = [head, 2 * upper_half + 1 - left, 2 * (1 - upper_half) + left, nh - 1 - head]

    def other(axis, o):
        if axis == HEAD_AXIS:
            return square[abs(o)]
        return lax.rem(me[axis] + o + count[axis], count[axis])

    def link(name, index, axis, o, src, dst):
        return pltpu.make_async_remote_copy(
            src_ref=src,
            dst_ref=dst,
            send_sem=getattr(r, name + "_s").at[index],
            recv_sem=getattr(r, name + "_r").at[index],
            device_id={axis: other(axis, o)},
            device_id_type=MESH,
        )

    def sent(name, index, axis, o, src):
        link(name, index, axis, o, src, src).wait_send()

    def came(name, index, axis, o, dst):
        link(name, index, axis, o, dst, dst).wait_recv()

    def gather_1(name, base, view):
        for o in (1, 2):
            link(name, base + o - 1, HEAD_AXIS, o, view(head), view(head)).start()

    def gather_2(name, base, view, half):
        for o in (1, 2):
            came(name, base + o - 1, HEAD_AXIS, o, view(square[o]))
            piece = half(square[o], o - 1)
            link(name, base + 1 + o, HEAD_AXIS, 3 - o, piece, piece).start()

    def gather_3(name, base, view, half):
        for o in (1, 2):
            came(name, base + 1 + o, HEAD_AXIS, 3 - o, half(square[3], o - 1))
            sent(name, base + o - 1, HEAD_AXIS, o, view(head))
            sent(name, base + 1 + o, HEAD_AXIS, 3 - o, half(square[o], o - 1))

    def scatter_1(name, base, block, inbox):
        for o in (1, 2):
            link(name, base + 2 * o - 2, HEAD_AXIS, o, block(square[o], o - 1), inbox.at[base + 2 * o - 2]).start()
            link(name, base + 2 * o - 1, HEAD_AXIS, o, block(square[3], o - 1), inbox.at[base + 2 * o - 1]).start()

    def scatter_2(name, base, block, inbox):
        for o in (1, 2):
            index = base + 2 * o - 1
            came(name, index, HEAD_AXIS, o, inbox.at[index])
            mine = block(square[3 - o], o - 1)
            mine[...] = (mine[...].astype(F32) + inbox[index].astype(F32)).astype(BF16)
            link(name, base + 3 + o, HEAD_AXIS, 3 - o, mine, inbox.at[base + 3 + o]).start()

    def scatter_3(name, base, block, inbox):
        totals = []
        for o in (1, 2):
            total = block(head, o - 1)[...].astype(F32)
            for index, by in ((base + 2 * o - 2, o), (base + 3 + o, 3 - o)):
                came(name, index, HEAD_AXIS, by, inbox.at[index])
                total = total + inbox[index].astype(F32)
            totals.append(total)
        return totals

    def scatter_sent(name, base, block):
        for o in (1, 2):
            sent(name, base + 2 * o - 2, HEAD_AXIS, o, block(square[o], o - 1))
            sent(name, base + 2 * o - 1, HEAD_AXIS, o, block(square[3], o - 1))
            sent(name, base + 3 + o, HEAD_AXIS, 3 - o, block(square[3 - o], o - 1))

    def cot_of(h):
        return r.cot_all.at[:, pl.ds(pl.multiple_of(h * part, part), part)]

    def cot_half(h, i):
        return r.cot_all.at[pl.ds(i * (tokens // 2), tokens // 2), pl.ds(pl.multiple_of(h * part, part), part)]

    moves = ((r.x_hbm, r.x), (r.wv_hbm, r.wv), (r.wbc_hbm, r.wbc), (r.cot, cot_of(head)), (r.wg_hbm, r.wg), (r.wo_hbm, r.wo))
    loads = [pltpu.make_async_copy(*move, r.load.at[i]) for i, move in enumerate(moves)]
    for load in loads:
        load.start()
    row, col = iota((BLOCK, BLOCK), 0), iota((BLOCK, BLOCK), 1)
    r.upper[...] = (row <= col).astype(BF16)
    r.eye[...] = (row == col).astype(BF16)
    dim = inner // heads
    r.spread[...] = (iota((heads, inner), 1) // dim == iota((heads, inner), 0)).astype(BF16)
    r.collect[...] = (iota((inner, heads), 0) // dim == iota((inner, heads), 1)).astype(BF16)
    for sel, lane in ((r.sel_step, STEP), (r.sel_end, TO_END), (r.sel_into, INTO)):
        sel[...] = (iota((256, inner), 1) // dim + lane == lax.rem(iota((256, inner), 0), 128)).astype(BF16)
    r.tok[...] = jnp.zeros_like(r.tok)
    r.doc_out[...] = jnp.broadcast_to(r.docs[0:1, tokens - 1 : tokens].astype(F32), r.doc_out.shape)
    barrier = pltpu.get_barrier_semaphore()
    for axis in (HEAD_AXIS, SEQ_AXIS, DP_AXIS):
        for o in range(1, count[axis]):
            pl.semaphore_signal(barrier, inc=1, device_id={axis: other(axis, o)}, device_id_type=MESH)
    for load in loads[:3]:
        load.wait()
    gain, out_gain = r.gain[...], r.og[...]

    def project(c):
        rows = at(c)
        normed = in_norm(r.x[rows, :].astype(F32), gain)
        r.normed[rows, :] = normed
        inside = pl.ds(pl.multiple_of(c * BLOCK + EDGE, EDGE), BLOCK)
        r.cin[inside, :inner] = dot(normed, r.wv[...])
        r.cin[inside, inner:] = dot(normed, r.wbc[...])
        r.tok[rows, 0:heads] = dot(normed, r.ws[...], NT) + r.dtb[...]

    repeat(EARLY, project)
    pl.semaphore_wait(barrier, nh + ns + 2 - 3)
    loads[3].wait()
    gather_1(COT, 0, cot_of)
    x_tail = r.x.at[pl.ds(tokens - TAIL, TAIL)]
    link(HALO, 0, SEQ_AXIS, 1, x_tail, r.halo_x).start()
    link(HALO, 1, SEQ_AXIS, 1, r.doc_out, r.doc_in).start()
    repeat(blocks - EARLY, lambda i: project(EARLY + i))

    taps = jnp.concatenate([r.cv[...], r.cb[...]], axis=1)
    rate = -jnp.exp(r.alog[...])
    same = iota((heads, heads), 0) == iota((heads, heads), 1)
    rate_col = jnp.sum(jnp.where(same, rate, 0.0), axis=1, keepdims=True)
    skip = dot_left(r.dskip[...], r.spread[...])
    def conv_pre(window, taps):
        pre = taps[n_taps : n_taps + 1, :] + taps[0:1, :] * window[EDGE:]
        for k in range(1, n_taps):
            pre = pre + taps[k : k + 1, :] * window[EDGE - k : EDGE - k + BLOCK]
        return pre

    def doc_row(c):
        return r.docs[0:1, at(c)].astype(F32)

    def expand_tok(marks, sel, cols=slice(None)):
        return dot(marks, sel[:, cols])

    came(HALO, 0, SEQ_AXIS, -1, r.halo_x)
    came(HALO, 1, SEQ_AXIS, -1, r.doc_in)
    opened = jnp.where(seq == 0, 0.0, 1.0)
    edge = in_norm(r.halo_x[...].astype(F32), gain)
    r.cin[0:EDGE, :inner] = dot(edge, r.wv[...])[TAIL - EDGE :] * opened
    r.cin[0:EDGE, inner:] = dot(edge, r.wbc[...])[TAIL - EDGE :] * opened
    r.doc_prev[...] = jnp.where(seq == 0, -1.0, r.doc_in[...])

    r.carry[...] = jnp.ones_like(r.carry)

    def steps(c):
        rows = at(c)
        around = pl.ds(pl.multiple_of(c * BLOCK, BLOCK), BLOCK + EDGE)
        pre = conv_pre(r.cin[around, inner:], taps[:, inner:])
        u = pre * sigmoid(pre)
        r.b[rows, :] = u[:, :state].astype(BF16)
        r.c[rows, :] = u[:, state:]
        docs = doc_row(c)
        prev = r.doc_prev[0:1, 0:1]
        before = jnp.concatenate([prev, docs[:, : BLOCK - 1]], axis=1)
        ends = docs[:, BLOCK - 1 :]
        marks = [docs, (docs == prev).astype(F32), (docs == before).astype(F32), (docs == ends).astype(F32)]
        vt = r.tok[rows, :].T[0:heads]
        step = softplus(vt)
        la_hi, la_lo = halves(rate_col * step)
        cum = dot(la_hi, r.upper[...]) + dot(la_lo, r.upper[...])
        r.cumt[:, at(c)] = cum
        total = cum[:, BLOCK - 1 :]
        columns = [vt, cum, *marks, jnp.zeros((12, BLOCK), F32), step, jnp.exp(total - cum) * marks[3]]
        columns += [jnp.exp(cum) * marks[1], jnp.zeros((72, BLOCK), F32)]
        r.tok[rows, :] = jnp.concatenate(columns, axis=0).T
        held = jnp.exp(total) * (ends == prev).astype(F32)
        kept = jnp.sum(r.spread[...].astype(F32) * held, axis=0, keepdims=True)
        r.kept[c] = kept
        r.carry[...] = r.carry[...] * kept
        r.doc_prev[...] = jnp.broadcast_to(ends, r.doc_prev.shape)

    repeat(blocks, steps)

    pairs = heads // 2
    for pair in range(pairs):
        r.carry_part[pair] = r.carry[:, pair * lanes : (pair + 1) * lanes]
    r.own[...] = jnp.zeros_like(r.own)

    def relay(turn):
        pair = turn - 2 * seq

        @pl.when(jnp.logical_and(pair >= 0, pair < pairs))
        def _():
            @pl.when(seq > 0)
            def _():
                came(ENDS, pair, SEQ_AXIS, -1, r.end_in.at[pair])

            into = jnp.where(seq > 0, r.end_in[pair], 0.0)
            r.end_out[pair] = r.carry_part[pair] * into + r.own[pair]
            r.own[pair] = into

            @pl.when(seq < ns - 1)
            def _():
                link(ENDS, pair, SEQ_AXIS, 1, r.end_out.at[pair], r.end_in.at[pair]).start()

    for pair in range(pairs):
        cols = slice(pair * lanes, (pair + 1) * lanes)

        def own_states(c, pair=pair, cols=cols):
            rows = at(c)
            around = pl.ds(pl.multiple_of(c * BLOCK, BLOCK), BLOCK + EDGE)
            pre = conv_pre(r.cin[around, cols], taps[:, cols])
            xh = pre * sigmoid(pre)
            marks = both(r.tok[rows, :])
            xs = xh * expand_tok(marks, r.sel_step, cols)
            r.xs[rows, cols] = xs.astype(BF16)
            r.y[rows, cols] = skip[:, cols] * xh
            inc = dot(r.b[rows, :], (xs * expand_tok(marks, r.sel_end, cols)).astype(BF16), TN)
            r.inc[c, :, cols] = inc
            r.own[pair] = r.kept[c, :, cols] * r.own[pair] + inc

        repeat(blocks // 3, lambda i, body=own_states: [body(3 * i + k) for k in range(3)])
        relay(pair)
        if pair == pairs - 2:
            gather_2(COT, 0, cot_of, cot_half)

    def relay_back(turn):
        distance = ns - 1 - seq
        for i in range(2):
            pair = 2 * (turn - 2 * distance) + i

            @pl.when(jnp.logical_and(distance > 0, jnp.logical_and(pair >= 0, pair < pairs)))
            def _(pair=pair):
                came(BACK, pair, SEQ_AXIS, 1, r.back_in.at[pair])
                into = r.back_in[pair].astype(F32)
                r.back_out[pair] = (r.carry_part[pair] * into + r.own[pair]).astype(BF16)
                r.own[pair] = into

                @pl.when(seq > 0)
                def _():
                    link(BACK, pair, SEQ_AXIS, -1, r.back_out.at[pair], r.back_in.at[pair]).start()

    first = iota((BLOCK, lanes), 1) < lanes // 2

    def split(pair):
        zero = jnp.zeros_like(pair)
        return jnp.where(first, pair, zero), jnp.where(first, zero, pair)

    def intra(c):
        rows = at(c)
        cum, cumt = r.tok[rows, CUM : CUM + heads], r.cumt[:, at(c)]
        mask = jnp.where((row >= col) & (r.tok[rows, AUX : AUX + 1] == doc_row(c)), 0.0, NEG)
        scores = score_pair(r.c[rows, :], r.b[rows, :], True)
        for pair in range(heads // 2):
            cols = slice(pair * lanes, (pair + 1) * lanes)
            mixed = []
            for h in (2 * pair, 2 * pair + 1):
                decay = jnp.exp(cum[:, h : h + 1] - cumt[h : h + 1, :] + mask)
                mixed.append((scores * decay).astype(BF16))
            two = jnp.concatenate(split(r.xs[rows, cols]), axis=0)
            r.y[rows, cols] += dot(jnp.concatenate(mixed, axis=1), two)
        r.z[rows, :] = dot(r.normed[rows, :], r.wg[...])
        relay(pairs + c)

    loads[4].wait()
    repeat(blocks // 2, lambda i: (intra(2 * i), intra(2 * i + 1)))
    loads[5].wait()

    if 2 * (ns - 1) > blocks:
        repeat(2 * (ns - 1) - blocks, lambda i: relay(pairs + blocks + i))
    for pair in range(pairs):
        r.end[:, pair * lanes : (pair + 1) * lanes] = r.own[pair]
    gather_3(COT, 0, cot_of, cot_half)

    def dgn_of(rows):
        return dot(r.cot_all[rows, :], r.wo[...], NT)

    lane8 = iota((BLOCK, 8), 1)

    def sums(c):
        rows = at(c)
        si = r.end[...]
        r.end[...] = r.kept[c] * si + r.inc[c]
        r.inc[c] = si
        into = expand_tok(both(r.tok[rows, :]), r.sel_into)
        y = r.y[rows, :] + into * dot3(r.c[rows, :], si)
        r.y[rows, :] = y
        z = r.z[rows, :]
        g = y * (z * sigmoid(z))
        squares = jnp.sum(g * g, axis=1, keepdims=True)
        products = jnp.sum(dgn_of(rows) * out_gain * g, axis=1, keepdims=True)
        cols_hi, cols_lo = halves(jnp.where(lane8 == 0, squares, jnp.where(lane8 == 1, products, 0.0)))
        r.sum_out[c] = dot(cols_hi, r.eye[...], TN) + dot(cols_lo, r.eye[...], TN)
        for o in range(1, nh):
            index = c * (nh - 1) + o - 1
            link(SUM, index, HEAD_AXIS, o, r.sum_out.at[c], r.sum_in.at[index]).start()
        r.parts[c] = dot((g * out_gain).astype(BF16), r.wo[...]).astype(BF16)

    def out_block(c):
        half = BLOCK // 2
        return lambda h, i: r.parts.at[c, pl.ds(i * half, half), pl.ds(pl.multiple_of(h * part, part), part)]

    repeat(blocks // 2, lambda i: (sums(2 * i), sums(2 * i + 1)))
    r.inc[blocks] = r.end[...]

    r.end[...] = jnp.zeros_like(r.end)
    r.prod[...] = jnp.ones_like(r.prod)
    r.pack[...] = jnp.zeros_like(r.pack)
    r.g_gain[...] = jnp.zeros_like(r.g_gain)

    def gate(c):
        rows = at(c)
        total = r.sum_out[c]
        for o in range(1, nh):
            index = c * (nh - 1) + o - 1
            came(SUM, index, HEAD_AXIS, -o, r.sum_in.at[index])
            total = total + r.sum_in[index]
        scatter_1(OUT, 6 * c, out_block(c), r.out_in)
        shares = dot_right(r.eye[...], total, NT)
        y, z = r.y[rows, :], r.z[rows, :]
        dgn = dgn_of(rows)
        sig = sigmoid(z)
        act = z * sig
        g = y * act
        rms = lax.rsqrt(shares[:, 0:1] / inner_all + EPS)
        r.tok[rows, RMS : RMS + 1] = rms
        gr = g * rms
        r.xs[rows, :] = (gr * out_gain).astype(BF16)
        r.g_gain[...] += jnp.sum(dgn * gr, axis=0, keepdims=True)
        dg = rms * (dgn * out_gain) - g * (rms * rms * rms * shares[:, 1:2] / inner_all)
        dy = dg * act
        dyb = dy.astype(BF16)
        r.dy[rows, :] = dyb
        r.dz[rows, :] = (dg * y * (sig * (1.0 + z * (1.0 - sig)))).astype(BF16)
        into = expand_tok(both(r.tok[rows, :]), r.sel_into)
        part_state = dot(r.c[rows, :].astype(BF16), (dy * into).astype(BF16), TN)
        r.adj[c] = part_state.astype(BF16)
        r.end[...] += r.prod[...] * part_state
        r.prod[...] = r.prod[...] * r.kept[c]

    repeat(blocks // 2, lambda i: (gate(2 * i), gate(2 * i + 1)))

    for pair in range(pairs):
        r.own[pair] = r.end[:, pair * lanes : (pair + 1) * lanes]

    @pl.when(seq == ns - 1)
    def _():
        for pair in range(pairs):
            r.back_out[pair] = r.own[pair].astype(BF16)
            link(BACK, pair, SEQ_AXIS, -1, r.back_out.at[pair], r.back_in.at[pair]).start()
        r.own[...] = jnp.zeros_like(r.own)

    r.gw_out[...] = jnp.zeros_like(r.gw_out)
    r.gw_gate[...] = jnp.zeros_like(r.gw_gate)

    def weight_grads(i):
        rows = pl.ds(pl.multiple_of(i * 2 * BLOCK, 2 * BLOCK), 2 * BLOCK)
        r.gw_out[...] += dot(r.xs[rows, :], r.cot_all[rows, :], TN)
        relay_back(2 * i)
        r.gw_gate[...] += dot(r.normed[rows, :], r.dz[rows, :], TN)
        r.tok[rows, DYY : DYY + heads] = dot_left(r.dy[rows, :].astype(F32) * r.y[rows, :], r.collect[...])
        relay_back(2 * i + 1)

    repeat(blocks // 2, weight_grads)

    def add_residual(c):
        cols = pl.ds(pl.multiple_of(head * part, part), part)
        half = BLOCK // 2
        for i, total in enumerate(scatter_3(OUT, 6 * c, out_block(c), r.out_in)):
            rows = pl.ds(pl.multiple_of(c * BLOCK + i * half, half), half)
            scaled = r.tok[rows, RMS : RMS + 1] * total
            r.block_out[rows, :] = (scaled + r.x[rows, cols].astype(F32)).astype(BF16)

    def ref(name, kind):
        return getattr(r, name + kind)

    def half_of(name, source, core):
        if name == WO:
            half = source.shape[1] // 2
            return source.at[:, pl.ds(pl.multiple_of(core * half, half), half)]
        half = source.shape[0] // 2
        return source.at[pl.ds(pl.multiple_of(core * half, half), half)]

    near = seq < ns // 2
    depth, last = jnp.where(near, seq, ns - 1 - seq), ns // 2 - 1
    inward = jnp.where(near, 1, -1)

    def piece_of(name, half, j):
        rows = half.shape[0] // PIECES[name]
        return half.at[pl.ds(j * rows, rows)]

    def result(name, core, j):
        whole = ref(name, "_sum")
        return piece_of(name, whole if name == WQ else half_of(name, whole, core), j)

    def total_a(name, source):
        return link(name + "a", 0, DP_AXIS, 1, half_of(name, source, 1 - dp), ref(name, "_pair"))

    def total_b(name, source):
        total_a(name, source).wait_send()
        came(name + "a", 0, DP_AXIS, 1, ref(name, "_pair"))
        mine = ref(name, "_mine")
        mine[...] = (half_of(name, source, dp)[...] + ref(name, "_pair")[...]).astype(mine.dtype)

        start_inward(name)

    def start_inward(name):
        mine = ref(name, "_mine")

        @pl.when(depth == 0)
        def _():
            for j in range(PIECES[name]):
                link(name + "b", j, SEQ_AXIS, inward, piece_of(name, mine, j), ref(name, "_in").at[j]).start()

    def total_c(name, pieces=None):
        @pl.when(depth > 0)
        def _():
            for j in pieces or range(PIECES[name]):
                came(name + "b", j, SEQ_AXIS, -inward, ref(name, "_in").at[j])
                mine = piece_of(name, ref(name, "_mine"), j)
                mine[...] = (mine[...].astype(F32) + ref(name, "_in")[j].astype(F32)).astype(mine.dtype)

                @pl.when(depth < last)
                def _():
                    link(name + "b", j, SEQ_AXIS, inward, mine, ref(name, "_in").at[j]).start()

                @pl.when(depth == last)
                def _():
                    link(name + "c", j, SEQ_AXIS, inward, mine, result(name, dp, j)).start()

    def total_d(name, middle, pieces=None):
        for j in pieces or range(PIECES[name]):
            total = result(name, dp, j)

            @pl.when(depth == last if middle else depth < last)
            def _():
                if middle:
                    came(name + "c", j, SEQ_AXIS, inward, total)
                    mine = piece_of(name, ref(name, "_mine"), j)
                    total[...] = (mine[...].astype(F32) + total[...].astype(F32)).astype(mine.dtype)
                else:
                    came(name + "f", j, SEQ_AXIS, inward, total)

                @pl.when(depth > 0)
                def _():
                    link(name + "f", j, SEQ_AXIS, -inward, total, total).start()

                if name != WQ:
                    link(name + "d", j, DP_AXIS, 1, total, total).start()

    def total_e(name):
        for j in range(PIECES[name]):
            total, mine = result(name, dp, j), piece_of(name, ref(name, "_mine"), j)
            if name != WQ:
                came(name + "d", j, DP_AXIS, 1, result(name, 1 - dp, j))
                sent(name + "d", j, DP_AXIS, 1, total)

            @pl.when(depth < last)
            def _():
                sent(name + "b", j, SEQ_AXIS, inward, mine)

            @pl.when(depth == last)
            def _():
                sent(name + "c", j, SEQ_AXIS, inward, mine)

            @pl.when(depth > 0)
            def _():
                sent(name + "f", j, SEQ_AXIS, -inward, total)

    total_a(WO, r.gw_out).start()
    total_a(WG, r.gw_gate).start()
    total_b(WO, r.gw_out)
    total_b(WG, r.gw_gate)

    if 2 * (ns - 1) + pairs // 2 > blocks:
        repeat(2 * (ns - 1) + pairs // 2 - blocks, lambda i: relay_back(blocks + i))
    for pair in range(pairs):
        r.end[:, pair * lanes : (pair + 1) * lanes] = r.own[pair]

    def chain(i):
        c = blocks - 1 - i
        here = r.end[...]
        r.end[...] = r.kept[c] * here + r.adj[c].astype(F32)
        r.adj[c] = here.astype(BF16)

    repeat(blocks, chain)
    repeat(blocks, lambda c: scatter_2(OUT, 6 * c, out_block(c), r.out_in))
    r.tail[...] = r.cin[0:EDGE, :]
    r.g_dt[...] = jnp.zeros_like(r.g_dt)
    r.g_log[...] = jnp.zeros_like(r.g_log)
    r.g_skip[...] = jnp.zeros_like(r.g_skip)
    r.g_conv[...] = jnp.zeros_like(r.g_conv)
    r.gw_bc[...] = jnp.zeros_like(r.gw_bc)
    r.g_norm[...] = jnp.zeros_like(r.g_norm)

    def back(c):
        rows = at(c)
        inside = pl.ds(pl.multiple_of(c * BLOCK + EDGE, EDGE), BLOCK)
        b_mat, c_full = r.b[rows, :], r.c[rows, :]
        c_mat = c_full.astype(BF16)
        v = r.tok[rows, 0:heads]
        step = r.tok[rows, STEP : STEP + heads]
        cum, cumt, aux = r.tok[rows, CUM : CUM + heads], r.cumt[:, at(c)], r.tok[rows, AUX : AUX + 8]
        mask = jnp.where((row <= col) & (aux[:, 0:1] == doc_row(c)), 0.0, NEG)
        scores = score_pair(c_full, b_mat, False)
        marks = both(r.tok[rows, :])
        d_scores = jnp.zeros((BLOCK, BLOCK), F32)
        d_b = jnp.zeros((BLOCK, state), F32)
        d_c = jnp.zeros((BLOCK, state), F32)
        d_step_own = jnp.zeros((BLOCK, heads), F32)
        d_cum = r.tok[rows, DYY : DYY + heads]
        through = jnp.zeros((1, heads), F32)

        def conv_grad(d_u, window, pre, sig, cols):
            d_pre = d_u * (sig * (1.0 + pre * (1.0 - sig)))
            for k in range(n_taps):
                shifted = window[EDGE - k : EDGE - k + BLOCK]
                r.g_conv[k : k + 1, cols] += jnp.sum(d_pre * shifted, axis=0, keepdims=True)
            r.g_conv[n_taps : n_taps + 1, cols] += jnp.sum(d_pre, axis=0, keepdims=True)
            r.tail[:, cols] = window[BLOCK:]
            r.cin[inside, cols] = d_pre

        def window_of(cols):
            return jnp.concatenate([r.tail[:, cols], r.cin[inside, cols]], axis=0)

        for pair in range(heads // 2):
            cols = slice(pair * lanes, (pair + 1) * lanes)
            window = window_of(cols)
            pre = conv_pre(window, taps[:, cols])
            sig = sigmoid(pre)
            xh = pre * sig
            step_e, to_end_e, into_e = (expand_tok(marks, sel, cols) for sel in (r.sel_step, r.sel_end, r.sel_into))
            xs = xh * step_e
            xsb = xs.astype(BF16)
            dyb = r.dy[rows, cols]
            dy = dyb.astype(F32)
            adjb = r.adj[c, :, cols]
            adj = adjb.astype(F32)
            dye = dy * into_e
            d_c = d_c + dot3(dye, r.inc[c, :, cols], NT)
            d_b = d_b + dot(both(xs * to_end_e), jnp.concatenate([adjb, adjb], axis=1), NT)
            d_xs_inter = to_end_e * dot(b_mat, adjb)
            two = split(dyb)
            mixed = []
            for i, h in enumerate((2 * pair, 2 * pair + 1)):
                decay = jnp.exp(cumt[h : h + 1, :] - cum[:, h : h + 1] + mask)
                mixed.append((scores * decay).astype(BF16))
                d_scores = d_scores + dot(xsb, two[i], NT) * decay
            d_xs_intra = dot(jnp.concatenate(mixed, axis=1), jnp.concatenate(two, axis=0))
            d_xs = d_xs_intra + d_xs_inter
            collect = jnp.concatenate([r.collect[cols, :]] * 2, axis=0)
            d_step_own = d_step_own + dot(both(xh * d_xs), collect)
            lost = skip[:, cols] * (dy * xh) + (xsb.astype(F32) * d_xs_intra + xs * d_xs_inter)
            d_cum = d_cum - dot(both(lost), collect)
            ended = jnp.sum(adj * r.inc[c + 1, :, cols], axis=0, keepdims=True)
            through = through + dot(both(ended), collect)
            r.g_skip[:, cols] += jnp.sum(dy * xh, axis=0, keepdims=True)
            conv_grad(skip[:, cols] * dy + step_e * d_xs, window, pre, sig, cols)
        d_sb = d_scores.astype(BF16)
        d_b = d_b + dot(d_sb, c_mat)
        d_c = d_c + dot(d_sb, b_mat, TN)
        cols = slice(inner, channels)
        window = window_of(cols)
        pre = conv_pre(window, taps[:, cols])
        conv_grad(jnp.concatenate([d_b, d_c], axis=1), window, pre, sigmoid(pre), cols)
        d_la = (dot_right(r.upper[...], d_cum) + through) * aux[:, 2:3]
        r.g_log[...] += jnp.sum(rate * step * d_la, axis=0, keepdims=True)
        d_v = (d_step_own + rate * d_la) * sigmoid(v)
        r.g_dt[...] += jnp.sum(d_v, axis=0, keepdims=True)
        r.dstep[rows, :] = d_v.astype(BF16)

    def project_back(c):
        rows = at(c)
        window = r.cin[pl.ds(pl.multiple_of(c * BLOCK + EDGE, EDGE), BLOCK + EDGE), :]
        d_in = taps[0:1, :] * window[:BLOCK]
        for k in range(1, n_taps):
            d_in = d_in + taps[k : k + 1, :] * window[k : k + BLOCK]
        d_inb = d_in.astype(BF16)
        d_val = d_inb[:, :inner]
        dstep = r.dstep[rows, :]
        normed = r.normed[rows, :]
        grads = dot(normed, d_inb, TN)
        r.gw_value[...] += grads[:, :inner]
        r.gw_bc[...] += grads[:, inner:]
        r.pack[0:heads, :] += dot(dstep, normed, TN)
        d_part = dot(r.dz[rows, :], r.wg[...], NT) + dot(d_val, r.wv[...], NT)
        d_part = d_part + dot(d_inb[:, inner:], r.wbc[...], NT) + dot(dstep, r.ws[...])
        scatter_sent(OUT, 6 * c, out_block(c))
        r.parts[c] = d_part.astype(BF16)
        scatter_1(PART, 6 * c, part_block(c), r.part_in)

    def part_block(c):
        half = slab // 2
        return lambda h, i: r.parts.at[c, pl.ds(pl.multiple_of(h * slab + i * half, half), half)]

    def combine(c):
        scatter_2(PART, 6 * c, part_block(c), r.part_in)

    def slab_of(c):
        return lambda h: r.normed.at[pl.ds(pl.multiple_of(c * BLOCK + h * slab, slab), slab)]

    def slab_half(c):
        half = slab // 2
        return lambda h, i: r.normed.at[pl.ds(pl.multiple_of(c * BLOCK + h * slab + i * half, half), half)]

    def forward(c):
        gather_2(GRAD, 4 * c, slab_of(c), slab_half(c))

    def own_slab(c):
        return pl.ds(pl.multiple_of(c * BLOCK + head * slab, slab), slab)

    def finish(c):
        rows = own_slab(c)
        total = jnp.concatenate(scatter_3(PART, 6 * c, part_block(c), r.part_in), axis=0)
        x = r.x[rows, :].astype(F32)
        norm = lax.rsqrt(jnp.mean(x * x, axis=1, keepdims=True) + EPS)
        xr = x * norm
        d_normed = total
        r.g_norm[...] += jnp.sum(d_normed * xr, axis=0, keepdims=True)
        q = d_normed * gain
        d_x = norm * q - xr * (norm * norm * jnp.mean(q * x, axis=1, keepdims=True))
        r.normed[rows, :] = (d_x + r.cot_all[rows, :].astype(F32)).astype(BF16)
        gather_1(GRAD, 4 * c, slab_of(c))

    first_rows = r.cin.at[pl.ds(EDGE, EDGE)]
    last_rows = r.cin.at[pl.ds(EDGE + tokens, EDGE)]

    def reverse(c):
        back(c)

        @pl.when(c == 0)
        def _():
            link(EDGES, 0, SEQ_AXIS, -1, first_rows, last_rows).start()
            r.gw_value[...] = jnp.zeros_like(r.gw_value)

        add_residual(c)

        @pl.when(c >= 1)
        def _():
            project_back(c - 1)

        @pl.when(c >= 2)
        def _():
            combine(c - 2)

        @pl.when(c == 2)
        def _():
            total_c(WO)

        @pl.when(c >= LAG)
        def _():
            finish(c - LAG)

        @pl.when(c >= LAG + 2)
        def _():
            forward(c - LAG - 2)

        @pl.when(c == 4)
        def _():
            total_c(WG)
            total_d(WO, True)

    repeat(blocks, reverse)

    unfinished, unsent = [*range(blocks - LAG, blocks)], [*range(max(blocks - LAG - 2, 0), blocks)]
    came(EDGES, 0, SEQ_AXIS, 1, last_rows)

    @pl.when(seq == ns - 1)
    def _():
        r.cin[EDGE + tokens :, :] = jnp.zeros((EDGE, channels), F32)

    project_back(blocks - 1)
    total_a(WV, r.gw_value).start()

    half_rows = width // 2
    quarter = half_rows // nh

    def bc_rows(whole, core, h):
        return whole.at[pl.ds(pl.multiple_of(core * half_rows + h * quarter, quarter), quarter)]

    def half_bc(core):
        return r.gw_bc.at[pl.ds(pl.multiple_of(core * half_rows, half_rows), half_rows)]

    link(BC, nh - 1, DP_AXIS, 1, half_bc(1 - dp), r.bc_pair).start()
    r.pack[9 : 9 + n_taps + 1, :channels] = r.g_conv[: n_taps + 1, :]
    r.pack[14:15, :inner] = r.g_gain[...]
    r.pack[15:16, 0:heads] = r.g_dt[...]
    r.pack[15:16, 128 : 128 + heads] = r.g_log[...]
    r.pack[15:16, 256 : 256 + heads] = dot_left(r.g_skip[...], r.collect[...])
    r.pack_out[...] = r.pack[8:16, :]
    for o in range(1, nh):
        link(PACK1, o - 1, HEAD_AXIS, o, r.pack_out, r.pack1_in.at[o - 1]).start()
    total_d(WG, True)
    total_b(WV, r.gw_value)
    came(BC, nh - 1, DP_AXIS, 1, r.bc_pair)
    r.bc_out[...] = (half_bc(dp)[...] + r.bc_pair[...]).astype(BF16)
    for o in range(1, nh):
        link(BC, o - 1, HEAD_AXIS, o, bc_rows(r.bc_out, 0, square[o]), r.bc_in[o - 1]).start()
    combine(blocks - 2)
    forward(unsent[0])
    finish(unfinished[0])
    total_c(WV, (0, 1))
    for o in range(1, nh):
        came(PACK1, o - 1, HEAD_AXIS, -o, r.pack1_in.at[o - 1])
        r.pack[9 : 9 + n_taps + 1, inner:channels] += r.pack1_in[o - 1, 1 : 2 + n_taps, inner:channels]
    total_a(WP, r.pack).start()
    combine(blocks - 1)
    total_c(WV, (2, 3))
    total_d(WV, True, (0, 1))
    for c in unfinished[1:-1]:
        finish(c)
    forward(unsent[1])
    total_c(WV, (4, 5))
    total_d(WV, True, (2, 3))
    mine = bc_rows(r.bc_out, 0, head)[...].astype(F32)
    for o in range(1, nh):
        came(BC, o - 1, HEAD_AXIS, -o, r.bc_in[o - 1])
        mine = mine + r.bc_in[o - 1][...].astype(F32)
    r.wq_mine[...] = mine.astype(BF16)
    start_inward(WQ)
    total_b(WP, r.pack)
    total_c(WV, (6, 7))
    total_d(WV, True, (4, 5))
    total_d(WO, False)
    total_d(WG, False)
    finish(blocks - 1)
    for o in range(1, nh):
        link(NORM, o - 1, HEAD_AXIS, o, r.g_norm, r.norm_in.at[o - 1]).start()
    total_d(WV, True, (6, 7))
    total_c(WP)
    total_c(WQ)
    for c in unsent[2:-1]:
        forward(c)
    total_d(WP, True)
    total_d(WQ, True)
    total_d(WV, False)
    total = r.g_norm[...]
    for o in range(1, nh):
        came(NORM, o - 1, HEAD_AXIS, -o, r.norm_in.at[o - 1])
        total = total + r.norm_in[o - 1]
    r.norm_out[0] = total
    link(NORM, nh - 1, DP_AXIS, 1, r.norm_out.at[0], r.norm_in.at[nh - 1]).start()
    forward(blocks - 1)
    total_d(WP, False)
    total_d(WQ, False)
    total_e(WQ)
    mine = bc_rows(r.bc_sum, dp, head)
    mine[...] = r.wq_sum[...]
    for o in range(1, nh):
        link(BCG, o - 1, HEAD_AXIS, o, mine, mine).start()
    link(BCG, nh - 1, DP_AXIS, 1, mine, mine).start()
    came(NORM, nh - 1, DP_AXIS, 1, r.norm_in.at[nh - 1])
    total = r.norm_out[0] + r.norm_in[nh - 1]
    r.norm_out[1] = total
    for o in range(1, ns):
        link(NORM, nh + o - 1, SEQ_AXIS, o, r.norm_out.at[1], r.norm_in.at[nh + o - 1]).start()
    for name in (WO, WG, WV, WP):
        total_e(name)

    r.norm_all[seq] = total
    for o in range(1, ns):
        came(NORM, nh + o - 1, SEQ_AXIS, -o, r.norm_in.at[nh + o - 1])
        r.norm_all[other(SEQ_AXIS, -o)] = r.norm_in[nh + o - 1]
    total = r.norm_all[0]
    for k in range(1, ns):
        total = total + r.norm_all[k]
    r.norm_sum[...] = total
    for o in range(1, nh):
        theirs = bc_rows(r.bc_sum, dp, square[o])
        came(BCG, o - 1, HEAD_AXIS, -o, theirs)
        link(BCG, nh - 1 + o, DP_AXIS, 1, theirs, theirs).start()
        sent(BCG, o - 1, HEAD_AXIS, o, mine)
        sent(BC, o - 1, HEAD_AXIS, o, bc_rows(r.bc_out, 0, square[o]))
        sent(PACK1, o - 1, HEAD_AXIS, o, r.pack_out)
        sent(NORM, o - 1, HEAD_AXIS, o, r.g_norm)
    for o in range(nh):
        came(BCG, nh - 1 + o, DP_AXIS, 1, bc_rows(r.bc_sum, 1 - dp, square[o]))
        sent(BCG, nh - 1 + o, DP_AXIS, 1, bc_rows(r.bc_sum, dp, square[o]))
    sent(BC, nh - 1, DP_AXIS, 1, half_bc(1 - dp))
    sent(NORM, nh - 1, DP_AXIS, 1, r.norm_out.at[0])
    for o in range(1, ns):
        sent(NORM, nh + o - 1, SEQ_AXIS, o, r.norm_out.at[1])
    sent(HALO, 0, SEQ_AXIS, 1, x_tail)
    sent(HALO, 1, SEQ_AXIS, 1, r.doc_out)
    sent(EDGES, 0, SEQ_AXIS, -1, first_rows)

    @pl.when(seq > 0)
    def _():
        for pair in range(pairs):
            sent(BACK, pair, SEQ_AXIS, -1, r.back_out.at[pair])

    @pl.when(seq < ns - 1)
    def _():
        for pair in range(pairs):
            sent(ENDS, pair, SEQ_AXIS, 1, r.end_out.at[pair])

    def drain(c):
        for o in range(1, nh):
            sent(SUM, c * (nh - 1) + o - 1, HEAD_AXIS, o, r.sum_out.at[c])
        scatter_sent(PART, 6 * c, part_block(c))
        gather_3(GRAD, 4 * c, slab_of(c), slab_half(c))
        store(c).start()

    def store(c):
        return pltpu.make_async_copy(r.normed.at[at(c)], r.grad_in.at[at(c)], r.stored.at[c])

    repeat(blocks, drain)
    repeat(blocks, lambda c: store(c).wait())


def write_kernel(n, *refs):
    small, norm_sum = refs[n : n + 2]
    for source, target in zip(refs[:n], refs[n + 2 :]):
        target[...] = source[...].astype(target.dtype)
    norm, step, conv_v, conv_b, dt, log, skip, gain = refs[2 * n + 2 :]
    inner, heads, taps = conv_v.shape[1], dt.shape[1], conv_v.shape[0]

    @pl.when(pl.program_id(0) == 0)
    def _():
        norm[...] = norm_sum[...]
        step[...] = small[0:heads, :]
        conv_v[...] = small[9 : 9 + taps, :inner]
        conv_b[...] = small[9 : 9 + taps, inner : inner + conv_b.shape[1]]
        dt[...] = small[15:16, 0:heads]
        log[...] = small[15:16, 128 : 128 + heads]
        skip[...] = small[15:16, 256 : 256 + heads]
        gain[...] = small[14:15, :inner]


def on_device(
    hidden_in, doc_ids, norm_gain, w_gate, w_value, w_bc, w_step, conv_value, conv_bc, dt_bias, a_log, d_skip,
    out_gain, w_out, cotangent,
):
    x, cot = hidden_in[0], cotangent[0]
    tokens, width = x.shape
    inner, heads = w_gate.shape[1], w_step.shape[1]
    bc_width, head_dim = w_bc.shape[1], inner // heads
    state = bc_width // 2
    channels = inner + bc_width
    blocks = tokens // BLOCK
    nh, ns = lax.axis_size(HEAD_AXIS), lax.axis_size(SEQ_AXIS)
    part, slab = width // nh, BLOCK // nh
    n_taps = conv_value.shape[0] - 1
    vmem, hbm = pltpu.VMEM, pl.ANY
    inputs = dict(
        x_hbm=x, cot=cot, docs=doc_ids, gain=norm_gain[None], wg_hbm=w_gate, wv_hbm=w_value, wbc_hbm=w_bc,
        ws=w_step.T, wo_hbm=w_out, cv=conv_value, cb=conv_bc, dtb=dt_bias[None], alog=a_log[None],
        dskip=d_skip[None], og=out_gain[None],
    )
    outputs = dict(
        block_out=((tokens, part), BF16),
        grad_in=((tokens, width), BF16),
        wg_sum=(w_gate.shape, BF16),
        wv_sum=(w_value.shape, BF16),
        wo_sum=(w_out.shape, BF16),
        bc_sum=(w_bc.shape, BF16),
        wp_sum=((16, width), F32),
        norm_sum=((1, width), F32),
    )
    scratch = dict(
        x=vmem((tokens, width), BF16),
        wg=vmem(w_gate.shape, BF16),
        wv=vmem(w_value.shape, BF16),
        wbc=vmem(w_bc.shape, BF16),
        wo=vmem(w_out.shape, BF16),
        cot_all=vmem((tokens, width), BF16),
        halo_x=vmem((TAIL, width), BF16),
        doc_out=vmem((8, 128), F32),
        doc_in=vmem((8, 128), F32),
        doc_prev=vmem((8, 128), F32),
        upper=vmem((BLOCK, BLOCK), BF16),
        eye=vmem((BLOCK, BLOCK), BF16),
        spread=vmem((heads, inner), BF16),
        collect=vmem((inner, heads), BF16),
        normed=vmem((tokens, width), BF16),
        z=vmem((tokens, inner), F32),
        cin=vmem((EDGE + tokens + EDGE, channels), F32),
        y=vmem((tokens, inner), F32),
        xs=vmem((tokens, inner), BF16),
        dy=vmem((tokens, inner), BF16),
        b=vmem((tokens, state), BF16),
        c=vmem((tokens, state), F32),
        tok=vmem((tokens, 128), F32),
        cumt=vmem((heads, tokens), F32),
        dstep=vmem((tokens, heads), BF16),
        inc=vmem((blocks + 1, state, inner), F32),
        kept=vmem((blocks, 1, inner), F32),
        end=vmem((state, inner), F32),
        adj=vmem((blocks, state, inner), BF16),
        tail=vmem((EDGE, channels), F32),
        own=vmem((heads // 2, state, 2 * head_dim), F32),
        end_out=vmem((heads // 2, state, 2 * head_dim), F32),
        end_in=vmem((heads // 2, state, 2 * head_dim), F32),
        carry_part=vmem((heads // 2, 1, 2 * head_dim), F32),
        sel_step=vmem((256, inner), BF16),
        sel_end=vmem((256, inner), BF16),
        sel_into=vmem((256, inner), BF16),
        back_out=vmem((heads // 2, state, 2 * head_dim), BF16),
        norm_in=vmem((nh + ns - 1, 1, width), F32),
        norm_out=vmem((2, 1, width), F32),
        norm_all=vmem((ns, 1, width), F32),
        back_in=vmem((heads // 2, state, 2 * head_dim), BF16),
        carry=vmem((1, inner), F32),
        prod=vmem((1, inner), F32),
        sum_out=vmem((blocks, 8, BLOCK), F32),
        sum_in=vmem((blocks * (nh - 1), 8, BLOCK), F32),
        parts=vmem((blocks, BLOCK, width), BF16),
        out_in=vmem((blocks * 6, BLOCK // 2, part), BF16),
        part_in=vmem((blocks * 6, slab // 2, width), BF16),
        gw_out=vmem(w_out.shape, F32),
        wq_sum=vmem((width // 2 // nh, bc_width), BF16),
        dz=vmem((tokens, inner), BF16),
        g_gain=vmem((1, inner), F32),
        g_dt=vmem((1, heads), F32),
        g_log=vmem((1, heads), F32),
        g_skip=vmem((1, inner), F32),
        g_conv=vmem((8, channels), F32),
        g_norm=vmem((1, width), F32),
        pack=vmem((16, width), F32),
        pack_out=vmem((8, width), F32),
        pack1_in=vmem((nh - 1, 8, width), F32),
        load=pltpu.SemaphoreType.DMA((6,)),
        stored=pltpu.SemaphoreType.DMA((blocks,)),
    )
    for name, (rows, cols), kind in (
        (WO, (inner, width // 2), BF16), (WG, (width // 2, inner), BF16), (WV, (width // 2, inner), BF16),
        (WQ, (width // 2 // nh, bc_width), BF16), (WP, (8, width), F32),
    ):
        if name not in (WV, WQ):
            scratch[name + "_pair"] = vmem((rows, cols), F32)
        if name != WV:
            scratch[name + "_mine"] = vmem((rows, cols), kind)
        scratch[name + "_in"] = vmem((PIECES[name], rows // PIECES[name], cols), kind)
    counts = dict(
        cot=4, halo=2, ends=heads // 2, back=heads // 2, norm=nh + ns - 1, sum=blocks * (nh - 1), out=blocks * 6,
        part=blocks * 6, grad=blocks * 4, edge=1, bc=nh, bcg=2 * nh - 1, pack1=nh - 1,
    )
    for name, n in PIECES.items():
        counts |= {name + "a": 1, name + "b": n, name + "c": n, name + "d": n, name + "f": n}
    for name, n in counts.items():
        scratch[name + "_s"] = pltpu.SemaphoreType.DMA((n,))
        scratch[name + "_r"] = pltpu.SemaphoreType.DMA((n,))
    names = [*inputs, *outputs, *scratch]

    def run(*refs):
        r = types.SimpleNamespace(**dict(zip(names, refs)))
        r.gw_gate = r.gw_value = r.z.at[pl.ds(0, width)]
        r.wv_pair = r.z.at[pl.ds(width, width // 2)]
        r.gw_bc = r.y.at[pl.ds(0, width), pl.ds(0, bc_width)]
        r.bc_pair = r.y.at[pl.ds(width, width // 2), pl.ds(0, bc_width)]
        r.bc_out = r.xs.at[pl.ds(0, width // 2), pl.ds(0, bc_width)]
        free = [pl.ds(width // 2 + o * (width // 2 // nh), width // 2 // nh) for o in range(nh - 1)]
        r.bc_in = [r.xs.at[rows, pl.ds(0, bc_width)] for rows in free]
        r.wv_mine = r.xs.at[pl.ds(width, width // 2)]
        kernel(r)

    block_out, grad_in, g_gate, g_value, g_out, g_bc, small, norm = pl.pallas_call(
        run,
        out_shape=[jax.ShapeDtypeStruct(*o) for o in outputs.values()],
        in_specs=[pl.BlockSpec(memory_space=hbm if name in LOADED else vmem) for name in inputs],
        out_specs=[pl.BlockSpec(memory_space=hbm if name == "grad_in" else vmem) for name in outputs],
        scratch_shapes=list(scratch.values()),
        compiler_params=pltpu.CompilerParams(
            collective_id=0, has_side_effects=True, vmem_limit_bytes=VMEM_LIMIT
        ),
        name="block",
    )(*inputs.values())
    steps = 2
    grads = (block_out, grad_in, g_gate, g_value, g_out, g_bc)
    kinds = (BF16, BF16, F32, F32, F32, F32)
    tiny = ((1, width), (heads, width), (n_taps + 1, inner), (n_taps + 1, bc_width), (1, heads), (1, heads), (1, heads),
            (1, inner))

    def split_rows(a):
        return pl.BlockSpec((a.shape[0] // steps, a.shape[1]), lambda i: (i, 0))

    def whole(dims):
        return pl.BlockSpec(dims, lambda i: (0, 0))

    outs = pl.pallas_call(
        functools.partial(write_kernel, len(grads)),
        grid=(steps,),
        in_specs=[*map(split_rows, grads), whole(small.shape), whole(norm.shape)],
        out_specs=[*map(split_rows, grads), *map(whole, tiny)],
        out_shape=[jax.ShapeDtypeStruct(a.shape, k) for a, k in zip(grads, kinds)]
        + [jax.ShapeDtypeStruct(dims, F32) for dims in tiny],
        compiler_params=pltpu.CompilerParams(vmem_limit_bytes=VMEM_LIMIT),
        name="write",
    )(*grads, small, norm)
    block_out, grad_in, g_gate, g_value, g_out, g_bc, g_norm, g_step, g_cv, g_cb, g_dt, g_log, g_skip, g_gain = outs
    return (
        block_out[None], grad_in[None], g_norm[0], g_gate, g_value, g_bc, g_step.T, g_cv, g_cb, g_dt[0], g_log[0],
        g_skip[0], g_gain[0], g_out,
    )


def solution(mesh):
    return jax.shard_map(
        on_device,
        mesh=mesh,
        in_specs=(
            P(DP_AXIS, SEQ_AXIS, None),
            P(DP_AXIS, SEQ_AXIS),
            P(),
            P(None, HEAD_AXIS),
            P(None, HEAD_AXIS),
            P(),
            P(None, HEAD_AXIS),
            P(None, HEAD_AXIS),
            P(),
            P(HEAD_AXIS),
            P(HEAD_AXIS),
            P(HEAD_AXIS),
            P(HEAD_AXIS),
            P(HEAD_AXIS, None),
            P(DP_AXIS, SEQ_AXIS, HEAD_AXIS),
        ),
        out_specs=(
            P(DP_AXIS, SEQ_AXIS, HEAD_AXIS),
            P(DP_AXIS, SEQ_AXIS, None),
            P(),
            P(None, HEAD_AXIS),
            P(None, HEAD_AXIS),
            P(),
            P(None, HEAD_AXIS),
            P(None, HEAD_AXIS),
            P(),
            P(HEAD_AXIS),
            P(HEAD_AXIS),
            P(HEAD_AXIS),
            P(HEAD_AXIS),
            P(HEAD_AXIS, None),
        ),
        check_vma=False,
    )
```
